32 devices in a mesh: dp: 8 (over y, x, core), ctx: 4 (over z).
Axes of the slice: x: 2, y: 2, z: 4, core: 2. Of those that a mesh axis runs over, the one named last changes fastest.
Arguments:
- tokens: bfloat16 [8, 1024, 1536], P('dp', 'ctx'), may hold values from -6 to 6
- lengths: int32 [8], P('dp'), may hold values from 256 to 1024, as said below
- routes: int32 [8, 1024, 8], P('dp', 'ctx'), may hold values from 0 to 15, all different within a row; in each aligned block of 256 rows (0 to 255, 256 to 511, ..., all dimensions but the last counted through in order) at most 144 rows name the same one
- cotangent: bfloat16 [8, 1024, 1536], P('dp', 'ctx'), may hold values from -6 to 6
- gain_attn: bfloat16 [1536], P('dp'), may hold values from 0.5 to 1.5
- gain_moe: bfloat16 [1536], P('dp'), may hold values from 0.5 to 1.5
- w_query: bfloat16 [1536, 1536], P('dp'), may hold values from -0.15625 to 0.15625
- w_keyval: bfloat16 [1536, 1024], P('dp'), may hold values from -0.15625 to 0.15625
- w_output: bfloat16 [1536, 1536], P('dp'), may hold values from -4 to 4
- w_router: bfloat16 [1536, 16], P('dp'), may hold values from -0.079589844 to 0.079589844
- w_gate_up: bfloat16 [16, 1536, 1024], P('dp'), may hold values from -0.15625 to 0.15625
- w_down: bfloat16 [16, 512, 1536], P('dp'), may hold values from -1 to 1
Outputs:
- outcome: bfloat16 [8, 1024, 1536], P('dp', 'ctx')
- grad_tokens: bfloat16 [8, 1024, 1536], P('dp', 'ctx')
- grad_gain_attn: float32 [1536], P('dp')
- grad_gain_moe: float32 [1536], P('dp')
- grad_w_query: float32 [1536, 1536], P('dp')
- grad_w_keyval: float32 [1536, 1024], P('dp')
- grad_w_output: float32 [1536, 1536], P('dp')
- grad_w_router: float32 [1536, 16], P('dp')
- grad_w_gate_up: float32 [16, 1536, 1024], P('dp')
- grad_w_down: float32 [16, 512, 1536], P('dp')
The draws below stay inside these ranges and needn't reach their ends.
Inputs may be any that keep to these rules, and one draw needn't show every extreme that they name: `lengths`: some slot holds 1024 live tokens in every draw. `routes`: each token names 8 different experts; within the 256 rows of one device no expert is named by more than 144 rows, and some expert reaches 144.
All inputs are finite; a program needn't handle non-finite values.
Results may differ from the reference program's by a relative error of at most 0.022.
Values may be sent and summed in bfloat16 or wider, within the bound.
No kernel may reach another device: no remote copies, remote signals or barrier semaphores. Data moves between devices by JAX's collectives and lax.ppermute only.
A program may use at most 256 MiB of HBM per device.

```python
import math
import jax
import jax.numpy as jnp
import numpy as np
from jax import lax

D = 1536
H = 24
KVH = 8
HD = 64
FF = 512
EXPERTS = 16
TOPK = 8
LEN = 1024
TOK_DEV = 256
CAP = 144
SLOTS = 8


def draw_lengths(key, part):
    key = jax.random.fold_in(key, 7)
    first_key, second_key = jax.random.split(key)
    spread = jax.random.randint(first_key, (SLOTS,), LEN // 4, LEN + 1)
    longest = jax.random.randint(second_key, (), 0, SLOTS)
    return jnp.where(jnp.arange(SLOTS) == longest, LEN, spread).astype(jnp.int32)


def shard_levels(rng, dims, shards, smallest, high):
    level = 1.0
    for position, parts in shards:
        draws = jax.random.uniform(jax.random.fold_in(jax.random.fold_in(rng, 6), position), (parts,), jnp.float32, smallest / len(shards), high / len(shards))
        level = level * jnp.repeat(jnp.exp(draws), dims[position] // parts).reshape((-1,) + (1,) * (len(dims) - 1 - position))
    return level


def shared_out(rng, own, number, rows, count, top, bound, skew):
    ranking = jax.random.permutation(rng, count)
    heavy_load, common = portions_of(count, rows * top, bound, skew, True), portions_of(count, rows * top, bound, skew, False)
    places = jnp.arange(count)

    def named(tallies, turn):
        used = int((tallies > 0).sum())
        fixed = max(1, used // 4)
        shifted = fixed + (places - fixed + turn * (used - fixed)) % max(1, count - fixed)
        return jnp.zeros((count,), jnp.int32).at[ranking[jnp.where(places < fixed, places, shifted)]].set(jnp.asarray(tallies, jnp.int32))

    tallies = jnp.where(number % 4 == 0, named(heavy_load, number // 4), named(common, number - number // 4 - 1))
    mixed = jax.random.permutation(jax.random.fold_in(own, 3), count)
    giver, taker = mixed[0:count // 2 * 2:2], mixed[1:count // 2 * 2:2]
    room = jnp.minimum(tallies[giver] - 1, bound - tallies[taker]) // 2
    room = jnp.where((giver == ranking[0]) | (taker == ranking[0]) | (tallies[taker] == 0), 0, jnp.maximum(room, 0))
    shifted = jax.random.randint(jax.random.fold_in(own, 4), (count // 2,), 0, 1 << 20) % (room + 1)
    tallies = tallies.at[giver].add(-shifted).at[taker].add(shifted)
    members = jnp.searchsorted(jnp.cumsum(tallies), jnp.arange(rows * top), side="right").astype(jnp.int32)
    table = members.reshape(top, rows).T
    table = table[jax.random.permutation(jax.random.fold_in(own, 1), rows)]
    turn = jax.random.randint(jax.random.fold_in(own, 2), (rows, 1), 0, top)
    return jnp.take_along_axis(table, (jnp.arange(top)[None, :] + turn) % top, axis=1)


def portions_of(number_of, total, limit, lean, full):
    loads = [(1 << 20) // math.isqrt(standing ** lean) + 1 for standing in range(1, number_of + 1)]
    largest = limit if full else min(limit, max(-(-total // number_of), total * loads[0] // sum(loads)))
    least = 1 if total - largest >= number_of - 1 else 0
    holding, surplus = [largest] + [least] * (number_of - 1), total - largest - least * (number_of - 1)
    while surplus > 0:
        movable = [i for i in range(1, number_of) if holding[i] < largest] or [i for i in range(1, number_of) if holding[i] < limit]
        mass, budget = sum([loads[i] for i in movable]), surplus
        for i in movable:
            more = min(limit - holding[i], max(1, budget * loads[i] // mass), surplus)
            holding[i] = holding[i] + more
            surplus = surplus - more
    return np.array(holding)


def bell_draw(key, shape, deviation, limit, cuts=(), kind=jnp.bfloat16):
    level = shard_levels(key, shape, cuts, -0.22, 0.18) if cuts else 1.0
    array = jax.random.normal(key, shape, jnp.float32) * deviation * level
    return jnp.minimum(jnp.maximum(array, -limit), limit).astype(kind)


def setup_inputs(seed: int = 0) -> dict:
    key_list = jax.random.split(jax.random.key(seed), 13)
    tokens = bell_draw(key_list[0], (SLOTS, LEN, D), 1.0, 6.0, ((0, 8), (1, 4)))
    lengths = draw_lengths(jax.random.fold_in(key_list[12], 71), 0)
    routes_keys = jax.random.split(jax.random.fold_in(key_list[2], 1), SLOTS * LEN // TOK_DEV)
    routes_turns = jax.random.permutation(jax.random.fold_in(key_list[2], 3), SLOTS * LEN // TOK_DEV)
    routes = jax.vmap(lambda own, number: shared_out(jax.random.fold_in(key_list[2], 2), own, number, TOK_DEV, EXPERTS, TOPK, CAP, 0))(routes_keys, routes_turns).reshape((SLOTS, LEN, TOPK))
    cotangent = bell_draw(key_list[3], (SLOTS, LEN, D), 1.0, 6.0, ((0, 8), (1, 4)))
    gain_attn = jnp.clip(1.0 + 0.1 * jax.random.normal(key_list[4], (D,), jnp.float32), 0.5, 1.5).astype(jnp.bfloat16)
    gain_moe = jnp.clip(1.0 + 0.1 * jax.random.normal(key_list[5], (D,), jnp.float32), 0.5, 1.5).astype(jnp.bfloat16)
    w_query = bell_draw(key_list[6], (D, H * HD), D ** -0.5, 0.15625, ((0, 8),))
    w_keyval = bell_draw(key_list[7], (D, 2 * KVH * HD), D ** -0.5, 0.15625, ((0, 8),))
    w_output = bell_draw(key_list[8], (H * HD, D), 2 ** -0.5, 4.0, ((0, 8),))
    w_router = bell_draw(key_list[9], (D, EXPERTS), 0.0128, 0.079589844, ((0, 8),))
    w_gate_up = bell_draw(key_list[10], (EXPERTS, D, 2 * FF), D ** -0.5, 0.15625, ((0, 8),))
    w_down = bell_draw(key_list[11], (EXPERTS, FF, D), (FF // 16) ** -0.5, 1.0, ((0, 8),))
    return {"tokens": tokens, "lengths": lengths, "routes": routes, "cotangent": cotangent, "gain_attn": gain_attn, "gain_moe": gain_moe, "w_query": w_query, "w_keyval": w_keyval, "w_output": w_output, "w_router": w_router, "w_gate_up": w_gate_up, "w_down": w_down}


NORM_EPS = 1e-06
ROPE_BASE = 10000.0
MASK_FLOOR = -1e+30

@jax.custom_vjp
def low(v):
    return lax.optimization_barrier(v.astype(jnp.bfloat16)).astype(jnp.float32)

@jax.custom_vjp
def low_back(v):
    return v

def low_keep(v):
    return (low(v), None)

def low_pass(kept, grad):
    return (grad,)

def back_keep(v):
    return (v, None)

def back_low(kept, grad):
    return (low(grad),)
low.defvjp(low_keep, low_pass)
low_back.defvjp(back_keep, back_low)

def matmul(left, right):
    return jnp.dot(left, right, precision=lax.Precision.HIGHEST)

def rotary(values, places, sine_sign):
    half_dim = values.shape[-1] // 2
    frequency = ROPE_BASE ** (-jnp.arange(half_dim, dtype=jnp.float32) * 2.0 / values.shape[-1])
    angles = places.astype(jnp.float32)[:, None] * frequency[None, :]
    cosine = jnp.cos(angles)[:, None, :]
    sine_part = sine_sign * jnp.sin(angles)[:, None, :]
    first_half = values[..., :half_dim]
    second_half = values[..., half_dim:]
    return jnp.concatenate([first_half * cosine - second_half * sine_part, second_half * cosine + first_half * sine_part], -1)

def attend(queries, keys, values, valid_rows, positions):
    block_rows = math.gcd(LEN, 512)
    block_count = LEN // block_rows
    score_scale = HD ** (-0.5)

    def one_block(item):
        query_block, query_places = item
        scores = low_back(jnp.einsum('rkgd,nkd->kgrn', query_block, keys, precision=lax.Precision.HIGHEST) * score_scale)
        allowed = (positions[None, :] <= query_places[:, None]) & valid_rows[None, :]
        masked = jnp.where(allowed, scores, MASK_FLOOR)
        top_score = lax.optimization_barrier(jnp.max(masked, -1, keepdims=True))
        weights = jnp.where(allowed, jnp.exp(masked - top_score), 0.0)
        total = lax.optimization_barrier(jnp.sum(weights, -1))
        unscaled = low_back(jnp.einsum('kgrn,nkd->kgrd', low(weights), values, precision=lax.Precision.HIGHEST))
        result = unscaled / total[..., None]
        return jnp.transpose(result, (2, 0, 1, 3)).reshape(block_rows, H * HD)
    outputs = lax.map(jax.checkpoint(one_block), (queries.reshape(block_count, block_rows, KVH, H // KVH, HD), positions.reshape(block_count, block_rows)))
    return outputs.reshape(LEN, H * HD)

def expert_block(hn_block, route_block, gate_block, gate_up_w, down_w):
    route_hits = route_block[:, :, None] == jnp.arange(EXPERTS, dtype=jnp.int32)[None, None, :]
    counts = lax.optimization_barrier(jnp.sum(route_hits.astype(jnp.int32), 1))
    places = jnp.cumsum(counts, 0) - 1
    slot_index = lax.optimization_barrier(jnp.sum(jnp.where(route_hits, places[:, None, :], 0), -1)).astype(jnp.int32)
    token_ids = jnp.broadcast_to(jnp.arange(TOK_DEV, dtype=jnp.int32)[:, None], (TOK_DEV, TOPK))
    source = jnp.full((EXPERTS, CAP), TOK_DEV, jnp.int32).at[route_block, slot_index].set(token_ids)
    padded = jnp.concatenate([hn_block, jnp.zeros((1, D), hn_block.dtype)], 0)
    expert_in = low_back(padded[source])
    gate_up = low_back(jnp.einsum('ecd,edf->ecf', expert_in, gate_up_w, precision=lax.Precision.HIGHEST))
    activity = jax.nn.silu(gate_up[..., :FF]) * gate_up[..., FF:]
    expert_out = low_back(low(jnp.einsum('ecf,efd->ecd', low(activity), down_w, precision=lax.Precision.HIGHEST)))
    picked = expert_out[route_block, slot_index]
    return lax.optimization_barrier(jnp.sum(gate_block[..., None] * picked, 1))

def layer(inputs, valid_rows, positions, route, gain_one, gain_two, query_w, keyval_w, output_w, router_w, gate_up_w, down_w):
    kv_width = KVH * HD
    inv_one = lax.rsqrt(lax.optimization_barrier(jnp.mean(inputs * inputs, -1, keepdims=True)) + NORM_EPS)
    hn_one = low(inputs * inv_one * gain_one)
    query_raw = low_back(matmul(hn_one, query_w))
    keyval_raw = low_back(matmul(hn_one, keyval_w))
    queries = low(rotary(query_raw.reshape(LEN, H, HD), positions, 1.0)).reshape(LEN, KVH, H // KVH, HD)
    keys = low(rotary(keyval_raw[:, :kv_width].reshape(LEN, KVH, HD), positions, 1.0))
    values = low(keyval_raw[:, kv_width:].reshape(LEN, KVH, HD))
    attn_heads = attend(queries, keys, values, valid_rows, positions)
    resid = inputs + low_back(matmul(low(attn_heads), output_w))
    inv_two = lax.rsqrt(lax.optimization_barrier(jnp.mean(resid * resid, -1, keepdims=True)) + NORM_EPS)
    hn_two = low(resid * inv_two * gain_two)
    logits = low_back(matmul(hn_two, router_w))
    route_hits = route[:, :, None] == jnp.arange(EXPERTS, dtype=jnp.int32)[None, None, :]
    chosen = lax.optimization_barrier(jnp.sum(jnp.where(route_hits, logits[:, None, :], 0.0), -1))
    gates = jax.nn.softmax(chosen, -1)
    block_count = LEN // TOK_DEV
    mixed = jax.vmap(expert_block, in_axes=(0, 0, 0, None, None))(hn_two.reshape(block_count, TOK_DEV, D), route.reshape(block_count, TOK_DEV, TOPK), gates.reshape(block_count, TOK_DEV, TOPK), gate_up_w, down_w)
    return jnp.where(valid_rows[:, None], resid + mixed.reshape(LEN, D), 0.0)

def reference(tokens, lengths, routes, cotangent, gain_attn, gain_moe, w_query, w_keyval, w_output, w_router, w_gate_up, w_down):
    params = tuple((item.astype(jnp.float32) for item in (gain_attn, gain_moe, w_query, w_keyval, w_output, w_router, w_gate_up, w_down)))
    positions = jnp.arange(LEN, dtype=jnp.int32)

    def per_slot(totals, item):
        slot_tokens, slot_length, slot_route, slot_grad = item
        valid_rows = positions < slot_length

        def forward(inputs, *weights_in):
            return layer(inputs, valid_rows, positions, slot_route, *weights_in)
        result, pull = jax.vjp(forward, slot_tokens.astype(jnp.float32), *params)
        pulled = pull(slot_grad.astype(jnp.float32))
        totals = tuple((left + right for left, right in zip(totals, pulled[1:])))
        return (totals, (result.astype(jnp.bfloat16), pulled[0].astype(jnp.bfloat16)))
    initial = tuple((jnp.zeros_like(item) for item in params))
    totals, (outcome, grad_tokens) = lax.scan(per_slot, initial, (tokens, lengths, routes, cotangent))
    return (outcome, grad_tokens, totals[0], totals[1], totals[2], totals[3], totals[4], totals[5], totals[6], totals[7])
```

```python
import functools

import jax
import jax.numpy as jnp
from jax import lax
from jax.experimental import pallas as pl
from jax.experimental.pallas import tpu as pltpu
from jax.sharding import PartitionSpec as P

HD = 64
NORM_EPS = 1e-06
ROPE_BASE = 10000.0
MASK_FLOOR = -1e30
F32 = jnp.float32
BF16 = jnp.bfloat16
MIB = 1024 * 1024
SIDE = 128


def params(mib):
    return pltpu.CompilerParams(vmem_limit_bytes=mib * MIB)


def cost(flops):
    return pl.CostEstimate(flops=int(flops), bytes_accessed=int(flops) // 512, transcendentals=0)


def up(v):
    return v.astype(F32)


def low(v):
    return v.astype(BF16)


def dot_nn(a, b):
    return lax.dot_general(a, b, (((1,), (0,)), ((), ())), preferred_element_type=F32)


def dot_nt(a, b):
    return lax.dot_general(a, b, (((1,), (1,)), ((), ())), preferred_element_type=F32)


def dot_tn(a, b):
    return lax.dot_general(a, b, (((0,), (0,)), ((), ())), preferred_element_type=F32)


def swap(v, mask):
    count = lax.axis_size("dp")
    return lax.ppermute(v, "dp", [(i, i ^ mask) for i in range(count)])


def halves(v):
    mid = v.shape[0] // 2
    return [v[:mid], v[mid:]]


class Gather:
    def __init__(self, v):
        self.special = lax.axis_size("dp") == 8
        self.stage = 0
        self.live = [v]

    def near(self):
        if self.special and self.stage == 0:
            v = self.live[0]
            self.live = [v, swap(v, 2), swap(v, 4)]
        self.stage = max(self.stage, 1)

    def far(self):
        self.near()
        if self.special and self.stage == 1:
            v, along_x, along_y = self.live
            self.live = self.live + [swap(halves(along_x)[0], 4), swap(halves(along_y)[1], 2)]
        self.stage = max(self.stage, 2)

    def pieces(self):
        self.far()
        if not self.special:
            out = [[self.live[0]]]
            bit = 1
            while bit < lax.axis_size("dp"):
                out = out + [[swap(h, bit) for h in piece] for piece in out]
                bit *= 2
            return out
        v, along_x, along_y, far_a, far_b = self.live
        even = [[v], [along_x], [along_y], [far_a, far_b]]
        out = []
        for piece in even:
            out += [piece, [swap(h, 1) for h in piece]]
        return out


def sync(*items):
    plain = [i.live if isinstance(i, (Gather, Scatter)) else i for i in items]
    plain = lax.optimization_barrier(plain)
    for item, got in zip(items, plain):
        if isinstance(item, (Gather, Scatter)):
            item.live = list(got)
    return plain


def add_low(a, b):
    return low(up(a) + up(b))


class Scatter:
    def __init__(self, even, odd):
        self.special = lax.axis_size("dp") == 8
        self.rows = even.shape[0] * 2 // lax.axis_size("dp")
        self.live = [even, odd]

    def core(self):
        even, odd = self.live
        self.live = [even, swap(odd, 1)]

    def part(self, n, lo, hi):
        at = slice(n * self.rows + lo, n * self.rows + hi)
        return up(self.live[0][at]) + up(self.live[1][at])

    def far(self):
        if not self.special:
            held = add_low(self.live[0], self.live[1])
            bit = lax.axis_size("dp") // 2
            while bit >= 2:
                cut = held.shape[0] // 2
                held = add_low(held[:cut], swap(held[cut:], bit))
                bit //= 2
            self.live = [held]
            return
        mid, rows = self.rows // 2, self.rows
        from_x = swap(low(self.part(3, 0, mid)), 2)
        from_y = swap(low(self.part(3, mid, rows)), 4)
        self.live = self.live + [from_x, from_y]

    def near(self):
        if not self.special:
            return
        mid, rows = self.rows // 2, self.rows
        from_x, from_y = self.live[2:]
        for_x = [low(self.part(1, 0, mid)), low(self.part(1, mid, rows) + up(from_y))]
        for_y = [low(self.part(2, 0, mid) + up(from_x)), low(self.part(2, mid, rows))]
        for_x, for_y = jnp.concatenate(for_x, 0), jnp.concatenate(for_y, 0)
        self.live = [low(self.part(0, 0, rows)), swap(for_x, 2), swap(for_y, 4)]


def total_of(parts):
    out = up(parts[0])
    for p in parts[1:]:
        out = out + up(p)
    return out


def shift(v, step):
    count = lax.axis_size("ctx")
    return lax.ppermute(
        v, "ctx", [(i, i + step) for i in range(count) if 0 <= i + step < count]
    )


class LineSums:
    def __init__(self):
        self.count = lax.axis_size("ctx")
        self.index = lax.axis_index("ctx")
        self.plain = self.count % 2 == 1 or self.count > 4
        self.mid = self.count // 2
        self.stages = 2 * self.mid - 1
        self.waiting = []
        self.moving = [[], []]
        self.done = {}
        self.marks = [[], []]

    def add(self, name, v):
        if self.plain:
            self.done[name] = lax.psum(v, "ctx")
        else:
            self.waiting.append((name, v))

    def send(self, v, stage):
        n, mid = self.count, self.mid
        if stage < mid - 1:
            pairs = [(stage, stage + 1), (n - 1 - stage, n - 2 - stage)]
        elif stage == mid - 1:
            pairs = [(mid - 1, mid), (mid, mid - 1)]
        else:
            k = 2 * mid - 2 - stage
            pairs = [(k + 1, k), (n - 2 - k, n - 1 - k)]
        return lax.ppermute(v, "ctx", pairs)

    def merge(self, v, got, stage):
        if stage <= self.mid - 1:
            return (up(v) + up(got)).astype(v.dtype)
        k = 2 * self.mid - 2 - stage
        return jnp.where((self.index == k) | (self.index == self.count - 1 - k), got, v)

    def busy(self):
        return bool(self.waiting or self.moving[0] or self.moving[1])

    def step(self, *critical):
        if self.plain:
            return critical
        ended = self.moving.pop(0)
        ready = []
        for name, v, got, stage in ended:
            ready.append((name, self.merge(v, got, stage), stage + 1))
        if self.waiting:
            name, v = self.waiting.pop(0)
            ready.append((name, v, 0))
        values, critical = lax.optimization_barrier(([v for _, v, _ in ready], tuple(critical)))
        self.moving.append([])
        for (name, _, stage), v in zip(ready, values):
            if stage == self.stages:
                self.done[name] = v
            else:
                self.moving[-1].append((name, v, self.send(v, stage), stage))
        return critical


def lay_rows(pieces, counts, index, put):
    n = 0
    for k, parts in enumerate(counts):
        rows = sum(pieces[n + i].shape[0] for i in range(parts))
        start = (index ^ k) * rows
        for i in range(parts):
            put(pl.multiple_of(start, 16), pieces[n + i])
            start = start + pieces[n + i].shape[0]
        n += parts


def turn(v, cosine, sine):
    lane = lax.broadcasted_iota(jnp.int32, v.shape, 1)
    first = lax.rem(lane, HD) < HD // 2
    partner = jnp.where(
        first, pltpu.roll(v, 2 * HD - HD // 2, 1), pltpu.roll(v, HD // 2, 1)
    )
    return v * cosine + partner * sine


def project_kernel(counts, blocks, experts, q_width, index_ref, *refs):
    pieces = refs[: sum(counts)]
    seq = refs[sum(counts) : sum(counts) + blocks]
    cos_ref, sin_ref = refs[sum(counts) + blocks : sum(counts) + blocks + 2]
    q_ref, kv_ref, hn_ref, wq_ref, wkv_ref, router_ref, gains_ref, small_ref = refs[
        sum(counts) + blocks + 2 :
    ]
    kv_width = wkv_ref.shape[1]

    def put(start, ref):
        at = pl.ds(start, ref.shape[0])
        wq_ref[at, :] = ref[:, :q_width]
        wkv_ref[at, :] = ref[:, q_width : q_width + kv_width]
        small_ref[at, :] = ref[:, q_width + kv_width :]

    lay_rows(pieces, counts, index_ref[0], put)
    small = up(small_ref[...])
    lane = lax.broadcasted_iota(jnp.int32, small.shape, 1)
    router_ref[...] = low(jnp.where(lane < experts, small, 0.0))
    gains_ref[...] = jnp.transpose(small)[experts : experts + 8]
    gain = gains_ref[0:1, :]
    rows = seq[0].shape[0]
    for r in range(blocks):
        x = up(seq[r][...])
        inv = lax.rsqrt(jnp.mean(x * x, -1, keepdims=True) + NORM_EPS)
        hn_ref[r * rows : (r + 1) * rows, :] = low(x * inv * gain)
    two = 2 * HD
    for c in range(0, q_width, 2 * two):
        raw = dot_nn(hn_ref[:rows, :], wq_ref[:, c : c + 2 * two])
        for d in (0, two):
            rot = turn(raw[:, d : d + two], cos_ref[:rows, :], sin_ref[:rows, :])
            q_ref[:, c + d : c + d + two] = low(up(low(rot)) * (HD ** (-0.5)))
    for r in range(blocks):
        at = slice(r * rows, (r + 1) * rows)
        raw = dot_nn(hn_ref[at, :], wkv_ref[...])
        for d in range(0, kv_width // 2, two):
            kv_ref[at, d : d + two] = low(
                turn(raw[:, d : d + two], cos_ref[at, :], sin_ref[at, :])
            )
        kv_ref[at, kv_width // 2 :] = low(raw[:, kv_width // 2 :])


def project(index, pieces, seq, cosine, sine, experts, q_width):
    counts = [len(p) for p in pieces]
    flat = [h for p in pieces for h in p]
    rows, width = seq[0].shape
    kv_width = flat[0].shape[1] - q_width - 128
    whole = pl.BlockSpec(memory_space=pltpu.VMEM)
    keys = rows * len(seq)
    return pl.pallas_call(
        functools.partial(project_kernel, counts, len(seq), experts, q_width),
        in_specs=[pl.BlockSpec(memory_space=pltpu.SMEM)] + [whole] * (len(flat) + len(seq) + 2),
        out_specs=[whole] * 7,
        out_shape=[
            jax.ShapeDtypeStruct((rows, q_width), BF16),
            jax.ShapeDtypeStruct((keys, kv_width), BF16),
            jax.ShapeDtypeStruct((keys, width), BF16),
            jax.ShapeDtypeStruct((width, q_width), BF16),
            jax.ShapeDtypeStruct((width, kv_width), BF16),
            jax.ShapeDtypeStruct((width, 128), BF16),
            jax.ShapeDtypeStruct((8, width), F32),
        ],
        scratch_shapes=[pltpu.VMEM((width, 128), BF16)],
        compiler_params=params(36),
        cost_estimate=cost(8 * width * (rows * q_width + keys * kv_width)),
        name="project",
    )(index, *flat, *seq, cosine, sine)


def after_attend_kernel(counts, index_ref, *refs):
    pieces = refs[: sum(counts)]
    attn_ref, tok_ref, gains_ref, wo_ref, resid_ref, hn_ref, low_ref = refs[sum(counts) :]

    def put(start, ref):
        wo_ref[pl.ds(start, ref.shape[0]), :] = ref[...]

    lay_rows(pieces, counts, index_ref[0], put)
    attn = low(attn_ref[...])
    low_ref[...] = attn
    resid = up(tok_ref[...]) + dot_nn(attn, wo_ref[...])
    resid_ref[...] = resid
    inv = lax.rsqrt(jnp.mean(resid * resid, -1, keepdims=True) + NORM_EPS)
    hn_ref[...] = low(resid * inv * gains_ref[1:2, :])


def after_attend(index, pieces, attn, tokens, gains):
    counts = [len(p) for p in pieces]
    flat = [h for p in pieces for h in p]
    rows, width = tokens.shape
    heads = attn.shape[1]
    whole = pl.BlockSpec(memory_space=pltpu.VMEM)
    return pl.pallas_call(
        functools.partial(after_attend_kernel, counts),
        in_specs=[pl.BlockSpec(memory_space=pltpu.SMEM)] + [whole] * (len(flat) + 3),
        out_specs=[whole] * 4,
        out_shape=[
            jax.ShapeDtypeStruct((heads, width), BF16),
            jax.ShapeDtypeStruct((rows, width), F32),
            jax.ShapeDtypeStruct((rows, width), BF16),
            jax.ShapeDtypeStruct((rows, heads), BF16),
        ],
        compiler_params=params(24),
        cost_estimate=cost(12 * rows * heads * width),
        name="after_attend",
    )(index, *flat, attn, tokens, gains)


def router_back_kernel(count, experts, *refs):
    parts = refs[:count]
    (
        gates_ref,
        router_ref,
        gains_ref,
        resid_ref,
        cot_ref,
        wo_ref,
        grad_ref,
        attn_ref,
        heads_ref,
        logits_ref,
        gain_ref,
    ) = refs[count:]
    width = resid_ref.shape[1]
    total = up(parts[0][...])
    for p in parts[1:]:
        total = total + up(p[...])
    side = total[:, width:]
    lane = lax.broadcasted_iota(jnp.int32, side.shape, 1)
    gate_grads = jnp.where(lane < experts, side + pltpu.roll(side, SIDE // 2, 1), 0.0)
    gates = gates_ref[...]
    mean = jnp.sum(gates * gate_grads, -1, keepdims=True)
    grad_logits = low(gates * (gate_grads - mean))
    logits_ref[...] = grad_logits
    grad_hn = total[:, :width] + dot_nt(grad_logits, router_ref[...])
    resid = resid_ref[...]
    inv = lax.rsqrt(jnp.mean(resid * resid, -1, keepdims=True) + NORM_EPS)
    normed = resid * inv
    gain_ref[...] = jnp.broadcast_to(jnp.sum(grad_hn * normed, 0, keepdims=True), gain_ref.shape)
    scaled = grad_hn * gains_ref[1:2, :]
    grad = up(cot_ref[...]) + inv * (scaled - normed * jnp.mean(scaled * normed, -1, keepdims=True))
    grad_ref[...] = grad
    grad_low = low(grad)
    attn_ref[...] = grad_low
    heads_ref[...] = dot_nt(grad_low, wo_ref[...])


def router_back(parts, gates, router, gains, resid, cot, wo, experts):
    rows, width = resid.shape
    heads = wo.shape[0]
    whole = pl.BlockSpec(memory_space=pltpu.VMEM)
    return pl.pallas_call(
        functools.partial(router_back_kernel, len(parts), experts),
        in_specs=[whole] * (len(parts) + 6),
        out_specs=[whole] * 5,
        out_shape=[
            jax.ShapeDtypeStruct((rows, width), F32),
            jax.ShapeDtypeStruct((rows, width), BF16),
            jax.ShapeDtypeStruct((rows, heads), F32),
            jax.ShapeDtypeStruct((rows, SIDE), BF16),
            jax.ShapeDtypeStruct((8, width), F32),
        ],
        compiler_params=params(28),
        cost_estimate=cost(14 * rows * heads * width),
        name="router_back",
    )(*parts, gates, router, gains, resid, cot, wo)


def transposed(v):
    return jnp.transpose(up(v))


def key_bias(place_ref, keys, rows):
    j = lax.broadcasted_iota(jnp.int32, (keys, rows), 0)
    i = lax.broadcasted_iota(jnp.int32, (keys, rows), 1)
    block = lax.div(j, rows)
    place = (place_ref[0] - block) * rows + (j - block * rows)
    allowed = (place >= 0) & (place <= place_ref[0] * rows + i) & (place < place_ref[1])
    return jnp.where(allowed, 0.0, MASK_FLOOR)


def widened(part, group):
    zero = jnp.zeros_like(part)
    return jnp.concatenate([part, zero] if group == 0 else [zero, part], 0)


def attend_kernel(groups, place_ref, q_ref, k_ref, v_ref, out_ref, max_ref, total_ref, bias_ref):
    rows = q_ref.shape[0]
    keys = k_ref.shape[0]

    @pl.when(pl.program_id(0) == 0)
    def _():
        bias_ref[...] = key_bias(place_ref, keys, rows)

    q_t = low(transposed(q_ref[...]))
    v_t = low(transposed(v_ref[...]))
    outs, maxes, totals = [], [], []
    for group in range(2):
        parts = [
            widened(q_t[(group * groups + h) * HD : (group * groups + h + 1) * HD], group)
            for h in range(groups)
        ]
        scores = dot_nn(k_ref[...], jnp.concatenate(parts, 1))
        weights = []
        for h in range(groups):
            s = scores[:, h * rows : (h + 1) * rows] + bias_ref[...]
            top = jnp.max(s, 0, keepdims=True)
            w = jnp.exp(s - top)
            totals.append(jnp.sum(w, 0, keepdims=True))
            maxes.append(top)
            weights.append(low(w))
        mixed = dot_nn(v_t, jnp.concatenate(weights, 1))
        for h in range(groups):
            part = mixed[group * HD : (group + 1) * HD, h * rows : (h + 1) * rows]
            outs.append(part / totals[group * groups + h])
    out_ref[...] = jnp.transpose(jnp.concatenate(outs, 0))
    pad = [jnp.ones((8 - 2 * groups, rows), F32)] if 2 * groups < 8 else []
    max_ref[0] = jnp.concatenate(maxes + pad, 0)
    total_ref[0] = jnp.concatenate(totals + pad, 0)


def attend(place, queries, keyval, groups):
    rows, width = queries.shape
    keys, kv = keyval.shape
    steps = kv // 2 // (2 * HD)
    heads = 2 * groups * HD
    return pl.pallas_call(
        functools.partial(attend_kernel, groups),
        grid_spec=pltpu.PrefetchScalarGridSpec(
            num_scalar_prefetch=1,
            grid=(steps,),
            in_specs=[
                pl.BlockSpec((rows, heads), lambda i, s: (0, i)),
                pl.BlockSpec((keys, 2 * HD), lambda i, s: (0, i)),
                pl.BlockSpec((keys, 2 * HD), lambda i, s: (0, steps + i)),
            ],
            out_specs=[
                pl.BlockSpec((rows, heads), lambda i, s: (0, i)),
                pl.BlockSpec((1, 8, rows), lambda i, s: (i, 0, 0)),
                pl.BlockSpec((1, 8, rows), lambda i, s: (i, 0, 0)),
            ],
            scratch_shapes=[pltpu.VMEM((keys, rows), F32)],
        ),
        out_shape=[
            jax.ShapeDtypeStruct((rows, width), F32),
            jax.ShapeDtypeStruct((steps, 8, rows), F32),
            jax.ShapeDtypeStruct((steps, 8, rows), F32),
        ],
        compiler_params=params(28),
        cost_estimate=cost(40 * rows * keys * width),
        name="attend",
    )(place, queries, keyval, keyval)


def attend_back_kernel(
    groups,
    place_ref,
    q_ref,
    k_ref,
    v_ref,
    grad_ref,
    out_ref,
    max_ref,
    total_ref,
    cos_ref,
    sin_ref,
    gq_ref,
    gk_ref,
    gv_ref,
    bias_ref,
):
    rows = q_ref.shape[0]
    keys = k_ref.shape[0]
    chunk = 256

    @pl.when(pl.program_id(0) == 0)
    def _():
        bias_ref[...] = key_bias(place_ref, keys, rows)

    q_t = low(transposed(q_ref[...]))
    k_t = low(transposed(k_ref[...]))
    grad_t = transposed(grad_ref[...])
    out_t = transposed(out_ref[...])
    q_parts, g_parts, deltas, tops, grads = [], [], [], [], []
    for group in range(2):
        q_part, g_part, delta = [], [], []
        for h in range(groups):
            n = group * groups + h
            total = total_ref[0, n : n + 1]
            grad = grad_t[n * HD : (n + 1) * HD]
            q_part.append(widened(q_t[n * HD : (n + 1) * HD], group))
            g_part.append(widened(low(grad / total), group))
            delta.append(jnp.sum(out_t[n * HD : (n + 1) * HD] * grad, 0, keepdims=True) / total)
        q_parts.append(jnp.concatenate(q_part, 1))
        g_parts.append(jnp.concatenate(g_part, 1))
        deltas.append(jnp.concatenate(delta, 1))
        tops.append(
            jnp.concatenate(
                [max_ref[0, group * groups + h : group * groups + h + 1] for h in range(groups)], 1
            )
        )
        grads.append(jnp.zeros((2 * HD, groups * rows), F32))
    for start in range(0, keys, chunk):
        bias = bias_ref[start : start + chunk]
        bias = jnp.concatenate([bias] * groups, 1)
        grad_k = jnp.zeros((chunk, 2 * HD), F32)
        grad_v = jnp.zeros((chunk, 2 * HD), F32)
        for group in range(2):
            scores = dot_nn(k_ref[start : start + chunk], q_parts[group])
            w = jnp.exp(scores + bias - tops[group])
            gp = dot_nn(v_ref[start : start + chunk], g_parts[group])
            gs = low(w * (gp - deltas[group]))
            grad_v = grad_v + dot_nt(low(w), g_parts[group])
            grad_k = grad_k + dot_nt(gs, q_parts[group])
            grads[group] = grads[group] + dot_nn(k_t[:, start : start + chunk], gs)
        at = slice(start, start + chunk)
        gk_ref[at] = low(turn(grad_k, cos_ref[at, :], -sin_ref[at, :]))
        gv_ref[at] = low(grad_v)
    parts = []
    for group in range(2):
        for h in range(groups):
            parts.append(grads[group][group * HD : (group + 1) * HD, h * rows : (h + 1) * rows])
    grad_q = jnp.transpose(jnp.concatenate(parts, 0)) * (HD ** (-0.5))
    for d in range(0, 2 * groups * HD, 2 * HD):
        gq_ref[:, d : d + 2 * HD] = low(
            turn(grad_q[:, d : d + 2 * HD], cos_ref[:rows, :], -sin_ref[:rows, :])
        )


def attend_back(place, queries, keyval, grad_heads, attn, tops, totals, cosine, sine, groups):
    rows, width = queries.shape
    keys, kv = keyval.shape
    steps = kv // 2 // (2 * HD)
    heads = 2 * groups * HD
    head_spec = pl.BlockSpec((rows, heads), lambda i, s: (0, i))
    key_spec = pl.BlockSpec((keys, 2 * HD), lambda i, s: (0, i))
    stat_spec = pl.BlockSpec((1, 8, rows), lambda i, s: (i, 0, 0))
    return pl.pallas_call(
        functools.partial(attend_back_kernel, groups),
        grid_spec=pltpu.PrefetchScalarGridSpec(
            num_scalar_prefetch=1,
            grid=(steps,),
            in_specs=[
                head_spec,
                key_spec,
                pl.BlockSpec((keys, 2 * HD), lambda i, s: (0, steps + i)),
                head_spec,
                head_spec,
                stat_spec,
                stat_spec,
                pl.BlockSpec((keys, 2 * HD), lambda i, s: (0, 0)),
                pl.BlockSpec((keys, 2 * HD), lambda i, s: (0, 0)),
            ],
            out_specs=[head_spec, key_spec, key_spec],
            scratch_shapes=[pltpu.VMEM((keys, rows), F32)],
        ),
        out_shape=[
            jax.ShapeDtypeStruct((rows, width), BF16),
            jax.ShapeDtypeStruct((keys, kv // 2), BF16),
            jax.ShapeDtypeStruct((keys, kv // 2), BF16),
        ],
        compiler_params=params(36),
        cost_estimate=cost(64 * rows * keys * width),
        name="attend_back",
    )(place, queries, keyval, keyval, grad_heads, attn, tops, totals, cosine, sine)


def expert_kernel(counts, cap, tile, experts, number_ref, *refs):
    parts = refs[: sum(counts)]
    cots = refs[sum(counts) : 2 * sum(counts)]
    (
        router_ref,
        wgu_ref,
        wd_ref,
        out_ref,
        gin_ref,
        gwgu_ref,
        gwd_ref,
        slots_ref,
        gates_ref,
        x_ref,
        c_ref,
        ggu_ref,
        act_ref,
        sg_ref,
        turned_ref,
    ) = refs[2 * sum(counts) :]
    blocks = len(counts)
    width = wd_ref.shape[1]
    rows = parts[0].shape[0]
    hidden = wd_ref.shape[0]
    total = blocks * cap
    expert = number_ref[1]
    below = lax.broadcasted_iota(jnp.int32, (rows, rows), 1) <= lax.broadcasted_iota(
        jnp.int32, (rows, rows), 0
    )
    below = low(jnp.where(below, 1.0, 0.0))
    place = lax.broadcasted_iota(jnp.int32, (cap, rows), 0)
    n = 0
    for b in range(blocks):
        hn, cot = parts[n : n + counts[b]], cots[n : n + counts[b]]
        n += counts[b]
        hits = jnp.concatenate([part[:, width:] for part in cot], 0)
        named = up(hits) > 0.5
        order = jnp.where(named, dot_nn(below, hits) - 1.0, -1.0)
        logits = [dot_nn(part[...], router_ref[...]) for part in hn]
        logits = jnp.where(named, jnp.concatenate(logits, 0), MASK_FLOOR)
        gates = jnp.where(named, jnp.exp(logits - jnp.max(logits, -1, keepdims=True)), 0.0)
        gates = gates / jnp.sum(gates, -1, keepdims=True)
        if b == 0:
            gates_ref[...] = gates
        turned_ref[0] = jnp.transpose(order)
        turned_ref[1] = jnp.transpose(gates)
        slot = turned_ref[0, pl.ds(expert, 1), :].astype(jnp.int32)
        slots_ref[b : b + 1, :] = slot
        hit = place == slot
        pick = low(jnp.where(hit, 1.0, 0.0))
        at = slice(b * cap, (b + 1) * cap)
        for from_parts, to_ref in ((hn, x_ref), (cot, c_ref)):
            taken, start = None, 0
            for part in from_parts:
                piece = dot_nn(pick[:, start : start + part.shape[0]], part[:, :width])
                taken = piece if taken is None else taken + piece
                start += part.shape[0]
            to_ref[at, :] = low(taken)
        gate = jnp.sum(
            jnp.where(hit, turned_ref[1, pl.ds(expert, 1), :], 0.0), 1, keepdims=True
        )
        sg_ref[at, :] = jnp.broadcast_to(gate, (cap, 128))

    def middle(t, carry):
        at = pl.ds(pl.multiple_of(t * tile, 16), tile)
        gate_up = dot_nn(x_ref[at, :], wgu_ref[...])
        g = gate_up[:, :hidden]
        u = gate_up[:, hidden:]
        sigma = jax.nn.sigmoid(g)
        silu = g * sigma
        act = low(silu * u)
        slot_gate = sg_ref[at, :][:, :1]
        back = dot_nt(c_ref[at, :], wd_ref[...])
        gate_grad = jnp.sum(up(act) * back, 1, keepdims=True)
        back = back * slot_gate
        act_ref[at, :] = low(up(act) * slot_gate)
        ggu_ref[at, :hidden] = low(back * u * (sigma * (1.0 + g * (1.0 - sigma))))
        ggu_ref[at, hidden:] = low(back * silu)
        out_ref[at, :] = low(dot_nn(act, wd_ref[...]) * slot_gate)
        gin_ref[at, :width] = low(dot_nt(ggu_ref[at, :], wgu_ref[...]))
        lane = lax.broadcasted_iota(jnp.int32, (tile, SIDE), 1)
        high = up(low(gate_grad))
        side = jnp.where(lane == expert, high, 0.0)
        side = jnp.where(lane == expert + SIDE // 2, gate_grad - high, side)
        gin_ref[at, width:] = low(side)
        return carry

    lax.fori_loop(0, total // tile, middle, 0)
    step = 256

    def down_grad(t, carry):
        at = pl.ds(pl.multiple_of(t * step, step), step)
        gwd_ref[at, :] = low(dot_tn(act_ref[:, at], c_ref[...]))
        return carry

    lax.fori_loop(0, hidden // step, down_grad, 0)

    def up_grad(t, carry):
        at = pl.ds(pl.multiple_of(t * step, step), step)
        gwgu_ref[at, :] = low(dot_tn(x_ref[:, at], ggu_ref[...]))
        return carry

    lax.fori_loop(0, width // step, up_grad, 0)


def run_expert(number, pieces, cots, router, wgu, wd, cap, experts):
    counts = [len(p) for p in pieces]
    flat = [h for p in pieces for h in p] + [h for p in cots for h in p]
    blocks = len(counts)
    rows = flat[0].shape[0]
    width = wd.shape[1]
    hidden = wd.shape[0]
    total = blocks * cap
    tile = max(t for t in range(16, 401, 16) if total % t == 0)
    whole = pl.BlockSpec(memory_space=pltpu.VMEM)
    return pl.pallas_call(
        functools.partial(expert_kernel, counts, cap, tile, experts),
        in_specs=[pl.BlockSpec(memory_space=pltpu.SMEM)] + [whole] * (len(flat) + 3),
        out_specs=[whole] * 6,
        out_shape=[
            jax.ShapeDtypeStruct((total, width), BF16),
            jax.ShapeDtypeStruct((total, width + SIDE), BF16),
            jax.ShapeDtypeStruct((width, 2 * hidden), BF16),
            jax.ShapeDtypeStruct((hidden, width), BF16),
            jax.ShapeDtypeStruct((blocks, rows), jnp.int32),
            jax.ShapeDtypeStruct((rows, SIDE), F32),
        ],
        scratch_shapes=[
            pltpu.VMEM((total, width), BF16),
            pltpu.VMEM((total, width), BF16),
            pltpu.VMEM((total, 2 * hidden), BF16),
            pltpu.VMEM((total, hidden), BF16),
            pltpu.VMEM((total, 128), F32),
            pltpu.VMEM((2, SIDE, rows), F32),
        ],
        compiler_params=params(52),
        cost_estimate=cost(44 * total * width * hidden),
        name="expert",
    )(number, *flat, router, wgu, wd)


def combine_kernel(count, cap, first, stride, number_ref, *refs):
    slots, parts, out_ref = refs[:count], refs[count : 2 * count], refs[2 * count]
    b = pl.program_id(0) * stride + first
    rows = slots[0].shape[1]
    place = lax.broadcasted_iota(jnp.int32, (cap, rows), 0)
    acc = None
    for e in range(count):
        pick = low(jnp.where(place == slots[e][pl.ds(b, 1), :], 1.0, 0.0))
        part = dot_tn(pick, parts[e][...])
        acc = part if acc is None else acc + part
    out_ref[...] = low(acc)


def combine(number, slots, parts, cap, chosen, order):
    blocks, rows = slots[0].shape
    count = len(parts)
    width = parts[0].shape[1]
    first, stride = chosen.start, chosen.step
    return pl.pallas_call(
        functools.partial(combine_kernel, count, cap, first, stride),
        grid_spec=pltpu.PrefetchScalarGridSpec(
            num_scalar_prefetch=1,
            grid=(len(chosen),),
            in_specs=[pl.BlockSpec((blocks, rows), lambda n, s: (0, 0))] * count
            + [pl.BlockSpec((cap, width), lambda n, s: (n * stride + first, 0))] * count,
            out_specs=pl.BlockSpec((rows, width), lambda n, s: (order(n, s[0]), 0)),
        ),
        out_shape=jax.ShapeDtypeStruct((len(chosen) * rows, width), BF16),
        compiler_params=params(20),
        cost_estimate=cost(10 * len(chosen) * cap * rows * width),
        name="combine",
    )(number, *slots, *parts)


def weight_grad_kernel(count, index_ref, hn_ref, gq_ref, gk_ref, gv_ref, even_ref, odd_ref):
    rows = gq_ref.shape[0]
    size = even_ref.shape[1]
    step = 256

    def put(value, col):
        for j in range(count):
            k = index_ref[0] ^ j
            block = low(value[j * size : (j + 1) * size])

            @pl.when(lax.rem(k, 2) == 0)
            def _():
                even_ref[k // 2, :, col : col + step] = block

            @pl.when(lax.rem(k, 2) == 1)
            def _():
                odd_ref[k // 2, :, col : col + step] = block

    col = 0
    for ref, taken in ((gq_ref, rows), (gk_ref, hn_ref.shape[0]), (gv_ref, hn_ref.shape[0])):
        for c in range(0, ref.shape[1], step):
            put(dot_tn(hn_ref[:taken, :], ref[:, c : c + step]), col)
            col += step


def weight_grad(index, hn, gq, gk, gv):
    count = lax.axis_size("dp")
    width = hn.shape[1]
    cols = gq.shape[1] + gk.shape[1] + gv.shape[1]
    shape = jax.ShapeDtypeStruct((count // 2, width // count, cols), BF16)
    whole = pl.BlockSpec(memory_space=pltpu.VMEM)
    even, odd = pl.pallas_call(
        functools.partial(weight_grad_kernel, count),
        in_specs=[pl.BlockSpec(memory_space=pltpu.SMEM)] + [whole] * 4,
        out_specs=[whole] * 2,
        out_shape=[shape, shape],
        compiler_params=params(32),
        cost_estimate=cost(8 * width * (hn.shape[0] * 2 * gk.shape[1] + gq.shape[0] * gq.shape[1])),
        name="weight_grad",
    )(index, hn, gq, gk, gv)
    return even.reshape(-1, cols), odd.reshape(-1, cols)


def rope_tables(places):
    half = HD // 2
    frequency = ROPE_BASE ** (-jnp.arange(half, dtype=F32) * 2.0 / HD)
    angles = places.astype(F32)[:, None] * frequency[None, :]
    cosine, sine = jnp.cos(angles), jnp.sin(angles)
    return jnp.concatenate([cosine] * 4, 1), jnp.concatenate([-sine, sine] * 2, 1)


def per_device(
    tokens,
    lengths,
    routes,
    cotangent,
    gain_attn,
    gain_moe,
    w_query,
    w_keyval,
    w_output,
    w_router,
    w_gate_up,
    w_down,
):
    rows = tokens.shape[1]
    width = tokens.shape[2]
    experts = w_router.shape[1]
    local_experts = w_gate_up.shape[0]
    kv_width = w_keyval.shape[1] // 2
    head_total = w_query.shape[1]
    groups = head_total // kv_width
    dp_count = lax.axis_size("dp")
    ctx_count = lax.axis_size("ctx")
    dp_index = lax.axis_index("dp").astype(jnp.int32)
    ctx_index = lax.axis_index("ctx").astype(jnp.int32)
    cap = -(-(rows * 9 // 16) // 16) * 16
    length = lengths[0]
    places = ctx_index * rows + jnp.arange(rows, dtype=jnp.int32)
    valid = (places < length)[:, None]
    index = jnp.reshape(dp_index, (1,))

    pad = jnp.zeros((w_router.shape[0], 128 - experts - 2), BF16)
    first_w = Gather(
        jnp.concatenate(
            [w_query, w_keyval, w_router, gain_attn[:, None], gain_moe[:, None], pad], 1
        )
    )
    output_g = Gather(w_output)

    seq = [tokens[0]]
    for n in range(ctx_count - 1):
        seq.append(shift(seq[-1], 1))
        if n == 0:
            first_w.near()
        elif n == 1:
            first_w.far()
        elif n == 2:
            output_g.near()
        seq[-1] = sync(seq[-1], first_w, output_g)[0]
    back = jnp.arange(ctx_count, dtype=jnp.int32)[:, None] * rows
    cosine, sine = rope_tables((places[None, :] - back).reshape(-1))

    hits = jnp.any(routes[0][..., None] == jnp.arange(SIDE, dtype=jnp.int32), 1)
    grad_y = jnp.where(valid, cotangent[0], BF16(0))
    cot = Gather(jnp.concatenate([grad_y, hits.astype(BF16)], 1))

    first_pieces = first_w.pieces()
    projected = project(index, first_pieces, seq, cosine, sine, experts, head_total)
    output_g.far()
    projected = sync(projected, output_g, cot)[0]
    queries, keyval, hn_seq, query_w, keyval_w, router_w, gains = projected

    place = jnp.stack([ctx_index, length])
    attended = attend(place, queries, keyval, groups)
    output_pieces = output_g.pieces()
    cot.near()
    attended = sync(attended, cot)[0]
    attn, tops, totals = attended
    cot.far()
    output_w, resid, hn_two, attn_low = sync(
        after_attend(index, output_pieces, attn, tokens[0], gains), cot
    )[0]

    hn_g = Gather(hn_two)
    hn_g.near()
    cot_pieces = cot.pieces()
    cot_pieces = sync(cot_pieces, hn_g)[0]
    hn_pieces = hn_g.pieces()
    sums = LineSums()
    outs, gins, slots = [], [], []
    chunks = 2 if ctx_count == 4 else 1
    for e in range(local_experts):
        number = jnp.stack([dp_index, dp_index * local_experts + e])
        out, gin, gwgu, gwd, slot, gates = run_expert(
            number, hn_pieces, cot_pieces, router_w, w_gate_up[e], w_down[e], cap, experts
        )
        outs.append(out)
        gins.append(gin)
        slots.append(slot)
        for c, v in enumerate(jnp.split(gwd, chunks, 0)):
            sums.add(("down", e, c), v)
        for c, v in enumerate(jnp.split(gwgu, 2 * chunks, 0)):
            sums.add(("up", e, c), v)
        if e + 1 < local_experts:
            hn_pieces, cot_pieces = sums.step(hn_pieces, cot_pieces)
            hn_pieces, cot_pieces = sums.step(hn_pieces, cot_pieces)
    gins, slots = sums.step(gins, slots)
    gins, slots = sums.step(gins, slots)
    half = dp_count // 2
    odd = combine(index, slots, gins, cap, range(1, dp_count, 2), lambda n, i: n)
    even = combine(index, slots, gins, cap, range(0, dp_count, 2), lambda n, i: n)
    gin_s = Scatter(even, odd)
    gin_s.core()
    gin_s.live = sums.step(gin_s.live)[0]
    gin_s.far()
    sync(gin_s)
    gin_s.near()
    gin_s.live, gates = sums.step(gin_s.live, gates)

    backed = router_back(gin_s.live, gates, router_w, gains, resid, grad_y, output_w, experts)
    grad_resid, grad_attn, grad_heads, grad_logits, part_gain_two = sums.step(*backed)
    part_output = low(dot_tn(attn_low, grad_attn))
    share_output = lax.psum_scatter(part_output, "dp", scatter_dimension=0, tiled=True)

    grad_query, grad_keys, grad_values = sums.step(
        *attend_back(
            place, queries, keyval, grad_heads, attn, tops, totals, cosine, sine, groups
        )
    )
    grad_kv = jnp.concatenate([grad_keys, grad_values], 1)
    blocks = [grad_kv[r * rows : (r + 1) * rows] for r in range(ctx_count)]
    even, odd = weight_grad(index, hn_seq, grad_query, grad_keys, grad_values)
    first_s = Scatter(even, odd)
    first_s.core()
    held = shift(blocks[-1], -1) if ctx_count > 1 else blocks[0]
    first_s.live, held = sums.step(first_s.live, held)
    first_s.far()
    for r in range(ctx_count - 2, -1, -1):
        held = add_low(held, blocks[r])
        if r:
            held = shift(held, -1)
        if r == 1:
            sync(first_s)
            first_s.near()
        if r > 0:
            first_s.live, held = sums.step(first_s.live, held)
    share_first = low(total_of(first_s.live))
    sums.add("first", share_first)
    sums.add("output", share_output)

    grad_hn_one = dot_nt(grad_query, query_w) + dot_nt(held, keyval_w)
    inputs = up(tokens[0])
    inv_one = lax.rsqrt(jnp.mean(inputs * inputs, -1, keepdims=True) + NORM_EPS)
    normed_one = inputs * inv_one
    scaled_one = grad_hn_one * gains[0:1]
    grad_inputs = grad_resid + inv_one * (
        scaled_one - normed_one * jnp.mean(scaled_one * normed_one, -1, keepdims=True)
    )
    grad_inputs = low(grad_inputs)

    part_router = dot_tn(hn_two, grad_logits)[:, :experts]
    part_gains = jnp.stack([jnp.sum(grad_hn_one * normed_one, 0), part_gain_two[0]], 1)
    part_small = jnp.concatenate([part_router, part_gains], 1)
    grad_inputs, part_small = sums.step(grad_inputs, part_small)
    share_small = lax.psum_scatter(part_small, "dp", scatter_dimension=0, tiled=True)

    out_tokens = combine(index, slots, outs, cap, range(0, dp_count, 1), lambda n, i: n ^ i)
    (out_tokens,) = sums.step(out_tokens)
    moe = lax.psum_scatter(out_tokens, "dp", scatter_dimension=0, tiled=True)
    outcome = low(jnp.where(valid, resid + up(moe), 0.0))
    sums.step()
    (share_small,) = sums.step(share_small)
    sums.add("small", share_small)

    while sums.busy():
        sums.step()
    total_small = sums.done["small"]
    total_first = up(sums.done["first"])
    down = [
        jnp.concatenate([up(sums.done["down", e, c]) for c in range(chunks)], 0)
        for e in range(local_experts)
    ]
    gate_up = [
        jnp.concatenate([up(sums.done["up", e, c]) for c in range(2 * chunks)], 0)
        for e in range(local_experts)
    ]
    return (
        outcome[None],
        grad_inputs[None],
        total_small[:, experts],
        total_small[:, experts + 1],
        total_first[:, :head_total],
        total_first[:, head_total:],
        up(sums.done["output"]),
        total_small[:, :experts],
        jnp.stack(gate_up),
        jnp.stack(down),
    )


def solution(mesh):
    in_specs = (
        P("dp", "ctx", None),
        P("dp"),
        P("dp", "ctx", None),
        P("dp", "ctx", None),
        P("dp"),
        P("dp"),
        P("dp", None),
        P("dp", None),
        P("dp", None),
        P("dp", None),
        P("dp", None, None),
        P("dp", None, None),
    )
    out_specs = (
        P("dp", "ctx", None),
        P("dp", "ctx", None),
        P("dp"),
        P("dp"),
        P("dp", None),
        P("dp", None),
        P("dp", None),
        P("dp", None),
        P("dp", None, None),
        P("dp", None, None),
    )
    return jax.shard_map(
        per_device, mesh=mesh, in_specs=in_specs, out_specs=out_specs, check_vma=False
    )
```

```python
import functools

import jax
import jax.numpy as jnp
from jax import lax
from jax.experimental import pallas as pl
from jax.experimental.pallas import tpu as pltpu
from jax.sharding import PartitionSpec as P

HD = 64
NORM_EPS = 1e-06
ROPE_BASE = 10000.0
MASK_FLOOR = -1e30
F32 = jnp.float32
BF16 = jnp.bfloat16
MIB = 1024 * 1024
SIDE = 128
WHOLE = pl.BlockSpec()


def params(mib):
    return pltpu.CompilerParams(vmem_limit_bytes=mib * MIB)


def hbm(*arrays_in):
    return [pltpu.with_memory_space_constraint(v, pltpu.HBM) for v in arrays_in]


def cost(flops):
    return pl.CostEstimate(flops=int(flops) // 64, bytes_accessed=1024, transcendentals=0)


def up(v):
    return v.astype(F32)


def low(v):
    return v.astype(BF16)


def dot_nn(a, b):
    return lax.dot_general(a, b, (((1,), (0,)), ((), ())), preferred_element_type=F32)


def dot_nt(a, b):
    return lax.dot_general(a, b, (((1,), (1,)), ((), ())), preferred_element_type=F32)


def dot_tn(a, b):
    return lax.dot_general(a, b, (((0,), (0,)), ((), ())), preferred_element_type=F32)


def swap(v, mask):
    count = lax.axis_size("dp")
    return lax.ppermute(v, "dp", [(i, i ^ mask) for i in range(count)])


def halves(v):
    mid = v.shape[0] // 2
    return [v[:mid], v[mid:]]


class Gather:
    def __init__(self, v):
        self.special = lax.axis_size("dp") == 8
        self.stage = 0
        self.live = [v]

    def near(self):
        if self.special and self.stage == 0:
            v = self.live[0]
            self.live = [v, swap(v, 2), swap(v, 4)]
        self.stage = max(self.stage, 1)

    def far(self):
        self.near()
        if self.special and self.stage == 1:
            v, along_x, along_y = self.live
            self.live = self.live + [swap(halves(along_x)[0], 4), swap(halves(along_y)[1], 2)]
        self.stage = max(self.stage, 2)

    def pieces(self):
        self.far()
        if not self.special:
            out = [[self.live[0]]]
            bit = 1
            while bit < lax.axis_size("dp"):
                out = out + [[swap(h, bit) for h in piece] for piece in out]
                bit *= 2
            return out
        v, along_x, along_y, far_a, far_b = self.live
        even = [[v], [along_x], [along_y], [far_a, far_b]]
        out = []
        for piece in even:
            out += [piece, [swap(h, 1) for h in piece]]
        return out


def sync(*items):
    plain = [i.live if isinstance(i, Gather) else i for i in items]
    plain = lax.optimization_barrier(plain)
    for item, got in zip(items, plain):
        if isinstance(item, Gather):
            item.live = list(got)
    return plain


def add_low(a, b):
    return low(up(a) + up(b))


def shift(v, step):
    count = lax.axis_size("ctx")
    return lax.ppermute(
        v, "ctx", [(i, i + step) for i in range(count) if 0 <= i + step < count]
    )


class LineSums:
    DEPTH = 1

    def __init__(self):
        count = lax.axis_size("ctx")
        index = lax.axis_index("ctx")
        self.plain = count != 4
        self.outer = (index == 0) | (index == count - 1)
        self.waiting = []
        self.flights = [[] for _ in range(self.DEPTH)]
        self.done = {}

    def add(self, name, v):
        if self.plain:
            self.done[name] = lax.psum(v, "ctx")
        else:
            self.waiting.append((name, v))

    def busy(self):
        return bool(self.waiting or any(self.flights))

    def step(self, *critical, take=1, flush=False):
        if self.plain:
            return critical
        got = self.flights.pop(0)
        while flush and self.flights:
            got = got + self.flights.pop(0)
        ready = {"first": [], "inner": [], "last": []}
        for kind, name, v, arrived in got:
            if kind == "first":
                ready["inner"].append((name, add_low(v, arrived)))
            elif kind == "inner":
                ready["last"].append((name, add_low(v, arrived)))
            else:
                self.done[name] = (v, arrived)
        for _ in range(take):
            if self.waiting:
                ready["first"].append(self.waiting.pop(0))
        shared = []
        for first in list(ready["first"]):
            for last in list(ready["last"]):
                if first[1].shape == last[1].shape:
                    shared.append((first[0], last[0], first[1], jnp.where(self.outer, first[1], last[1])))
                    ready["first"] = [r for r in ready["first"] if r is not first]
                    ready["last"] = [r for r in ready["last"] if r is not last]
                    break
        both = [(own, payload) for _, _, own, payload in shared]
        alone = {kind: [v for _, v in entries] for kind, entries in ready.items()}
        held = lax.optimization_barrier((both, alone, self.done, critical))
        both, alone, self.done, critical = held
        flight = []
        for (first, last, _, _), (own, payload) in zip(shared, both):
            back = lax.ppermute(payload, "ctx", [(0, 1), (1, 0), (2, 3), (3, 2)])
            flight.append(("first", first, own, back))
            flight.append(("last", last, payload, back))
        routes = {
            "first": [(0, 1), (3, 2)],
            "inner": [(1, 2), (2, 1)],
            "last": [(1, 0), (2, 3)],
        }
        for kind, pairs in routes.items():
            for (name, _), v in zip(ready[kind], alone[kind]):
                flight.append((kind, name, v, lax.ppermute(v, "ctx", pairs)))
        self.flights.append(flight)
        return critical

    def total(self, name):
        if self.plain:
            return up(self.done[name])
        v, arrived = self.done[name]
        return up(jnp.where(self.outer, arrived, v))


def lay_rows(pieces, counts, index, put):
    n = 0
    for k, parts in enumerate(counts):
        rows = sum(pieces[n + i].shape[0] for i in range(parts))
        start = (index ^ k) * rows
        for i in range(parts):
            put(pl.multiple_of(start, 16), pieces[n + i])
            start = start + pieces[n + i].shape[0]
        n += parts


def turn(v, cosine, sine):
    lane = lax.broadcasted_iota(jnp.int32, v.shape, 1)
    first = lax.rem(lane, HD) < HD // 2
    partner = jnp.where(
        first, pltpu.roll(v, 2 * HD - HD // 2, 1), pltpu.roll(v, HD // 2, 1)
    )
    return v * cosine + partner * sine


def normed_rows(parts, gain):
    x = jnp.concatenate([up(p[...]) for p in parts], 0)
    return low(x * lax.rsqrt(jnp.mean(x * x, -1, keepdims=True) + NORM_EPS) * gain)


def key_rows(hn, wkv_ref, cosine, sine):
    raw = dot_nn(hn, wkv_ref[...])
    two = 2 * HD
    keys = raw.shape[1] // 2
    turned = [turn(raw[:, d : d + two], cosine, sine) for d in range(0, keys, two)]
    return low(jnp.concatenate(turned + [raw[:, keys:]], 1))


def project_kernel(counts, blocks, experts, index_ref, *refs):
    pieces = refs[: sum(counts)]
    seq = refs[sum(counts) : sum(counts) + 2 * blocks]
    cos_ref, sin_ref = refs[sum(counts) + 2 * blocks : sum(counts) + 2 * blocks + 2]
    q_ref, kv_ref, hn_ref, wq_ref, wkv_ref, router_ref, gains_ref, small_ref = refs[
        sum(counts) + 2 * blocks + 2 :
    ]
    q_width, kv_width = wq_ref.shape[1], wkv_ref.shape[1]

    def put(start, ref):
        at = pl.ds(start, ref.shape[0])
        wq_ref[at, :] = ref[:, :q_width]
        wkv_ref[at, :] = ref[:, q_width : q_width + kv_width]
        small_ref[at, :] = ref[:, q_width + kv_width :]

    lay_rows(pieces, counts, index_ref[0], put)
    small = up(small_ref[...])
    lane = lax.broadcasted_iota(jnp.int32, small.shape, 1)
    router_ref[...] = low(jnp.where(lane < experts, small, 0.0))
    gains_ref[...] = jnp.transpose(small)[experts : experts + 8]
    gain = gains_ref[0:1, :]
    rows = 2 * seq[0].shape[0]
    for r in range(blocks):
        at = slice(r * rows, (r + 1) * rows)
        hn = normed_rows(seq[2 * r : 2 * r + 2], gain)
        hn_ref[at, :] = hn
        kv_ref[at, :] = key_rows(hn, wkv_ref, cos_ref[at, :], sin_ref[at, :])
    two = 2 * HD
    for c in range(0, q_width, 2 * two):
        raw = dot_nn(hn_ref[:rows, :], wq_ref[:, c : c + 2 * two])
        for d in (0, two):
            rot = turn(raw[:, d : d + two], cos_ref[:rows, :], sin_ref[:rows, :])
            q_ref[:, c + d : c + d + two] = low(up(low(rot)) * (HD ** (-0.5)))


def project(index, pieces, seq, cosine, sine, experts, q_width):
    counts = [len(p) for p in pieces]
    flat = [h for p in pieces for h in p]
    halves_in = [h for pair in seq[:-1] for h in pair]
    rows, width = 2 * seq[0][0].shape[0], seq[0][0].shape[1]
    kv_width = flat[0].shape[1] - q_width - 128
    keys = rows * len(seq)
    return pl.pallas_call(
        functools.partial(project_kernel, counts, len(seq) - 1, experts),
        in_specs=[pl.BlockSpec(memory_space=pltpu.SMEM)] + [WHOLE] * (len(flat) + len(halves_in) + 2),
        out_specs=[WHOLE] * 7,
        out_shape=[
            jax.ShapeDtypeStruct((rows, q_width), BF16),
            jax.ShapeDtypeStruct((keys, kv_width), BF16),
            jax.ShapeDtypeStruct((keys, width), BF16),
            jax.ShapeDtypeStruct((width, q_width), BF16),
            jax.ShapeDtypeStruct((width, kv_width), BF16),
            jax.ShapeDtypeStruct((width, 128), BF16),
            jax.ShapeDtypeStruct((8, width), F32),
        ],
        scratch_shapes=[pltpu.VMEM((width, 128), BF16)],
        compiler_params=params(40),
        cost_estimate=cost(8 * width * (rows * q_width + keys * kv_width)),
        name="project",
    )(index, *flat, *halves_in, cosine, sine)


def project_last_kernel(
    a_ref, b_ref, gains_ref, wkv_ref, cos_ref, sin_ref, kv_in, hn_in, kv_out, hn_out, kv_ref, hn_ref, sems
):
    rows = kv_ref.shape[0]
    start = kv_out.shape[0] - rows
    hn = normed_rows((a_ref, b_ref), gains_ref[0:1, :])
    hn_ref[...] = hn
    hn_copy = pltpu.make_async_copy(hn_ref, hn_out.at[start : start + rows], sems.at[0])
    hn_copy.start()
    at = slice(start, start + rows)
    kv_ref[...] = key_rows(hn, wkv_ref, cos_ref[at, :], sin_ref[at, :])
    kv_copy = pltpu.make_async_copy(kv_ref, kv_out.at[start : start + rows], sems.at[1])
    kv_copy.start()
    hn_copy.wait()
    kv_copy.wait()


def project_last(last, gains, wkv, cosine, sine, keyval, hn):
    rows = 2 * last[0].shape[0]
    anywhere = pl.BlockSpec(memory_space=pl.ANY)
    return pl.pallas_call(
        project_last_kernel,
        in_specs=[WHOLE] * 6 + [anywhere] * 2,
        out_specs=[anywhere] * 2,
        out_shape=[
            jax.ShapeDtypeStruct(keyval.shape, BF16),
            jax.ShapeDtypeStruct(hn.shape, BF16),
        ],
        scratch_shapes=[
            pltpu.VMEM((rows, keyval.shape[1]), BF16),
            pltpu.VMEM((rows, hn.shape[1]), BF16),
            pltpu.SemaphoreType.DMA((2,)),
        ],
        input_output_aliases={6: 0, 7: 1},
        compiler_params=params(24),
        cost_estimate=cost(8 * rows * keyval.shape[1] * hn.shape[1]),
        name="project_last",
    )(*last, gains, wkv, cosine, sine, *hbm(keyval, hn))


def router_back_kernel(
    experts,
    total_ref,
    gates_ref,
    router_ref,
    gains_ref,
    resid_ref,
    cot_ref,
    wo_ref,
    hn_ref,
    attn_ref,
    grad_ref,
    heads_ref,
    part_ref,
    held_ref,
    sems,
):
    width = resid_ref.shape[1]
    total = up(total_ref[...])
    side = total[:, width:]
    lane = lax.broadcasted_iota(jnp.int32, side.shape, 1)
    gate_grads = jnp.where(lane < experts, side + pltpu.roll(side, SIDE // 2, 1), 0.0)
    gates = gates_ref[...]
    mean = jnp.sum(gates * gate_grads, -1, keepdims=True)
    grad_logits = low(gates * (gate_grads - mean))
    grad_hn = total[:, :width] + dot_nt(grad_logits, router_ref[...])
    resid = resid_ref[...]
    inv = lax.rsqrt(jnp.mean(resid * resid, -1, keepdims=True) + NORM_EPS)
    normed = resid * inv
    gain = jnp.sum(grad_hn * normed, 0, keepdims=True)
    scaled = grad_hn * gains_ref[1:2, :]
    grad = up(cot_ref[...]) + inv * (scaled - normed * jnp.mean(scaled * normed, -1, keepdims=True))
    grad_ref[...] = grad
    grad_low = low(grad)
    heads_ref[...] = dot_nt(grad_low, wo_ref[...])
    copies = []

    def put(cols, value):
        held_ref[:, cols] = low(value)
        copies.append(
            pltpu.make_async_copy(held_ref.at[:, cols], part_ref.at[:, cols], sems.at[len(copies)])
        )
        copies[-1].start()

    small = dot_tn(hn_ref[:, :width], grad_logits)
    lane = lax.broadcasted_iota(jnp.int32, small.shape, 1)
    gain = jnp.transpose(jnp.broadcast_to(gain, (SIDE, width)))
    put(slice(width, width + SIDE), jnp.where(lane == experts, gain, small))
    attn_t = low(transposed(attn_ref[...]))
    for c in range(0, width, 256):
        put(slice(c, c + 256), dot_nn(attn_t, grad_low[:, c : c + 256]))
    for copy in copies:
        copy.wait()


def router_back(total, gates, router, gains, resid, cot, wo, hn, attn, experts):
    rows, width = resid.shape
    heads = wo.shape[0]
    return pl.pallas_call(
        functools.partial(router_back_kernel, experts),
        in_specs=[WHOLE] * 9,
        out_specs=[WHOLE, WHOLE, pl.BlockSpec(memory_space=pl.ANY)],
        out_shape=[
            pltpu.HBM((rows, width), F32),
            pltpu.HBM((rows, heads), F32),
            pltpu.HBM((heads, width + SIDE), BF16),
        ],
        scratch_shapes=[
            pltpu.VMEM((heads, width + SIDE), BF16),
            pltpu.SemaphoreType.DMA((width // 256 + 1,)),
        ],
        compiler_params=params(36),
        cost_estimate=cost(14 * rows * heads * width),
        name="router_back",
    )(*hbm(total, gates, router), gains, *hbm(resid, cot, wo, hn, attn))


def transposed(v):
    return jnp.transpose(up(v))


def key_bias(place_ref, keys, rows):
    j = lax.broadcasted_iota(jnp.int32, (keys, rows), 0)
    i = lax.broadcasted_iota(jnp.int32, (keys, rows), 1)
    block = lax.div(j, rows)
    place = (place_ref[0] - block) * rows + (j - block * rows)
    allowed = (place >= 0) & (place <= place_ref[0] * rows + i) & (place < place_ref[1])
    return jnp.where(allowed, 0.0, MASK_FLOOR)


def widened(part, group):
    zero = jnp.zeros_like(part)
    return jnp.concatenate([part, zero] if group == 0 else [zero, part], 0)


def attend_kernel(
    groups,
    place_ref,
    q_ref,
    k_ref,
    v_ref,
    tok_ref,
    gains_ref,
    router_ref,
    named_ref,
    wo_all_ref,
    out_ref,
    max_ref,
    total_ref,
    resid_ref,
    hn_ref,
    low_ref,
    gates_ref,
    bias_ref,
    wo_ref,
    sem,
):
    rows = q_ref.shape[0]
    keys = k_ref.shape[0]
    width = tok_ref.shape[1]
    step = pl.program_id(0)
    load = pltpu.make_async_copy(wo_all_ref, wo_ref, sem)

    @pl.when(step == 0)
    def _():
        load.start()
        bias_ref[...] = key_bias(place_ref, keys, rows)

    q_t = low(transposed(q_ref[...]))
    v_t = low(transposed(v_ref[...]))
    outs, maxes, totals = [], [], []
    for group in range(2):
        parts = [
            widened(q_t[(group * groups + h) * HD : (group * groups + h + 1) * HD], group)
            for h in range(groups)
        ]
        scores = dot_nn(k_ref[...], jnp.concatenate(parts, 1))
        weights = []
        for h in range(groups):
            s = scores[:, h * rows : (h + 1) * rows] + bias_ref[...]
            top = jnp.max(s, 0, keepdims=True)
            w = jnp.exp(s - top)
            totals.append(jnp.sum(w, 0, keepdims=True))
            maxes.append(top)
            weights.append(low(w))
        mixed = dot_nn(v_t, jnp.concatenate(weights, 1))
        for h in range(groups):
            part = mixed[group * HD : (group + 1) * HD, h * rows : (h + 1) * rows]
            outs.append(part / totals[group * groups + h])
    attn = jnp.transpose(jnp.concatenate(outs, 0))
    out_ref[...] = attn
    heads = 2 * groups * HD
    low_ref[:, pl.ds(pl.multiple_of(step * heads, 2 * HD), heads)] = low(attn)
    pad = [jnp.ones((8 - 2 * groups, rows), F32)] if 2 * groups < 8 else []
    max_ref[0] = jnp.concatenate(maxes + pad, 0)
    total_ref[0] = jnp.concatenate(totals + pad, 0)

    @pl.when(step == pl.num_programs(0) - 1)
    def _():
        load.wait()
        resid = up(tok_ref[...]) + dot_nn(low_ref[...], wo_ref[...])
        resid_ref[...] = resid
        inv = lax.rsqrt(jnp.mean(resid * resid, -1, keepdims=True) + NORM_EPS)
        hn = low(resid * inv * gains_ref[1:2, :])
        hn_ref[:, :width] = hn
        named = up(named_ref[...]) > 0.5
        logits = jnp.where(named, dot_nn(hn, router_ref[...]), MASK_FLOOR)
        gates = jnp.where(named, jnp.exp(logits - jnp.max(logits, -1, keepdims=True)), 0.0)
        gates = gates / jnp.sum(gates, -1, keepdims=True)
        gates_ref[...] = gates
        high = up(low(gates))
        hn_ref[:, width:] = low(high + pltpu.roll(gates - high, SIDE // 2, 1))


def attend(place, queries, keyval, tokens, gains, router, named, wo, groups):
    rows, heads_all = queries.shape
    width = tokens.shape[1]
    keys, kv = keyval.shape
    steps = kv // 2 // (2 * HD)
    heads = 2 * groups * HD

    def same(*shape):
        return pl.BlockSpec(shape, lambda i, s: (0,) * len(shape))

    return pl.pallas_call(
        functools.partial(attend_kernel, groups),
        grid_spec=pltpu.PrefetchScalarGridSpec(
            num_scalar_prefetch=1,
            grid=(steps,),
            in_specs=[
                pl.BlockSpec((rows, heads), lambda i, s: (0, i)),
                pl.BlockSpec((keys, 2 * HD), lambda i, s: (0, i)),
                pl.BlockSpec((keys, 2 * HD), lambda i, s: (0, steps + i)),
                same(rows, width),
                same(8, width),
                same(width, SIDE),
                same(rows, SIDE),
                pl.BlockSpec(memory_space=pl.ANY),
            ],
            out_specs=[
                pl.BlockSpec((rows, heads), lambda i, s: (0, i)),
                pl.BlockSpec((1, 8, rows), lambda i, s: (i, 0, 0)),
                pl.BlockSpec((1, 8, rows), lambda i, s: (i, 0, 0)),
                same(rows, width),
                same(rows, width + SIDE),
                same(rows, heads_all),
                same(rows, SIDE),
            ],
            scratch_shapes=[
                pltpu.VMEM((keys, rows), F32),
                pltpu.VMEM((heads_all, width), BF16),
                pltpu.SemaphoreType.DMA,
            ],
        ),
        out_shape=[
            pltpu.HBM((rows, heads_all), F32),
            jax.ShapeDtypeStruct((steps, 8, rows), F32),
            jax.ShapeDtypeStruct((steps, 8, rows), F32),
            pltpu.HBM((rows, width), F32),
            jax.ShapeDtypeStruct((rows, width + SIDE), BF16),
            pltpu.HBM((rows, heads_all), BF16),
            jax.ShapeDtypeStruct((rows, SIDE), F32),
        ],
        compiler_params=params(40),
        cost_estimate=cost(50 * rows * keys * heads_all),
        name="attend",
    )(place, *hbm(queries, keyval, keyval, tokens), gains, router, named, *hbm(wo))


def attend_back_kernel(
    groups,
    place_ref,
    q_ref,
    k_ref,
    v_ref,
    grad_ref,
    out_ref,
    max_ref,
    total_ref,
    cos_ref,
    sin_ref,
    hn_ref,
    gq_ref,
    gk_ref,
    gv_ref,
    part_ref,
    bias_ref,
    held_ref,
    hn_t_ref,
    sems,
):
    rows = q_ref.shape[0]
    keys = k_ref.shape[0]
    chunk = 256

    @pl.when(pl.program_id(0) == 0)
    def _():
        bias_ref[...] = key_bias(place_ref, keys, rows)
        for start in range(0, keys, rows):
            hn_t_ref[:, start : start + rows] = low(transposed(hn_ref[start : start + rows, :]))

    q_t = low(transposed(q_ref[...]))
    k_t = low(transposed(k_ref[...]))
    grad_t = transposed(grad_ref[...])
    out_t = transposed(out_ref[...])
    q_parts, g_parts, deltas, tops, grads = [], [], [], [], []
    for group in range(2):
        q_part, g_part, delta = [], [], []
        for h in range(groups):
            n = group * groups + h
            total = total_ref[0, n : n + 1]
            grad = grad_t[n * HD : (n + 1) * HD]
            q_part.append(widened(q_t[n * HD : (n + 1) * HD], group))
            g_part.append(widened(low(grad / total), group))
            delta.append(jnp.sum(out_t[n * HD : (n + 1) * HD] * grad, 0, keepdims=True) / total)
        q_parts.append(jnp.concatenate(q_part, 1))
        g_parts.append(jnp.concatenate(g_part, 1))
        deltas.append(jnp.concatenate(delta, 1))
        tops.append(
            jnp.concatenate(
                [max_ref[0, group * groups + h : group * groups + h + 1] for h in range(groups)], 1
            )
        )
        grads.append(jnp.zeros((2 * HD, groups * rows), F32))
    for start in range(0, keys, chunk):
        bias = bias_ref[start : start + chunk]
        bias = jnp.concatenate([bias] * groups, 1)
        grad_k = jnp.zeros((chunk, 2 * HD), F32)
        grad_v = jnp.zeros((chunk, 2 * HD), F32)
        for group in range(2):
            scores = dot_nn(k_ref[start : start + chunk], q_parts[group])
            w = jnp.exp(scores + bias - tops[group])
            gp = dot_nn(v_ref[start : start + chunk], g_parts[group])
            gs = low(w * (gp - deltas[group]))
            grad_v = grad_v + dot_nt(low(w), g_parts[group])
            grad_k = grad_k + dot_nt(gs, q_parts[group])
            grads[group] = grads[group] + dot_nn(k_t[:, start : start + chunk], gs)
        at = slice(start, start + chunk)
        gk_ref[at] = low(turn(grad_k, cos_ref[at, :], -sin_ref[at, :]))
        gv_ref[at] = low(grad_v)
    step, slot = pl.program_id(0), lax.rem(pl.program_id(0), 2)
    steps = part_ref.shape[1] // held_ref.shape[2]
    heads, two = 2 * groups * HD, 2 * HD

    def copies(n, slot):
        spans = ((0, heads), (steps * heads, two), (steps * (heads + two), two))
        out, col = [], 0
        for i, (first, size) in enumerate(spans):
            dst = pl.ds(pl.multiple_of(first + n * size, two), size)
            src = held_ref.at[slot, :, col : col + size]
            out.append(pltpu.make_async_copy(src, part_ref.at[:, dst], sems.at[slot, i]))
            col += size
        return out

    @pl.when(step >= 2)
    def _():
        for copy in copies(step - 2, slot):
            copy.wait()

    both = jnp.concatenate([gk_ref[...], gv_ref[...]], 1)
    held_ref[slot, :, heads:] = low(dot_nn(hn_t_ref[...], both))
    parts = []
    for group in range(2):
        for h in range(groups):
            parts.append(grads[group][group * HD : (group + 1) * HD, h * rows : (h + 1) * rows])
    grad_q = jnp.transpose(jnp.concatenate(parts, 0)) * (HD ** (-0.5))
    for d in range(0, 2 * groups * HD, 2 * HD):
        gq_ref[:, d : d + 2 * HD] = low(
            turn(grad_q[:, d : d + 2 * HD], cos_ref[:rows, :], -sin_ref[:rows, :])
        )
    held_ref[slot, :, :heads] = low(dot_nn(hn_t_ref[:, :rows], gq_ref[...]))
    for copy in copies(step, slot):
        copy.start()

    @pl.when(step == steps - 1)
    def _():
        for copy in copies(step, slot):
            copy.wait()

    @pl.when((step == steps - 1) & (step >= 1))
    def _():
        for copy in copies(step - 1, 1 - slot):
            copy.wait()


def attend_back(place, queries, keyval, grad_heads, attn, tops, totals, cosine, sine, hn, groups):
    rows, width = queries.shape
    keys, kv = keyval.shape
    steps = kv // 2 // (2 * HD)
    heads = 2 * groups * HD
    model = hn.shape[1]
    head_spec = pl.BlockSpec((rows, heads), lambda i, s: (0, i))
    key_spec = pl.BlockSpec((keys, 2 * HD), lambda i, s: (0, i))
    stat_spec = pl.BlockSpec((1, 8, rows), lambda i, s: (i, 0, 0))
    return pl.pallas_call(
        functools.partial(attend_back_kernel, groups),
        grid_spec=pltpu.PrefetchScalarGridSpec(
            num_scalar_prefetch=1,
            grid=(steps,),
            in_specs=[
                head_spec,
                key_spec,
                pl.BlockSpec((keys, 2 * HD), lambda i, s: (0, steps + i)),
                head_spec,
                head_spec,
                stat_spec,
                stat_spec,
                pl.BlockSpec((keys, 2 * HD), lambda i, s: (0, 0)),
                pl.BlockSpec((keys, 2 * HD), lambda i, s: (0, 0)),
                pl.BlockSpec((keys, model), lambda i, s: (0, 0)),
            ],
            out_specs=[
                head_spec,
                key_spec,
                key_spec,
                pl.BlockSpec(memory_space=pl.ANY),
            ],
            scratch_shapes=[
                pltpu.VMEM((keys, rows), F32),
                pltpu.VMEM((2, model, heads + 4 * HD), BF16),
                pltpu.VMEM((model, keys), BF16),
                pltpu.SemaphoreType.DMA((2, 3)),
            ],
        ),
        out_shape=[
            jax.ShapeDtypeStruct((rows, width), BF16),
            jax.ShapeDtypeStruct((keys, kv // 2), BF16),
            jax.ShapeDtypeStruct((keys, kv // 2), BF16),
            pltpu.HBM((model, width + kv), BF16),
        ],
        compiler_params=params(44),
        cost_estimate=cost(64 * rows * keys * width),
        name="attend_back",
    )(place, *hbm(queries, keyval, keyval, grad_heads, attn, tops, totals, cosine, sine, hn))


def slot_pick(slot, cap):
    place = lax.broadcasted_iota(jnp.int32, (cap, slot.shape[1]), 0).astype(F32)
    return place == slot


def weight_chunks(grads, x_ref, c_ref, ggu_ref, act_ref):
    hidden, width = act_ref.shape[1], c_ref.shape[1]
    size, wide = grads[0].shape
    rest = width - wide
    half = hidden // 2
    for h in range(2):
        at = slice(h * half, (h + 1) * half)
        part = low(dot_tn(act_ref[:, at], c_ref[...]))
        grads[0][at, :] = part[:, :wide]
        grads[0][hidden:, h * rest : (h + 1) * rest] = part[:, wide:]
    step = size // 2
    for c, ref in enumerate(grads[1:]):
        for h in range(2):
            cols = slice(c * size + h * step, c * size + (h + 1) * step)
            ref[h * step : (h + 1) * step, :] = low(dot_tn(x_ref[:, cols], ggu_ref[...]))


def expert_kernel(counts, cap, tile, e, earlier, last, number_ref, *refs):
    parts, refs = refs[: sum(counts)], refs[sum(counts) :]
    cot_ref, wgu_all_ref, wd_all_ref = refs[:3]
    gin_before, refs = refs[3 : 3 + earlier], refs[3 + earlier :]
    out_ref, slots_ref, result_ref = refs[:3]
    grads = refs[3:6]
    x_ref, c_ref, ggu_ref, act_ref, sg_ref, wgu_ref, wd_ref, sems = refs[6:14]
    if last:
        gin_ref, load_ref, store_ref = refs[14:]
    else:
        gin_ref = result_ref
    loads = [
        pltpu.make_async_copy(wgu_all_ref.at[e], wgu_ref, sems.at[0]),
        pltpu.make_async_copy(wd_all_ref.at[e], wd_ref, sems.at[1]),
    ]
    for load in loads:
        load.start()
    blocks = len(counts)
    hidden, width = wd_ref.shape
    rows = cot_ref.shape[0] // blocks
    total = blocks * cap
    index, expert = number_ref[0], number_ref[1]
    lane = lax.broadcasted_iota(jnp.int32, (8, SIDE), 1)
    pick_slot = low(jnp.where(lane == expert, 1.0, 0.0))
    pick_gate = low(jnp.where((lane == expert) | (lane == expert + SIDE // 2), 1.0, 0.0))
    n = 0
    for b in range(blocks):
        hn = parts[n : n + counts[b]]
        n += counts[b]
        src = pl.ds(pl.multiple_of((index ^ b) * rows, rows), rows)
        slot = dot_nt(pick_slot, cot_ref[src, width:])[:1] - 1.0
        gate = [dot_nt(pick_gate, part[:, width:]) for part in hn]
        gate = (jnp.concatenate(gate, 1) if len(gate) > 1 else gate[0])[:1]
        slots_ref[b : b + 1, :] = slot
        hit = slot_pick(slot, cap)
        pick = low(jnp.where(hit, 1.0, 0.0))
        at = slice(b * cap, (b + 1) * cap)
        taken, start = None, 0
        for part in hn:
            piece = dot_nn(pick[:, start : start + part.shape[0]], part[:, :width])
            taken = piece if taken is None else taken + piece
            start += part.shape[0]
        x_ref[at, :] = low(taken)
        c_ref[at, :] = low(dot_nn(pick, cot_ref[src, :width]))
        gate = jnp.sum(jnp.where(hit, gate, 0.0), 1, keepdims=True)
        sg_ref[at, :] = jnp.broadcast_to(gate, (cap, 128))

    def middle(t, carry):
        at = pl.ds(pl.multiple_of(t * tile, 16), tile)
        gate_up = dot_nn(x_ref[at, :], wgu_ref[...])
        g = gate_up[:, :hidden]
        u = gate_up[:, hidden:]
        sigma = jax.nn.sigmoid(g)
        silu = g * sigma
        act = low(silu * u)
        slot_gate = sg_ref[at, :][:, :1]
        back = dot_nt(c_ref[at, :], wd_ref[...])
        gate_grad = jnp.sum(up(act) * back, 1, keepdims=True)
        back = back * slot_gate
        act_ref[at, :] = low(up(act) * slot_gate)
        ggu_ref[at, :hidden] = low(back * u * (sigma * (1.0 + g * (1.0 - sigma))))
        ggu_ref[at, hidden:] = low(back * silu)
        out_ref[at, :] = low(dot_nn(act, wd_ref[...]) * slot_gate)
        gin_ref[at, :width] = low(dot_nt(ggu_ref[at, :], wgu_ref[...]))
        lane = lax.broadcasted_iota(jnp.int32, (tile, SIDE), 1)
        high = up(low(gate_grad))
        side = jnp.where(lane == expert, high, 0.0)
        side = jnp.where(lane == expert + SIDE // 2, gate_grad - high, side)
        gin_ref[at, width:] = low(side)
        return carry

    for load in loads:
        load.wait()
    lax.fori_loop(0, total // tile, middle, 0)
    if not last:
        weight_chunks(grads, x_ref, c_ref, ggu_ref, act_ref)
        return

    def load_before(b):
        return [
            pltpu.make_async_copy(
                ref.at[b * cap : (b + 1) * cap], load_ref.at[b % 2, i], sems.at[2 + 2 * i + b % 2]
            )
            for i, ref in enumerate(gin_before)
        ]

    def store(b):
        dst = pl.ds(pl.multiple_of((index ^ b) * rows, rows), rows)
        return pltpu.make_async_copy(
            store_ref.at[b % 2], result_ref.at[dst], sems.at[2 + 2 * earlier + b % 2]
        )

    for load in load_before(0):
        load.start()
    for b in range(blocks):
        if b + 1 < blocks:
            for load in load_before(b + 1):
                load.start()
        src = pl.ds(pl.multiple_of((index ^ b) * rows, rows), rows)
        order = up(cot_ref[src, width:])
        lane = lax.broadcasted_iota(jnp.int32, order.shape, 1)
        place = lax.broadcasted_iota(jnp.int32, (rows, cap), 1).astype(F32)

        def pick(number):
            slot = jnp.sum(jnp.where(lane == number, order, 0.0), 1, keepdims=True) - 1.0
            return low(jnp.where(place == slot, 1.0, 0.0))

        acc = dot_nn(pick(expert), gin_ref[b * cap : (b + 1) * cap, :])
        for i, load in enumerate(load_before(b)):
            load.wait()
            acc = acc + dot_nn(pick(expert - earlier + i), load_ref[b % 2, i])
        if b >= 2:
            store(b - 2).wait()
        store_ref[b % 2] = low(acc)
        store(b).start()
    weight_chunks(grads, x_ref, c_ref, ggu_ref, act_ref)
    for b in range(max(blocks - 2, 0), blocks):
        store(b).wait()


def unpack_down(chunk, hidden):
    rest = chunk.shape[1] // 2
    right = jnp.concatenate([chunk[hidden:, :rest], chunk[hidden:, rest:]], 0)
    return jnp.concatenate([chunk[:hidden], right], 1)


def run_expert(number, pieces, cot, w_gate_up, w_down, e, cap, gins):
    counts = [len(p) for p in pieces]
    flat = [h for p in pieces for h in p]
    blocks = len(counts)
    rows = cot.shape[0] // blocks
    hidden, width = w_down.shape[1:]
    total = blocks * cap
    tile = max(t for t in range(16, 401, 16) if total % t == 0)
    last = e + 1 == w_down.shape[0]
    earlier = len(gins) if last else 0
    anywhere = pl.BlockSpec(memory_space=pl.ANY)
    chunk = jax.ShapeDtypeStruct((width // 2, 2 * hidden), BF16)
    work = [(total, width), (total, width), (total, 2 * hidden), (total, hidden)]
    gin_shape = (total, width + SIDE)
    scratch = [pltpu.VMEM(shape, BF16) for shape in work] + [
        pltpu.VMEM((total, 128), F32),
        pltpu.VMEM((width, 2 * hidden), BF16),
        pltpu.VMEM((hidden, width), BF16),
        pltpu.SemaphoreType.DMA((4 + 2 * earlier,)),
    ]
    if last:
        scratch += [
            pltpu.VMEM(gin_shape, BF16),
            pltpu.VMEM((2, max(earlier, 1), cap, width + SIDE), BF16),
            pltpu.VMEM((2, rows, width + SIDE), BF16),
        ]
    result = pltpu.HBM((blocks * rows, width + SIDE) if last else gin_shape, BF16)
    got = pl.pallas_call(
        functools.partial(expert_kernel, counts, cap, tile, e, earlier, last),
        in_specs=[pl.BlockSpec(memory_space=pltpu.SMEM)]
        + [WHOLE] * (len(flat) + 1)
        + [anywhere] * (2 + earlier),
        out_specs=[WHOLE, WHOLE, anywhere if last else WHOLE] + [WHOLE] * 3,
        out_shape=[
            pltpu.HBM((total, width), BF16),
            jax.ShapeDtypeStruct((blocks, rows), F32),
            result,
        ]
        + [chunk] * 3,
        scratch_shapes=scratch,
        compiler_params=params(56),
        cost_estimate=cost(44 * total * width * hidden),
        name="expert",
    )(number, *flat, cot, w_gate_up, w_down, *gins[:earlier])
    return got[0], got[1], got[2], got[3:]


def combine_kernel(count, cap, first, stride, number_ref, *refs):
    slots, parts, out_ref = refs[:count], refs[count : 2 * count], refs[2 * count]
    b = pl.program_id(0) * stride + first
    rows = slots[0].shape[1]
    place = lax.broadcasted_iota(jnp.int32, (cap, rows), 0).astype(F32)
    acc = None
    for e in range(count):
        pick = low(jnp.where(place == slots[e][pl.ds(b, 1), :], 1.0, 0.0))
        part = dot_tn(pick, parts[e][...])
        acc = part if acc is None else acc + part
    out_ref[...] = low(acc)


def combine(number, slots, parts, cap, chosen, order):
    blocks, rows = slots[0].shape
    count = len(parts)
    width = parts[0].shape[1]
    first, stride = chosen.start, chosen.step
    return pl.pallas_call(
        functools.partial(combine_kernel, count, cap, first, stride),
        grid_spec=pltpu.PrefetchScalarGridSpec(
            num_scalar_prefetch=1,
            grid=(len(chosen),),
            in_specs=[pl.BlockSpec((blocks, rows), lambda n, s: (0, 0))] * count
            + [pl.BlockSpec((cap, width), lambda n, s: (n * stride + first, 0))] * count,
            out_specs=pl.BlockSpec((rows, width), lambda n, s: (order(n, s[0]), 0)),
        ),
        out_shape=pltpu.HBM((len(chosen) * rows, width), BF16),
        compiler_params=params(20),
        cost_estimate=cost(10 * len(chosen) * cap * rows * width),
        name="combine",
    )(number, *slots, *parts)


def rope_tables(places):
    half = HD // 2
    frequency = ROPE_BASE ** (-jnp.arange(half, dtype=F32) * 2.0 / HD)
    angles = places.astype(F32)[:, None] * frequency[None, :]
    cosine, sine = jnp.cos(angles), jnp.sin(angles)
    return jnp.concatenate([cosine] * 4, 1), jnp.concatenate([-sine, sine] * 2, 1)


def per_device(
    tokens,
    lengths,
    routes,
    cotangent,
    gain_attn,
    gain_moe,
    w_query,
    w_keyval,
    w_output,
    w_router,
    w_gate_up,
    w_down,
):
    rows = tokens.shape[1]
    width = tokens.shape[2]
    experts = w_router.shape[1]
    local_experts = w_gate_up.shape[0]
    kv_width = w_keyval.shape[1] // 2
    head_total = w_query.shape[1]
    groups = head_total // kv_width
    dp_count = lax.axis_size("dp")
    ctx_count = lax.axis_size("ctx")
    dp_index = lax.axis_index("dp").astype(jnp.int32)
    ctx_index = lax.axis_index("ctx").astype(jnp.int32)
    cap = -(-(rows * 9 // 16) // 16) * 16
    length = lengths[0]
    places = ctx_index * rows + jnp.arange(rows, dtype=jnp.int32)
    valid = (places < length)[:, None]
    index = jnp.reshape(dp_index, (1,))

    pad = jnp.zeros((w_router.shape[0], 128 - experts - 2), BF16)
    first_w = Gather(
        jnp.concatenate(
            [w_query, w_keyval, w_router, gain_attn[:, None], gain_moe[:, None], pad], 1
        )
    )

    named = jnp.any(routes[0][..., None] == jnp.arange(SIDE, dtype=jnp.int32), 1).astype(BF16)
    order = dot_nn(jnp.tril(jnp.ones((rows, rows), BF16)), named) * up(named)
    grad_y = jnp.where(valid, cotangent[0], BF16(0))
    cot = jnp.concatenate([grad_y, low(order)], 1)

    seq = [halves(tokens[0])]
    back = jnp.arange(ctx_count, dtype=jnp.int32)[:, None] * rows
    tables = rope_tables((places[None, :] - back).reshape(-1))

    def next_block(part):
        return shift(seq[-1][part], 1)

    first_w.near()
    seq.append([next_block(0), next_block(1)])
    early = next_block(0)
    output_w = lax.all_gather(w_output, "dp", axis=0, tiled=True)
    _, tables, cot, seq[1], early = sync(first_w, tables, cot, seq[1], early)
    cot_all = lax.all_gather(cot, "dp", axis=0, tiled=True)
    first_w.far()
    seq.append([early, next_block(1)])
    early = next_block(0)
    _, seq[2], early = sync(first_w, seq[2], early)
    seq.append([early, next_block(1)])
    for _ in range(ctx_count - 4):
        seq.append([next_block(0), next_block(1)])
    cosine, sine = tables
    projected = project(index, first_w.pieces(), seq, cosine, sine, experts, head_total)
    queries, keyval, hn_seq, query_w, keyval_w, router_w, gains = projected
    keyval, hn_seq = project_last(seq[-1], gains, keyval_w, cosine, sine, keyval, hn_seq)

    place = jnp.stack([ctx_index, length])
    attn, tops, totals, resid, hn_two, attn_low, gates = attend(
        place, queries, keyval, tokens[0], gains, router_w, named, output_w, groups
    )

    hn_g = Gather(hn_two)
    hn_g.near()
    sync(hn_g)
    hn_pieces = hn_g.pieces()
    sums = LineSums()
    outs, gins, slots = [], [], []
    for e in range(local_experts):
        number = jnp.stack([dp_index, dp_index * local_experts + e])
        out, slot, gin, grads = run_expert(
            number, hn_pieces, cot_all, w_gate_up, w_down, e, cap, gins
        )
        outs.append(out)
        gins.append(gin)
        slots.append(slot)
        if e + 1 < local_experts:
            for c, v in enumerate(grads):
                sums.add(f"{e}.{c}", v)
            hn_pieces, cot_all = sums.step(hn_pieces, cot_all)
    for c, v in enumerate(grads):
        sums.add(f"{local_experts - 1}.{c}", v)
    (gin_tokens,) = sums.step(gins[-1])
    gin_sum = lax.psum_scatter(gin_tokens, "dp", scatter_dimension=0, tiled=True)
    outs, slots = sums.step(outs, slots)
    out_tokens = combine(index, slots, outs, cap, range(0, dp_count, 1), lambda n, i: n ^ i)
    gin_sum, out_tokens = sums.step(gin_sum, out_tokens)

    grad_resid, grad_heads, part_output = router_back(
        gin_sum, gates, router_w, gains, resid, grad_y, output_w, hn_two, attn_low, experts
    )

    backed = attend_back(
        place, queries, keyval, grad_heads, attn, tops, totals, cosine, sine, hn_seq, groups
    )
    backed = sums.step(*backed, part_output)
    grad_query, grad_keys, grad_values, part_first, part_output = backed
    share_first = lax.psum_scatter(part_first, "dp", scatter_dimension=0, tiled=True)
    (part_output,) = sums.step(part_output)
    share_output = lax.psum_scatter(part_output, "dp", scatter_dimension=0, tiled=True)
    share_query, share_keyval = share_first[:, :head_total], share_first[:, head_total:]
    gain_grad = jnp.sum(up(share_query) * up(w_query), 1, keepdims=True) + jnp.sum(
        up(share_keyval) * up(w_keyval), 1, keepdims=True
    )
    gain_grad = jnp.broadcast_to(gain_grad / up(gain_attn)[:, None], (w_query.shape[0], SIDE))
    share_keyval = jnp.concatenate([share_keyval, low(gain_grad)], 1)
    sums.add("query", share_query)
    sums.add("keyval", share_keyval)
    sums.step(take=2)
    sums.add("output", share_output)
    grad_kv = jnp.concatenate([grad_keys, grad_values], 1)
    blocks = [grad_kv[r * rows : (r + 1) * rows] for r in range(ctx_count)]
    held = blocks[-1]
    for r in range(ctx_count - 2, -1, -1):
        pairs = [(i, i - 1) for i in range(r + 1, ctx_count)]
        held = add_low(lax.ppermute(held, "ctx", pairs), blocks[r])
        if r:
            held, out_tokens = sums.step(held, out_tokens)
    moe = lax.psum_scatter(out_tokens, "dp", scatter_dimension=0, tiled=True)

    grad_hn_one = dot_nt(grad_query, query_w) + dot_nt(held, keyval_w)
    inputs = up(tokens[0])
    inv_one = lax.rsqrt(jnp.mean(inputs * inputs, -1, keepdims=True) + NORM_EPS)
    normed_one = inputs * inv_one
    scaled_one = grad_hn_one * gains[0:1]
    grad_inputs = grad_resid + inv_one * (
        scaled_one - normed_one * jnp.mean(scaled_one * normed_one, -1, keepdims=True)
    )
    grad_inputs = low(grad_inputs)

    outcome = low(jnp.where(valid, resid + up(moe), 0.0))

    wanted = [f"{e}.{c}" for e in range(local_experts) for c in range(3)]
    while not all(name in sums.done for name in wanted):
        sums.step(take=2)
    gate_up, down = jnp.zeros(w_gate_up.shape, F32), []
    for e in range(local_experts):
        chunks = [sums.total(f"{e}.{c}") for c in range(3)]
        for c, part in enumerate(chunks[1:]):
            gate_up = lax.dynamic_update_slice(gate_up, part[None], (e, c * part.shape[0], 0))
        down.append(unpack_down(chunks[0], w_down.shape[1]))
    down = jnp.stack(down)
    gate_up, down, grad_inputs = sums.step(gate_up, down, grad_inputs)
    if "query" not in sums.done:
        sums.step()
    total_query, total_keyval = sums.total("query"), sums.total("keyval")
    ready = (total_query, total_keyval[:, : 2 * kv_width], total_keyval[:, 2 * kv_width])
    total_query, total_keyval, total_gain = sums.step(*ready)
    while sums.busy():
        sums.step()
    total_output = sums.total("output")
    return (
        outcome[None],
        grad_inputs[None],
        total_gain,
        total_output[:, width + experts],
        total_query,
        total_keyval,
        total_output[:, :width],
        total_output[:, width : width + experts],
        gate_up,
        down,
    )


def solution(mesh):
    in_specs = (
        P("dp", "ctx", None),
        P("dp"),
        P("dp", "ctx", None),
        P("dp", "ctx", None),
        P("dp"),
        P("dp"),
        P("dp", None),
        P("dp", None),
        P("dp", None),
        P("dp", None),
        P("dp", None, None),
        P("dp", None, None),
    )
    out_specs = (
        P("dp", "ctx", None),
        P("dp", "ctx", None),
        P("dp"),
        P("dp"),
        P("dp", None),
        P("dp", None),
        P("dp", None),
        P("dp", None),
        P("dp", None, None),
        P("dp", None, None),
    )
    return jax.shard_map(
        per_device, mesh=mesh, in_specs=in_specs, out_specs=out_specs, check_vma=False
    )
```

```python
import functools

import jax
import jax.numpy as jnp
from jax import lax
from jax.experimental import pallas as pl
from jax.experimental.pallas import tpu as pltpu
from jax.sharding import PartitionSpec as P

HD = 64
NORM_EPS = 1e-06
ROPE_BASE = 10000.0
MASK_FLOOR = -1e30
F32 = jnp.float32
BF16 = jnp.bfloat16
MIB = 1024 * 1024
SIDE = 128
WHOLE = pl.BlockSpec()


def params(mib):
    return pltpu.CompilerParams(vmem_limit_bytes=mib * MIB)


def hbm(*arrays_in):
    return [pltpu.with_memory_space_constraint(v, pltpu.HBM) for v in arrays_in]


def cost(flops):
    return pl.CostEstimate(flops=int(flops) // 64, bytes_accessed=1024, transcendentals=0)


def up(v):
    return v.astype(F32)


def low(v):
    return v.astype(BF16)


def dot_nn(a, b):
    return lax.dot_general(a, b, (((1,), (0,)), ((), ())), preferred_element_type=F32)


def dot_nt(a, b):
    return lax.dot_general(a, b, (((1,), (1,)), ((), ())), preferred_element_type=F32)


def dot_tn(a, b):
    return lax.dot_general(a, b, (((0,), (0,)), ((), ())), preferred_element_type=F32)


def swap(v, mask):
    count = lax.axis_size("dp")
    return lax.ppermute(v, "dp", [(i, i ^ mask) for i in range(count)])


def halves(v):
    mid = v.shape[0] // 2
    return [v[:mid], v[mid:]]


class Gather:
    def __init__(self, v):
        self.special = lax.axis_size("dp") == 8
        self.stage = 0
        self.live = [v]

    def near(self):
        if self.special and self.stage == 0:
            v = self.live[0]
            self.live = [v, swap(v, 2), swap(v, 4)]
        self.stage = max(self.stage, 1)

    def far(self):
        self.near()
        if self.special and self.stage == 1:
            v, along_x, along_y = self.live
            self.live = self.live + [swap(halves(along_x)[0], 4), swap(halves(along_y)[1], 2)]
        self.stage = max(self.stage, 2)

    def pieces(self):
        self.far()
        if not self.special:
            out = [[self.live[0]]]
            bit = 1
            while bit < lax.axis_size("dp"):
                out = out + [[swap(h, bit) for h in piece] for piece in out]
                bit *= 2
            return out
        v, along_x, along_y, far_a, far_b = self.live
        even = [[v], [along_x], [along_y], [far_a, far_b]]
        out = []
        for piece in even:
            out += [piece, [swap(h, 1) for h in piece]]
        return out


def sync(*items):
    plain = [i.live if isinstance(i, Gather) else i for i in items]
    plain = lax.optimization_barrier(plain)
    for item, got in zip(items, plain):
        if isinstance(item, Gather):
            item.live = list(got)
    return plain


def add_low(a, b):
    return low(up(a) + up(b))


def shift(v, step):
    count = lax.axis_size("ctx")
    return lax.ppermute(
        v, "ctx", [(i, i + step) for i in range(count) if 0 <= i + step < count]
    )


class LineSums:
    DEPTH = 1

    def __init__(self):
        count = lax.axis_size("ctx")
        index = lax.axis_index("ctx")
        self.plain = count != 4
        self.outer = (index == 0) | (index == count - 1)
        self.waiting = []
        self.flights = [[] for _ in range(self.DEPTH)]
        self.done = {}

    def add(self, name, v):
        if self.plain:
            self.done[name] = lax.psum(v, "ctx")
        else:
            self.waiting.append((name, v))

    def busy(self):
        return bool(self.waiting or any(self.flights))

    def step(self, *critical, take=1, flush=False):
        if self.plain:
            return critical
        got = self.flights.pop(0)
        while flush and self.flights:
            got = got + self.flights.pop(0)
        ready = {"first": [], "inner": [], "last": []}
        for kind, name, v, arrived in got:
            if kind == "first":
                ready["inner"].append((name, add_low(v, arrived)))
            elif kind == "inner":
                ready["last"].append((name, add_low(v, arrived)))
            else:
                self.done[name] = (v, arrived)
        for _ in range(take):
            if self.waiting:
                ready["first"].append(self.waiting.pop(0))
        shared = []
        for first in list(ready["first"]):
            for last in list(ready["last"]):
                if first[1].shape == last[1].shape:
                    shared.append((first[0], last[0], first[1], jnp.where(self.outer, first[1], last[1])))
                    ready["first"] = [r for r in ready["first"] if r is not first]
                    ready["last"] = [r for r in ready["last"] if r is not last]
                    break
        both = [(own, payload) for _, _, own, payload in shared]
        alone = {kind: [v for _, v in entries] for kind, entries in ready.items()}
        held = lax.optimization_barrier((both, alone, self.done, critical))
        both, alone, self.done, critical = held
        flight = []
        for (first, last, _, _), (own, payload) in zip(shared, both):
            back = lax.ppermute(payload, "ctx", [(0, 1), (1, 0), (2, 3), (3, 2)])
            flight.append(("first", first, own, back))
            flight.append(("last", last, payload, back))
        routes = {
            "first": [(0, 1), (3, 2)],
            "inner": [(1, 2), (2, 1)],
            "last": [(1, 0), (2, 3)],
        }
        for kind, pairs in routes.items():
            for (name, _), v in zip(ready[kind], alone[kind]):
                flight.append((kind, name, v, lax.ppermute(v, "ctx", pairs)))
        self.flights.append(flight)
        return critical

    def hold(self, *critical):
        if self.plain:
            return critical
        own = [[entry[2] for entry in flight] for flight in self.flights]
        own, critical = lax.optimization_barrier((own, critical))
        for n, flight in enumerate(self.flights):
            self.flights[n] = [
                (kind, name, v, arrived)
                for (kind, name, _, arrived), v in zip(flight, own[n])
            ]
        return critical

    def total(self, name):
        if self.plain:
            return up(self.done[name])
        v, arrived = self.done[name]
        return up(jnp.where(self.outer, arrived, v))


def lay_rows(pieces, counts, index, put):
    n = 0
    for k, parts in enumerate(counts):
        rows = sum(pieces[n + i].shape[0] for i in range(parts))
        start = (index ^ k) * rows
        for i in range(parts):
            put(pl.multiple_of(start, 16), pieces[n + i])
            start = start + pieces[n + i].shape[0]
        n += parts


def turn(v, cosine, sine):
    lane = lax.broadcasted_iota(jnp.int32, v.shape, 1)
    first = lax.rem(lane, HD) < HD // 2
    partner = jnp.where(
        first, pltpu.roll(v, 2 * HD - HD // 2, 1), pltpu.roll(v, HD // 2, 1)
    )
    return v * cosine + partner * sine


def normed_rows(parts, gain):
    x = jnp.concatenate([up(p[...]) for p in parts], 0)
    return low(x * lax.rsqrt(jnp.mean(x * x, -1, keepdims=True) + NORM_EPS) * gain)


def key_rows(hn, wkv_ref, cosine, sine):
    raw = dot_nn(hn, wkv_ref[...])
    two = 2 * HD
    keys = raw.shape[1] // 2
    turned = [turn(raw[:, d : d + two], cosine, sine) for d in range(0, keys, two)]
    return low(jnp.concatenate(turned + [raw[:, keys:]], 1))


def project_kernel(counts, blocks, experts, index_ref, *refs):
    pieces = refs[: sum(counts)]
    seq = refs[sum(counts) : sum(counts) + 2 * blocks]
    cos_ref, sin_ref = refs[sum(counts) + 2 * blocks : sum(counts) + 2 * blocks + 2]
    q_ref, kv_ref, hn_ref, wq_ref, wkv_ref, router_ref, gains_ref, small_ref = refs[
        sum(counts) + 2 * blocks + 2 :
    ]
    q_width, kv_width = wq_ref.shape[1], wkv_ref.shape[1]

    def put(start, ref):
        at = pl.ds(start, ref.shape[0])
        wq_ref[at, :] = ref[:, :q_width]
        wkv_ref[at, :] = ref[:, q_width : q_width + kv_width]
        small_ref[at, :] = ref[:, q_width + kv_width :]

    lay_rows(pieces, counts, index_ref[0], put)
    small = up(small_ref[...])
    lane = lax.broadcasted_iota(jnp.int32, small.shape, 1)
    router_ref[...] = low(jnp.where(lane < experts, small, 0.0))
    gains_ref[...] = jnp.transpose(small)[experts : experts + 8]
    gain = gains_ref[0:1, :]
    rows = 2 * seq[0].shape[0]
    for r in range(blocks):
        at = slice(r * rows, (r + 1) * rows)
        hn = normed_rows(seq[2 * r : 2 * r + 2], gain)
        hn_ref[at, :] = hn
        kv_ref[at, :] = key_rows(hn, wkv_ref, cos_ref[at, :], sin_ref[at, :])
    two = 2 * HD
    for c in range(0, q_width, 2 * two):
        raw = dot_nn(hn_ref[:rows, :], wq_ref[:, c : c + 2 * two])
        for d in (0, two):
            rot = turn(raw[:, d : d + two], cos_ref[:rows, :], sin_ref[:rows, :])
            q_ref[:, c + d : c + d + two] = low(up(low(rot)) * (HD ** (-0.5)))


def project(index, pieces, seq, cosine, sine, experts, q_width):
    counts = [len(p) for p in pieces]
    flat = [h for p in pieces for h in p]
    halves_in = [h for pair in seq[:-1] for h in pair]
    rows, width = 2 * seq[0][0].shape[0], seq[0][0].shape[1]
    kv_width = flat[0].shape[1] - q_width - 128
    keys = rows * len(seq)
    return pl.pallas_call(
        functools.partial(project_kernel, counts, len(seq) - 1, experts),
        in_specs=[pl.BlockSpec(memory_space=pltpu.SMEM)] + [WHOLE] * (len(flat) + len(halves_in) + 2),
        out_specs=[WHOLE] * 7,
        out_shape=[
            jax.ShapeDtypeStruct((rows, q_width), BF16),
            jax.ShapeDtypeStruct((keys, kv_width), BF16),
            jax.ShapeDtypeStruct((keys, width), BF16),
            jax.ShapeDtypeStruct((width, q_width), BF16),
            jax.ShapeDtypeStruct((width, kv_width), BF16),
            jax.ShapeDtypeStruct((width, 128), BF16),
            jax.ShapeDtypeStruct((8, width), F32),
        ],
        scratch_shapes=[pltpu.VMEM((width, 128), BF16)],
        compiler_params=params(40),
        cost_estimate=cost(8 * width * (rows * q_width + keys * kv_width)),
        name="project",
    )(index, *flat, *halves_in, cosine, sine)


def project_last_kernel(
    a_ref, b_ref, gains_ref, wkv_ref, cos_ref, sin_ref, kv_in, hn_in, kv_out, hn_out, kv_ref, hn_ref, sems
):
    rows = kv_ref.shape[0]
    start = kv_out.shape[0] - rows
    hn = normed_rows((a_ref, b_ref), gains_ref[0:1, :])
    hn_ref[...] = hn
    hn_copy = pltpu.make_async_copy(hn_ref, hn_out.at[start : start + rows], sems.at[0])
    hn_copy.start()
    at = slice(start, start + rows)
    kv_ref[...] = key_rows(hn, wkv_ref, cos_ref[at, :], sin_ref[at, :])
    kv_copy = pltpu.make_async_copy(kv_ref, kv_out.at[start : start + rows], sems.at[1])
    kv_copy.start()
    hn_copy.wait()
    kv_copy.wait()


def project_last(last, gains, wkv, cosine, sine, keyval, hn):
    rows = 2 * last[0].shape[0]
    anywhere = pl.BlockSpec(memory_space=pl.ANY)
    return pl.pallas_call(
        project_last_kernel,
        in_specs=[WHOLE] * 6 + [anywhere] * 2,
        out_specs=[anywhere] * 2,
        out_shape=[
            jax.ShapeDtypeStruct(keyval.shape, BF16),
            jax.ShapeDtypeStruct(hn.shape, BF16),
        ],
        scratch_shapes=[
            pltpu.VMEM((rows, keyval.shape[1]), BF16),
            pltpu.VMEM((rows, hn.shape[1]), BF16),
            pltpu.SemaphoreType.DMA((2,)),
        ],
        input_output_aliases={6: 0, 7: 1},
        compiler_params=params(24),
        cost_estimate=cost(8 * rows * keyval.shape[1] * hn.shape[1]),
        name="project_last",
    )(*last, gains, wkv, cosine, sine, *hbm(keyval, hn))


def router_back_kernel(
    experts,
    total_ref,
    gates_ref,
    router_ref,
    gains_ref,
    resid_ref,
    cot_ref,
    wo_ref,
    grad_ref,
    heads_ref,
    attn_ref,
    logits_ref,
    gain_ref,
):
    width = resid_ref.shape[1]
    total = up(total_ref[...])
    side = total[:, width:]
    lane = lax.broadcasted_iota(jnp.int32, side.shape, 1)
    gate_grads = jnp.where(lane < experts, side + pltpu.roll(side, SIDE // 2, 1), 0.0)
    gates = gates_ref[...]
    mean = jnp.sum(gates * gate_grads, -1, keepdims=True)
    grad_logits = low(gates * (gate_grads - mean))
    grad_hn = total[:, :width] + dot_nt(grad_logits, router_ref[...])
    resid = resid_ref[...]
    inv = lax.rsqrt(jnp.mean(resid * resid, -1, keepdims=True) + NORM_EPS)
    normed = resid * inv
    gain = jnp.sum(grad_hn * normed, 0, keepdims=True)
    scaled = grad_hn * gains_ref[1:2, :]
    grad = up(cot_ref[...]) + inv * (scaled - normed * jnp.mean(scaled * normed, -1, keepdims=True))
    grad_ref[...] = grad
    grad_low = low(grad)
    heads_ref[...] = dot_nt(grad_low, wo_ref[...])
    attn_ref[...] = grad_low
    logits_ref[...] = grad_logits
    gain_ref[...] = jnp.broadcast_to(gain, gain_ref.shape)


def output_grad_kernel(
    experts, attn_ref, grad_ref, hn_ref, logits_ref, gain_ref, part_ref, held_ref, sems
):
    width = grad_ref.shape[1]
    copies = []

    def put(cols, value):
        held_ref[:, cols] = low(value)
        copies.append(
            pltpu.make_async_copy(held_ref.at[:, cols], part_ref.at[:, cols], sems.at[len(copies)])
        )
        copies[-1].start()

    small = dot_tn(hn_ref[:, :width], logits_ref[...])
    lane = lax.broadcasted_iota(jnp.int32, small.shape, 1)
    gain = jnp.transpose(jnp.broadcast_to(gain_ref[:1, :], (SIDE, width)))
    put(slice(width, width + SIDE), jnp.where(lane == experts, gain, small))
    attn_t = low(transposed(attn_ref[...]))
    for c in range(0, width, 256):
        put(slice(c, c + 256), dot_nn(attn_t, grad_ref[:, c : c + 256]))
    for copy in copies:
        copy.wait()


def output_grad(attn, grad, hn, logits, gain, experts):
    heads, width = attn.shape[1], grad.shape[1]
    return pl.pallas_call(
        functools.partial(output_grad_kernel, experts),
        in_specs=[WHOLE] * 5,
        out_specs=pl.BlockSpec(memory_space=pl.ANY),
        out_shape=pltpu.HBM((heads, width + SIDE), BF16),
        scratch_shapes=[
            pltpu.VMEM((heads, width + SIDE), BF16),
            pltpu.SemaphoreType.DMA((width // 256 + 1,)),
        ],
        compiler_params=params(28),
        cost_estimate=cost(4 * attn.shape[0] * heads * width),
        name="output_grad",
    )(*hbm(attn, grad, hn, logits, gain))


def router_back(total, gates, router, gains, resid, cot, wo, experts):
    rows, width = resid.shape
    heads = wo.shape[0]
    return pl.pallas_call(
        functools.partial(router_back_kernel, experts),
        in_specs=[WHOLE] * 7,
        out_specs=[WHOLE] * 5,
        out_shape=[
            pltpu.HBM((rows, width), F32),
            pltpu.HBM((rows, heads), F32),
            pltpu.HBM((rows, width), BF16),
            pltpu.HBM((rows, SIDE), BF16),
            pltpu.HBM((8, width), F32),
        ],
        compiler_params=params(30),
        cost_estimate=cost(14 * rows * heads * width),
        name="router_back",
    )(*hbm(total, gates, router), gains, *hbm(resid, cot, wo))


def transposed(v):
    return jnp.transpose(up(v))


def key_bias(place_ref, keys, rows):
    j = lax.broadcasted_iota(jnp.int32, (keys, rows), 0)
    i = lax.broadcasted_iota(jnp.int32, (keys, rows), 1)
    block = lax.div(j, rows)
    place = (place_ref[0] - block) * rows + (j - block * rows)
    allowed = (place >= 0) & (place <= place_ref[0] * rows + i) & (place < place_ref[1])
    return jnp.where(allowed, 0.0, MASK_FLOOR)


def widened(part, group):
    zero = jnp.zeros_like(part)
    return jnp.concatenate([part, zero] if group == 0 else [zero, part], 0)


def attend_kernel(
    groups,
    place_ref,
    q_ref,
    k_ref,
    v_ref,
    tok_ref,
    gains_ref,
    router_ref,
    named_ref,
    wo_all_ref,
    out_ref,
    max_ref,
    total_ref,
    resid_ref,
    hn_ref,
    low_ref,
    gates_ref,
    bias_ref,
    wo_ref,
    sem,
):
    rows = q_ref.shape[0]
    keys = k_ref.shape[0]
    width = tok_ref.shape[1]
    step = pl.program_id(0)
    load = pltpu.make_async_copy(wo_all_ref, wo_ref, sem)

    @pl.when(step == 0)
    def _():
        load.start()
        bias_ref[...] = key_bias(place_ref, keys, rows)

    q_t = low(transposed(q_ref[...]))
    v_t = low(transposed(v_ref[...]))
    outs, maxes, totals = [], [], []
    for group in range(2):
        parts = [
            widened(q_t[(group * groups + h) * HD : (group * groups + h + 1) * HD], group)
            for h in range(groups)
        ]
        scores = dot_nn(k_ref[...], jnp.concatenate(parts, 1))
        weights = []
        for h in range(groups):
            s = scores[:, h * rows : (h + 1) * rows] + bias_ref[...]
            top = jnp.max(s, 0, keepdims=True)
            w = jnp.exp(s - top)
            totals.append(jnp.sum(w, 0, keepdims=True))
            maxes.append(top)
            weights.append(low(w))
        mixed = dot_nn(v_t, jnp.concatenate(weights, 1))
        for h in range(groups):
            part = mixed[group * HD : (group + 1) * HD, h * rows : (h + 1) * rows]
            outs.append(part / totals[group * groups + h])
    attn = jnp.transpose(jnp.concatenate(outs, 0))
    out_ref[...] = attn
    heads = 2 * groups * HD
    low_ref[:, pl.ds(pl.multiple_of(step * heads, 2 * HD), heads)] = low(attn)
    pad = [jnp.ones((8 - 2 * groups, rows), F32)] if 2 * groups < 8 else []
    max_ref[0] = jnp.concatenate(maxes + pad, 0)
    total_ref[0] = jnp.concatenate(totals + pad, 0)

    @pl.when(step == pl.num_programs(0) - 1)
    def _():
        load.wait()
        resid = up(tok_ref[...]) + dot_nn(low_ref[...], wo_ref[...])
        resid_ref[...] = resid
        inv = lax.rsqrt(jnp.mean(resid * resid, -1, keepdims=True) + NORM_EPS)
        hn = low(resid * inv * gains_ref[1:2, :])
        hn_ref[:, :width] = hn
        named = up(named_ref[...]) > 0.5
        logits = jnp.where(named, dot_nn(hn, router_ref[...]), MASK_FLOOR)
        gates = jnp.where(named, jnp.exp(logits - jnp.max(logits, -1, keepdims=True)), 0.0)
        gates = gates / jnp.sum(gates, -1, keepdims=True)
        gates_ref[...] = gates
        high = up(low(gates))
        hn_ref[:, width:] = low(high + pltpu.roll(gates - high, SIDE // 2, 1))


def attend(place, queries, keyval, tokens, gains, router, named, wo, groups):
    rows, heads_all = queries.shape
    width = tokens.shape[1]
    keys, kv = keyval.shape
    steps = kv // 2 // (2 * HD)
    heads = 2 * groups * HD

    def same(*shape):
        return pl.BlockSpec(shape, lambda i, s: (0,) * len(shape))

    return pl.pallas_call(
        functools.partial(attend_kernel, groups),
        grid_spec=pltpu.PrefetchScalarGridSpec(
            num_scalar_prefetch=1,
            grid=(steps,),
            in_specs=[
                pl.BlockSpec((rows, heads), lambda i, s: (0, i)),
                pl.BlockSpec((keys, 2 * HD), lambda i, s: (0, i)),
                pl.BlockSpec((keys, 2 * HD), lambda i, s: (0, steps + i)),
                same(rows, width),
                same(8, width),
                same(width, SIDE),
                same(rows, SIDE),
                pl.BlockSpec(memory_space=pl.ANY),
            ],
            out_specs=[
                pl.BlockSpec((rows, heads), lambda i, s: (0, i)),
                pl.BlockSpec((1, 8, rows), lambda i, s: (i, 0, 0)),
                pl.BlockSpec((1, 8, rows), lambda i, s: (i, 0, 0)),
                same(rows, width),
                same(rows, width + SIDE),
                same(rows, heads_all),
                same(rows, SIDE),
            ],
            scratch_shapes=[
                pltpu.VMEM((keys, rows), F32),
                pltpu.VMEM((heads_all, width), BF16),
                pltpu.SemaphoreType.DMA,
            ],
        ),
        out_shape=[
            pltpu.HBM((rows, heads_all), F32),
            jax.ShapeDtypeStruct((steps, 8, rows), F32),
            jax.ShapeDtypeStruct((steps, 8, rows), F32),
            pltpu.HBM((rows, width), F32),
            jax.ShapeDtypeStruct((rows, width + SIDE), BF16),
            pltpu.HBM((rows, heads_all), BF16),
            jax.ShapeDtypeStruct((rows, SIDE), F32),
        ],
        compiler_params=params(40),
        cost_estimate=cost(50 * rows * keys * heads_all),
        name="attend",
    )(place, *hbm(queries, keyval, keyval, tokens), gains, router, named, *hbm(wo))


def attend_back_kernel(
    groups,
    place_ref,
    q_ref,
    k_ref,
    v_ref,
    grad_ref,
    out_ref,
    max_ref,
    total_ref,
    cos_ref,
    sin_ref,
    hn_ref,
    gq_ref,
    gk_ref,
    gv_ref,
    part_ref,
    bias_ref,
    held_ref,
    hn_t_ref,
    sems,
):
    rows = q_ref.shape[0]
    keys = k_ref.shape[0]
    chunk = 256

    @pl.when(pl.program_id(0) == 0)
    def _():
        bias_ref[...] = key_bias(place_ref, keys, rows)
        for start in range(0, keys, rows):
            hn_t_ref[:, start : start + rows] = low(transposed(hn_ref[start : start + rows, :]))

    q_t = low(transposed(q_ref[...]))
    k_t = low(transposed(k_ref[...]))
    grad_t = transposed(grad_ref[...])
    out_t = transposed(out_ref[...])
    q_parts, g_parts, deltas, tops, grads = [], [], [], [], []
    for group in range(2):
        q_part, g_part, delta = [], [], []
        for h in range(groups):
            n = group * groups + h
            total = total_ref[0, n : n + 1]
            grad = grad_t[n * HD : (n + 1) * HD]
            q_part.append(widened(q_t[n * HD : (n + 1) * HD], group))
            g_part.append(widened(low(grad / total), group))
            delta.append(jnp.sum(out_t[n * HD : (n + 1) * HD] * grad, 0, keepdims=True) / total)
        q_parts.append(jnp.concatenate(q_part, 1))
        g_parts.append(jnp.concatenate(g_part, 1))
        deltas.append(jnp.concatenate(delta, 1))
        tops.append(
            jnp.concatenate(
                [max_ref[0, group * groups + h : group * groups + h + 1] for h in range(groups)], 1
            )
        )
        grads.append(jnp.zeros((2 * HD, groups * rows), F32))
    for start in range(0, keys, chunk):
        bias = bias_ref[start : start + chunk]
        bias = jnp.concatenate([bias] * groups, 1)
        grad_k = jnp.zeros((chunk, 2 * HD), F32)
        grad_v = jnp.zeros((chunk, 2 * HD), F32)
        for group in range(2):
            scores = dot_nn(k_ref[start : start + chunk], q_parts[group])
            w = jnp.exp(scores + bias - tops[group])
            gp = dot_nn(v_ref[start : start + chunk], g_parts[group])
            gs = low(w * (gp - deltas[group]))
            grad_v = grad_v + dot_nt(low(w), g_parts[group])
            grad_k = grad_k + dot_nt(gs, q_parts[group])
            grads[group] = grads[group] + dot_nn(k_t[:, start : start + chunk], gs)
        at = slice(start, start + chunk)
        gk_ref[at] = low(turn(grad_k, cos_ref[at, :], -sin_ref[at, :]))
        gv_ref[at] = low(grad_v)
    step, slot = pl.program_id(0), lax.rem(pl.program_id(0), 2)
    steps = part_ref.shape[1] // held_ref.shape[2]
    heads, two = 2 * groups * HD, 2 * HD

    def copies(n, slot):
        spans = ((0, heads), (steps * heads, two), (steps * (heads + two), two))
        out, col = [], 0
        for i, (first, size) in enumerate(spans):
            dst = pl.ds(pl.multiple_of(first + n * size, two), size)
            src = held_ref.at[slot, :, col : col + size]
            out.append(pltpu.make_async_copy(src, part_ref.at[:, dst], sems.at[slot, i]))
            col += size
        return out

    @pl.when(step >= 2)
    def _():
        for copy in copies(step - 2, slot):
            copy.wait()

    both = jnp.concatenate([gk_ref[...], gv_ref[...]], 1)
    held_ref[slot, :, heads:] = low(dot_nn(hn_t_ref[...], both))
    parts = []
    for group in range(2):
        for h in range(groups):
            parts.append(grads[group][group * HD : (group + 1) * HD, h * rows : (h + 1) * rows])
    grad_q = jnp.transpose(jnp.concatenate(parts, 0)) * (HD ** (-0.5))
    for d in range(0, 2 * groups * HD, 2 * HD):
        gq_ref[:, d : d + 2 * HD] = low(
            turn(grad_q[:, d : d + 2 * HD], cos_ref[:rows, :], -sin_ref[:rows, :])
        )
    held_ref[slot, :, :heads] = low(dot_nn(hn_t_ref[:, :rows], gq_ref[...]))
    for copy in copies(step, slot):
        copy.start()

    @pl.when(step == steps - 1)
    def _():
        for copy in copies(step, slot):
            copy.wait()

    @pl.when((step == steps - 1) & (step >= 1))
    def _():
        for copy in copies(step - 1, 1 - slot):
            copy.wait()


def attend_back(place, queries, keyval, grad_heads, attn, tops, totals, cosine, sine, hn, groups):
    rows, width = queries.shape
    keys, kv = keyval.shape
    steps = kv // 2 // (2 * HD)
    heads = 2 * groups * HD
    model = hn.shape[1]
    head_spec = pl.BlockSpec((rows, heads), lambda i, s: (0, i))
    key_spec = pl.BlockSpec((keys, 2 * HD), lambda i, s: (0, i))
    stat_spec = pl.BlockSpec((1, 8, rows), lambda i, s: (i, 0, 0))
    return pl.pallas_call(
        functools.partial(attend_back_kernel, groups),
        grid_spec=pltpu.PrefetchScalarGridSpec(
            num_scalar_prefetch=1,
            grid=(steps,),
            in_specs=[
                head_spec,
                key_spec,
                pl.BlockSpec((keys, 2 * HD), lambda i, s: (0, steps + i)),
                head_spec,
                head_spec,
                stat_spec,
                stat_spec,
                pl.BlockSpec((keys, 2 * HD), lambda i, s: (0, 0)),
                pl.BlockSpec((keys, 2 * HD), lambda i, s: (0, 0)),
                pl.BlockSpec((keys, model), lambda i, s: (0, 0)),
            ],
            out_specs=[
                head_spec,
                key_spec,
                key_spec,
                pl.BlockSpec(memory_space=pl.ANY),
            ],
            scratch_shapes=[
                pltpu.VMEM((keys, rows), F32),
                pltpu.VMEM((2, model, heads + 4 * HD), BF16),
                pltpu.VMEM((model, keys), BF16),
                pltpu.SemaphoreType.DMA((2, 3)),
            ],
        ),
        out_shape=[
            jax.ShapeDtypeStruct((rows, width), BF16),
            jax.ShapeDtypeStruct((keys, kv // 2), BF16),
            jax.ShapeDtypeStruct((keys, kv // 2), BF16),
            pltpu.HBM((model, width + kv), BF16),
        ],
        compiler_params=params(44),
        cost_estimate=cost(64 * rows * keys * width),
        name="attend_back",
    )(place, *hbm(queries, keyval, keyval, grad_heads, attn, tops, totals, cosine, sine, hn))


def slot_pick(slot, cap):
    place = lax.broadcasted_iota(jnp.int32, (cap, slot.shape[1]), 0).astype(F32)
    return place == slot


def weight_chunks(grads, x_ref, c_ref, ggu_ref, act_ref):
    hidden, width = act_ref.shape[1], c_ref.shape[1]
    size, wide = grads[0].shape
    rest = width - wide
    half = hidden // 2
    for h in range(2):
        at = slice(h * half, (h + 1) * half)
        part = low(dot_tn(act_ref[:, at], c_ref[...]))
        grads[0][at, :] = part[:, :wide]
        grads[0][hidden:, h * rest : (h + 1) * rest] = part[:, wide:]
    step = size // 2
    for c, ref in enumerate(grads[1:]):
        for h in range(2):
            cols = slice(c * size + h * step, c * size + (h + 1) * step)
            ref[h * step : (h + 1) * step, :] = low(dot_tn(x_ref[:, cols], ggu_ref[...]))


def expert_kernel(counts, cap, tile, e, earlier, last, number_ref, *refs):
    parts, refs = refs[: sum(counts)], refs[sum(counts) :]
    cot_ref, wgu_all_ref, wd_all_ref = refs[:3]
    gin_before, refs = refs[3 : 3 + earlier], refs[3 + earlier :]
    out_ref, slots_ref, result_ref = refs[:3]
    grads = refs[3:6]
    x_ref, c_ref, ggu_ref, act_ref, sg_ref, wgu_ref, wd_ref, sems = refs[6:14]
    if last:
        gin_ref, load_ref, store_ref = refs[14:]
    else:
        gin_ref = result_ref
    loads = [
        pltpu.make_async_copy(wgu_all_ref.at[e], wgu_ref, sems.at[0]),
        pltpu.make_async_copy(wd_all_ref.at[e], wd_ref, sems.at[1]),
    ]
    for load in loads:
        load.start()
    blocks = len(counts)
    hidden, width = wd_ref.shape
    rows = cot_ref.shape[0] // blocks
    total = blocks * cap
    index, expert = number_ref[0], number_ref[1]
    lane = lax.broadcasted_iota(jnp.int32, (8, SIDE), 1)
    pick_slot = low(jnp.where(lane == expert, 1.0, 0.0))
    pick_gate = low(jnp.where((lane == expert) | (lane == expert + SIDE // 2), 1.0, 0.0))
    n = 0
    for b in range(blocks):
        hn = parts[n : n + counts[b]]
        n += counts[b]
        src = pl.ds(pl.multiple_of((index ^ b) * rows, rows), rows)
        slot = dot_nt(pick_slot, cot_ref[src, width:])[:1] - 1.0
        gate = [dot_nt(pick_gate, part[:, width:]) for part in hn]
        gate = (jnp.concatenate(gate, 1) if len(gate) > 1 else gate[0])[:1]
        slots_ref[b : b + 1, :] = slot
        hit = slot_pick(slot, cap)
        pick = low(jnp.where(hit, 1.0, 0.0))
        at = slice(b * cap, (b + 1) * cap)
        taken, start = None, 0
        for part in hn:
            piece = dot_nn(pick[:, start : start + part.shape[0]], part[:, :width])
            taken = piece if taken is None else taken + piece
            start += part.shape[0]
        x_ref[at, :] = low(taken)
        c_ref[at, :] = low(dot_nn(pick, cot_ref[src, :width]))
        gate = jnp.sum(jnp.where(hit, gate, 0.0), 1, keepdims=True)
        sg_ref[at, :] = jnp.broadcast_to(gate, (cap, 128))

    def middle(t, carry):
        at = pl.ds(pl.multiple_of(t * tile, 16), tile)
        gate_up = dot_nn(x_ref[at, :], wgu_ref[...])
        g = gate_up[:, :hidden]
        u = gate_up[:, hidden:]
        sigma = jax.nn.sigmoid(g)
        silu = g * sigma
        act = low(silu * u)
        slot_gate = sg_ref[at, :][:, :1]
        back = dot_nt(c_ref[at, :], wd_ref[...])
        gate_grad = jnp.sum(up(act) * back, 1, keepdims=True)
        back = back * slot_gate
        act_ref[at, :] = low(up(act) * slot_gate)
        ggu_ref[at, :hidden] = low(back * u * (sigma * (1.0 + g * (1.0 - sigma))))
        ggu_ref[at, hidden:] = low(back * silu)
        out_ref[at, :] = low(dot_nn(act, wd_ref[...]) * slot_gate)
        gin_ref[at, :width] = low(dot_nt(ggu_ref[at, :], wgu_ref[...]))
        lane = lax.broadcasted_iota(jnp.int32, (tile, SIDE), 1)
        high = up(low(gate_grad))
        side = jnp.where(lane == expert, high, 0.0)
        side = jnp.where(lane == expert + SIDE // 2, gate_grad - high, side)
        gin_ref[at, width:] = low(side)
        return carry

    for load in loads:
        load.wait()
    lax.fori_loop(0, total // tile, middle, 0)
    if not last:
        weight_chunks(grads, x_ref, c_ref, ggu_ref, act_ref)
        return

    def load_before(b):
        return [
            pltpu.make_async_copy(
                ref.at[b * cap : (b + 1) * cap], load_ref.at[b % 2, i], sems.at[2 + 2 * i + b % 2]
            )
            for i, ref in enumerate(gin_before)
        ]

    def store(b):
        dst = pl.ds(pl.multiple_of((index ^ b) * rows, rows), rows)
        return pltpu.make_async_copy(
            store_ref.at[b % 2], result_ref.at[dst], sems.at[2 + 2 * earlier + b % 2]
        )

    for load in load_before(0):
        load.start()
    for b in range(blocks):
        if b + 1 < blocks:
            for load in load_before(b + 1):
                load.start()
        src = pl.ds(pl.multiple_of((index ^ b) * rows, rows), rows)
        order = up(cot_ref[src, width:])
        lane = lax.broadcasted_iota(jnp.int32, order.shape, 1)
        place = lax.broadcasted_iota(jnp.int32, (rows, cap), 1).astype(F32)

        def pick(number):
            slot = jnp.sum(jnp.where(lane == number, order, 0.0), 1, keepdims=True) - 1.0
            return low(jnp.where(place == slot, 1.0, 0.0))

        acc = dot_nn(pick(expert), gin_ref[b * cap : (b + 1) * cap, :])
        for i, load in enumerate(load_before(b)):
            load.wait()
            acc = acc + dot_nn(pick(expert - earlier + i), load_ref[b % 2, i])
        if b >= 2:
            store(b - 2).wait()
        store_ref[b % 2] = low(acc)
        store(b).start()
    weight_chunks(grads, x_ref, c_ref, ggu_ref, act_ref)
    for b in range(max(blocks - 2, 0), blocks):
        store(b).wait()


def unpack_down(chunk, hidden):
    rest = chunk.shape[1] // 2
    right = jnp.concatenate([chunk[hidden:, :rest], chunk[hidden:, rest:]], 0)
    return jnp.concatenate([chunk[:hidden], right], 1)


def run_expert(number, pieces, cot, w_gate_up, w_down, e, cap, gins):
    counts = [len(p) for p in pieces]
    flat = [h for p in pieces for h in p]
    blocks = len(counts)
    rows = cot.shape[0] // blocks
    hidden, width = w_down.shape[1:]
    total = blocks * cap
    tile = max(t for t in range(16, 401, 16) if total % t == 0)
    last = e + 1 == w_down.shape[0]
    earlier = len(gins) if last else 0
    anywhere = pl.BlockSpec(memory_space=pl.ANY)
    chunk = jax.ShapeDtypeStruct((width // 2, 2 * hidden), BF16)
    work = [(total, width), (total, width), (total, 2 * hidden), (total, hidden)]
    gin_shape = (total, width + SIDE)
    scratch = [pltpu.VMEM(shape, BF16) for shape in work] + [
        pltpu.VMEM((total, 128), F32),
        pltpu.VMEM((width, 2 * hidden), BF16),
        pltpu.VMEM((hidden, width), BF16),
        pltpu.SemaphoreType.DMA((4 + 2 * earlier,)),
    ]
    if last:
        scratch += [
            pltpu.VMEM(gin_shape, BF16),
            pltpu.VMEM((2, max(earlier, 1), cap, width + SIDE), BF16),
            pltpu.VMEM((2, rows, width + SIDE), BF16),
        ]
    result = pltpu.HBM((blocks * rows, width + SIDE) if last else gin_shape, BF16)
    got = pl.pallas_call(
        functools.partial(expert_kernel, counts, cap, tile, e, earlier, last),
        in_specs=[pl.BlockSpec(memory_space=pltpu.SMEM)]
        + [WHOLE] * (len(flat) + 1)
        + [anywhere] * (2 + earlier),
        out_specs=[WHOLE, WHOLE, anywhere if last else WHOLE] + [WHOLE] * 3,
        out_shape=[
            pltpu.HBM((total, width), BF16),
            jax.ShapeDtypeStruct((blocks, rows), F32),
            result,
        ]
        + [chunk] * 3,
        scratch_shapes=scratch,
        compiler_params=params(56),
        cost_estimate=cost(44 * total * width * hidden),
        name="expert",
    )(number, *flat, cot, w_gate_up, w_down, *gins[:earlier])
    return got[0], got[1], got[2], got[3:]


def combine_kernel(count, cap, first, stride, number_ref, *refs):
    slots, parts, out_ref = refs[:count], refs[count : 2 * count], refs[2 * count]
    b = pl.program_id(0) * stride + first
    rows = slots[0].shape[1]
    place = lax.broadcasted_iota(jnp.int32, (cap, rows), 0).astype(F32)
    acc = None
    for e in range(count):
        pick = low(jnp.where(place == slots[e][pl.ds(b, 1), :], 1.0, 0.0))
        part = dot_tn(pick, parts[e][...])
        acc = part if acc is None else acc + part
    out_ref[...] = low(acc)


def combine(number, slots, parts, cap, chosen, order):
    blocks, rows = slots[0].shape
    count = len(parts)
    width = parts[0].shape[1]
    first, stride = chosen.start, chosen.step
    return pl.pallas_call(
        functools.partial(combine_kernel, count, cap, first, stride),
        grid_spec=pltpu.PrefetchScalarGridSpec(
            num_scalar_prefetch=1,
            grid=(len(chosen),),
            in_specs=[pl.BlockSpec((blocks, rows), lambda n, s: (0, 0))] * count
            + [pl.BlockSpec((cap, width), lambda n, s: (n * stride + first, 0))] * count,
            out_specs=pl.BlockSpec((rows, width), lambda n, s: (order(n, s[0]), 0)),
        ),
        out_shape=pltpu.HBM((len(chosen) * rows, width), BF16),
        compiler_params=params(20),
        cost_estimate=cost(10 * len(chosen) * cap * rows * width),
        name="combine",
    )(number, *slots, *parts)


def rope_tables(places):
    half = HD // 2
    frequency = ROPE_BASE ** (-jnp.arange(half, dtype=F32) * 2.0 / HD)
    angles = places.astype(F32)[:, None] * frequency[None, :]
    cosine, sine = jnp.cos(angles), jnp.sin(angles)
    return jnp.concatenate([cosine] * 4, 1), jnp.concatenate([-sine, sine] * 2, 1)


def per_device(
    tokens,
    lengths,
    routes,
    cotangent,
    gain_attn,
    gain_moe,
    w_query,
    w_keyval,
    w_output,
    w_router,
    w_gate_up,
    w_down,
):
    rows = tokens.shape[1]
    width = tokens.shape[2]
    experts = w_router.shape[1]
    local_experts = w_gate_up.shape[0]
    kv_width = w_keyval.shape[1] // 2
    head_total = w_query.shape[1]
    groups = head_total // kv_width
    dp_count = lax.axis_size("dp")
    ctx_count = lax.axis_size("ctx")
    dp_index = lax.axis_index("dp").astype(jnp.int32)
    ctx_index = lax.axis_index("ctx").astype(jnp.int32)
    cap = -(-(rows * 9 // 16) // 16) * 16
    length = lengths[0]
    places = ctx_index * rows + jnp.arange(rows, dtype=jnp.int32)
    valid = (places < length)[:, None]
    index = jnp.reshape(dp_index, (1,))

    pad = jnp.zeros((w_router.shape[0], 128 - experts - 2), BF16)
    first_w = Gather(
        jnp.concatenate(
            [w_query, w_keyval, w_router, gain_attn[:, None], gain_moe[:, None], pad], 1
        )
    )

    named = jnp.any(routes[0][..., None] == jnp.arange(SIDE, dtype=jnp.int32), 1).astype(BF16)
    order = dot_nn(jnp.tril(jnp.ones((rows, rows), BF16)), named) * up(named)
    grad_y = jnp.where(valid, cotangent[0], BF16(0))
    cot = jnp.concatenate([grad_y, low(order)], 1)

    seq = [halves(tokens[0])]
    back = jnp.arange(ctx_count, dtype=jnp.int32)[:, None] * rows
    tables = rope_tables((places[None, :] - back).reshape(-1))

    def next_block(part):
        return shift(seq[-1][part], 1)

    first_w.near()
    seq.append([next_block(0), next_block(1)])
    early = next_block(0)
    output_w = lax.all_gather(w_output, "dp", axis=0, tiled=True)
    _, tables, cot, seq[1], early = sync(first_w, tables, cot, seq[1], early)
    cot_all = lax.all_gather(cot, "dp", axis=0, tiled=True)
    first_w.far()
    seq.append([early, next_block(1)])
    early = next_block(0)
    _, seq[2], early = sync(first_w, seq[2], early)
    seq.append([early, next_block(1)])
    for _ in range(ctx_count - 4):
        seq.append([next_block(0), next_block(1)])
    cosine, sine = tables
    projected = project(index, first_w.pieces(), seq, cosine, sine, experts, head_total)
    queries, keyval, hn_seq, query_w, keyval_w, router_w, gains = projected
    keyval, hn_seq = project_last(seq[-1], gains, keyval_w, cosine, sine, keyval, hn_seq)

    place = jnp.stack([ctx_index, length])
    attn, tops, totals, resid, hn_two, attn_low, gates = attend(
        place, queries, keyval, tokens[0], gains, router_w, named, output_w, groups
    )

    hn_g = Gather(hn_two)
    hn_g.near()
    sync(hn_g)
    hn_pieces = hn_g.pieces()
    sums = LineSums()
    outs, gins, slots = [], [], []
    for e in range(local_experts):
        number = jnp.stack([dp_index, dp_index * local_experts + e])
        out, slot, gin, grads = run_expert(
            number, hn_pieces, cot_all, w_gate_up, w_down, e, cap, gins
        )
        outs.append(out)
        gins.append(gin)
        slots.append(slot)
        if e + 1 < local_experts:
            for c, v in enumerate(grads):
                sums.add(f"{e}.{c}", v)
            hn_pieces, cot_all = sums.step(hn_pieces, cot_all)
    for c, v in enumerate(grads):
        sums.add(f"{local_experts - 1}.{c}", v)
    (gin_tokens,) = sums.step(gins[-1])
    gin_sum = lax.psum_scatter(gin_tokens, "dp", scatter_dimension=0, tiled=True)
    outs, slots = sums.step(outs, slots)
    out_tokens = combine(index, slots, outs, cap, range(0, dp_count, 1), lambda n, i: n ^ i)

    backed = router_back(gin_sum, gates, router_w, gains, resid, grad_y, output_w, experts)
    *backed, out_tokens = sums.step(*sums.hold(*backed, out_tokens))
    grad_resid, grad_heads, *for_output = backed

    backed = attend_back(
        place, queries, keyval, grad_heads, attn, tops, totals, cosine, sine, hn_seq, groups
    )
    backed = sums.step(*backed, *for_output)
    grad_query, grad_keys, grad_values, part_first, grad_attn, grad_logits, gain_two = backed
    share_first = lax.psum_scatter(part_first, "dp", scatter_dimension=0, tiled=True)
    part_output = output_grad(attn_low, grad_attn, hn_two, grad_logits, gain_two, experts)
    (part_output,) = sums.step(part_output)
    share_output = lax.psum_scatter(part_output, "dp", scatter_dimension=0, tiled=True)
    share_query, share_keyval = share_first[:, :head_total], share_first[:, head_total:]
    gain_grad = jnp.sum(up(share_query) * up(w_query), 1, keepdims=True) + jnp.sum(
        up(share_keyval) * up(w_keyval), 1, keepdims=True
    )
    gain_grad = jnp.broadcast_to(gain_grad / up(gain_attn)[:, None], (w_query.shape[0], SIDE))
    share_keyval = jnp.concatenate([share_keyval, low(gain_grad)], 1)
    sums.add("query", share_query)
    sums.add("keyval", share_keyval)
    sums.step(take=2)
    gate_up, down = jnp.zeros(w_gate_up.shape, F32), jnp.zeros(w_down.shape, F32)
    placed = set()

    def place_done(gate_up, down):
        for e in range(local_experts):
            for c in range(3):
                if f"{e}.{c}" not in sums.done or f"{e}.{c}" in placed:
                    continue
                placed.add(f"{e}.{c}")
                part = sums.total(f"{e}.{c}")
                if c == 0:
                    part = unpack_down(part, w_down.shape[1])
                    down = lax.dynamic_update_slice(down, part[None], (e, 0, 0))
                else:
                    at = (e, (c - 1) * part.shape[0], 0)
                    gate_up = lax.dynamic_update_slice(gate_up, part[None], at)
        return gate_up, down

    grad_kv = jnp.concatenate([grad_keys, grad_values], 1)
    blocks = [grad_kv[r * rows : (r + 1) * rows] for r in range(ctx_count)]
    held = blocks[-1]
    for r in range(ctx_count - 2, -1, -1):
        pairs = [(i, i - 1) for i in range(r + 1, ctx_count)]
        held = add_low(lax.ppermute(held, "ctx", pairs), blocks[r])
        if r == max(ctx_count - 2, 1):
            held, out_tokens = sums.step(held, out_tokens)
            moe = lax.psum_scatter(out_tokens, "dp", scatter_dimension=0, tiled=True)
            sums.add("output", share_output)
        elif r:
            (held,) = sums.step(held)

    grad_hn_one = dot_nt(grad_query, query_w) + dot_nt(held, keyval_w)
    inputs = up(tokens[0])
    inv_one = lax.rsqrt(jnp.mean(inputs * inputs, -1, keepdims=True) + NORM_EPS)
    normed_one = inputs * inv_one
    scaled_one = grad_hn_one * gains[0:1]
    grad_inputs = grad_resid + inv_one * (
        scaled_one - normed_one * jnp.mean(scaled_one * normed_one, -1, keepdims=True)
    )
    grad_inputs = low(grad_inputs)

    outcome = low(jnp.where(valid, resid + up(moe), 0.0))

    wanted = [f"{e}.{c}" for e in range(local_experts) for c in range(3)]
    while not all(name in sums.done for name in wanted):
        sums.step()
    gate_up, down = place_done(gate_up, down)
    gate_up, down, grad_inputs = sums.step(gate_up, down, grad_inputs)
    while not ("query" in sums.done and "keyval" in sums.done):
        sums.step()
    total_query, total_keyval = sums.total("query"), sums.total("keyval")
    ready = (total_query, total_keyval[:, : 2 * kv_width], total_keyval[:, 2 * kv_width])
    total_query, total_keyval, total_gain, outcome = sums.step(*ready, outcome)
    while sums.busy():
        sums.step()
    total_output = sums.total("output")
    return (
        outcome[None],
        grad_inputs[None],
        total_gain,
        total_output[:, width + experts],
        total_query,
        total_keyval,
        total_output[:, :width],
        total_output[:, width : width + experts],
        gate_up,
        down,
    )


def solution(mesh):
    in_specs = (
        P("dp", "ctx", None),
        P("dp"),
        P("dp", "ctx", None),
        P("dp", "ctx", None),
        P("dp"),
        P("dp"),
        P("dp", None),
        P("dp", None),
        P("dp", None),
        P("dp", None),
        P("dp", None, None),
        P("dp", None, None),
    )
    out_specs = (
        P("dp", "ctx", None),
        P("dp", "ctx", None),
        P("dp"),
        P("dp"),
        P("dp", None),
        P("dp", None),
        P("dp", None),
        P("dp", None),
        P("dp", None, None),
        P("dp", None, None),
    )
    return jax.shard_map(
        per_device, mesh=mesh, in_specs=in_specs, out_specs=out_specs, check_vma=False
    )
```

```python
import functools

import jax
import jax.numpy as jnp
from jax import lax
from jax.experimental import pallas as pl
from jax.experimental.pallas import tpu as pltpu
from jax.sharding import PartitionSpec as P

HD = 64
NORM_EPS = 1e-06
ROPE_BASE = 10000.0
MASK_FLOOR = -1e30
F32 = jnp.float32
BF16 = jnp.bfloat16
MIB = 1024 * 1024
SIDE = 128
WHOLE = pl.BlockSpec()


def params(mib):
    return pltpu.CompilerParams(vmem_limit_bytes=mib * MIB)


def hbm(*arrays_in):
    return [pltpu.with_memory_space_constraint(v, pltpu.HBM) for v in arrays_in]


def cost(flops):
    return pl.CostEstimate(flops=int(flops) // 64, bytes_accessed=1024, transcendentals=0)


def up(v):
    return v.astype(F32)


def low(v):
    return v.astype(BF16)


def dot_nn(a, b):
    return lax.dot_general(a, b, (((1,), (0,)), ((), ())), preferred_element_type=F32)


def dot_nt(a, b):
    return lax.dot_general(a, b, (((1,), (1,)), ((), ())), preferred_element_type=F32)


def dot_tn(a, b):
    return lax.dot_general(a, b, (((0,), (0,)), ((), ())), preferred_element_type=F32)


def swap(v, mask):
    count = lax.axis_size("dp")
    return lax.ppermute(v, "dp", [(i, i ^ mask) for i in range(count)])


def halves(v):
    mid = v.shape[0] // 2
    return [v[:mid], v[mid:]]


class Gather:
    def __init__(self, v):
        self.special = lax.axis_size("dp") == 8
        self.stage = 0
        self.live = [v]

    def near(self):
        if self.special and self.stage == 0:
            v = self.live[0]
            self.live = [v, swap(v, 2), swap(v, 4)]
        self.stage = max(self.stage, 1)

    def far(self):
        self.near()
        if self.special and self.stage == 1:
            v, along_x, along_y = self.live
            self.live = self.live + [swap(halves(along_x)[0], 4), swap(halves(along_y)[1], 2)]
        self.stage = max(self.stage, 2)

    def pieces(self):
        self.far()
        if not self.special:
            out = [[self.live[0]]]
            bit = 1
            while bit < lax.axis_size("dp"):
                out = out + [[swap(h, bit) for h in piece] for piece in out]
                bit *= 2
            return out
        v, along_x, along_y, far_a, far_b = self.live
        even = [[v], [along_x], [along_y], [far_a, far_b]]
        out = []
        for piece in even:
            out += [piece, [swap(h, 1) for h in piece]]
        return out


def sync(*items):
    plain = [i.live if isinstance(i, Gather) else i for i in items]
    plain = lax.optimization_barrier(plain)
    for item, got in zip(items, plain):
        if isinstance(item, Gather):
            item.live = list(got)
    return plain


def add_low(a, b):
    return low(up(a) + up(b))


def shift(v, step):
    count = lax.axis_size("ctx")
    return lax.ppermute(
        v, "ctx", [(i, i + step) for i in range(count) if 0 <= i + step < count]
    )


class LineSums:
    DEPTH = 1

    def __init__(self):
        count = lax.axis_size("ctx")
        index = lax.axis_index("ctx")
        self.plain = count != 4
        self.outer = (index == 0) | (index == count - 1)
        self.waiting = []
        self.flights = [[] for _ in range(self.DEPTH)]
        self.done = {}

    def add(self, name, v):
        if self.plain:
            self.done[name] = lax.psum(v, "ctx")
        else:
            self.waiting.append((name, v))

    def busy(self):
        return bool(self.waiting or any(self.flights))

    def step(self, *critical, take=1, flush=False):
        if self.plain:
            return critical
        got = self.flights.pop(0)
        while flush and self.flights:
            got = got + self.flights.pop(0)
        ready = {"first": [], "inner": [], "last": []}
        for kind, name, v, arrived in got:
            if kind == "first":
                ready["inner"].append((name, add_low(v, arrived)))
            elif kind == "inner":
                ready["last"].append((name, add_low(v, arrived)))
            else:
                self.done[name] = (v, arrived)
        for _ in range(take):
            if self.waiting:
                ready["first"].append(self.waiting.pop(0))
        shared = []
        for first in list(ready["first"]):
            for last in list(ready["last"]):
                if first[1].shape == last[1].shape:
                    shared.append((first[0], last[0], first[1], jnp.where(self.outer, first[1], last[1])))
                    ready["first"] = [r for r in ready["first"] if r is not first]
                    ready["last"] = [r for r in ready["last"] if r is not last]
                    break
        both = [(own, payload) for _, _, own, payload in shared]
        alone = {kind: [v for _, v in entries] for kind, entries in ready.items()}
        held = lax.optimization_barrier((both, alone, self.done, critical))
        both, alone, self.done, critical = held
        flight = []
        for (first, last, _, _), (own, payload) in zip(shared, both):
            back = lax.ppermute(payload, "ctx", [(0, 1), (1, 0), (2, 3), (3, 2)])
            flight.append(("first", first, own, back))
            flight.append(("last", last, payload, back))
        routes = {
            "first": [(0, 1), (3, 2)],
            "inner": [(1, 2), (2, 1)],
            "last": [(1, 0), (2, 3)],
        }
        for kind, pairs in routes.items():
            for (name, _), v in zip(ready[kind], alone[kind]):
                flight.append((kind, name, v, lax.ppermute(v, "ctx", pairs)))
        self.flights.append(flight)
        return critical

    def launch(self, name, v):
        if self.plain:
            self.add(name, v)
        else:
            got = lax.ppermute(v, "ctx", [(0, 1), (3, 2)])
            self.flights[-1].append(("first", name, v, got))

    def hold(self, *critical):
        if self.plain:
            return critical
        own = [[entry[2] for entry in flight] for flight in self.flights]
        own, critical = lax.optimization_barrier((own, critical))
        for n, flight in enumerate(self.flights):
            self.flights[n] = [
                (kind, name, v, arrived)
                for (kind, name, _, arrived), v in zip(flight, own[n])
            ]
        return critical

    def total(self, name):
        if self.plain:
            return up(self.done[name])
        v, arrived = self.done[name]
        return up(jnp.where(self.outer, arrived, v))


def lay_rows(pieces, counts, index, put):
    n = 0
    for k, parts in enumerate(counts):
        rows = sum(pieces[n + i].shape[0] for i in range(parts))
        start = (index ^ k) * rows
        for i in range(parts):
            put(pl.multiple_of(start, 16), pieces[n + i])
            start = start + pieces[n + i].shape[0]
        n += parts


def turn(v, cosine, sine):
    lane = lax.broadcasted_iota(jnp.int32, v.shape, 1)
    first = lax.rem(lane, HD) < HD // 2
    partner = jnp.where(
        first, pltpu.roll(v, 2 * HD - HD // 2, 1), pltpu.roll(v, HD // 2, 1)
    )
    return v * cosine + partner * sine


def normed_rows(parts, gain):
    x = jnp.concatenate([up(p[...]) for p in parts], 0)
    return low(x * lax.rsqrt(jnp.mean(x * x, -1, keepdims=True) + NORM_EPS) * gain)


def key_rows(hn, wkv_ref, cosine, sine):
    raw = dot_nn(hn, wkv_ref[...])
    two = 2 * HD
    keys = raw.shape[1] // 2
    turned = [turn(raw[:, d : d + two], cosine, sine) for d in range(0, keys, two)]
    return low(jnp.concatenate(turned + [raw[:, keys:]], 1))


def project_kernel(counts, blocks, experts, index_ref, *refs):
    pieces = refs[: sum(counts)]
    seq = refs[sum(counts) : sum(counts) + 2 * blocks]
    cos_ref, sin_ref = refs[sum(counts) + 2 * blocks : sum(counts) + 2 * blocks + 2]
    q_ref, kv_ref, hn_ref, wq_ref, wkv_ref, router_ref, gains_ref, small_ref = refs[
        sum(counts) + 2 * blocks + 2 :
    ]
    q_width, kv_width = wq_ref.shape[1], wkv_ref.shape[1]

    def put(start, ref):
        at = pl.ds(start, ref.shape[0])
        wq_ref[at, :] = ref[:, :q_width]
        wkv_ref[at, :] = ref[:, q_width : q_width + kv_width]
        small_ref[at, :] = ref[:, q_width + kv_width :]

    lay_rows(pieces, counts, index_ref[0], put)
    small = up(small_ref[...])
    lane = lax.broadcasted_iota(jnp.int32, small.shape, 1)
    router_ref[...] = low(jnp.where(lane < experts, small, 0.0))
    gains_ref[...] = jnp.transpose(small)[experts : experts + 8]
    gain = gains_ref[0:1, :]
    rows = 2 * seq[0].shape[0]
    for r in range(blocks):
        at = slice(r * rows, (r + 1) * rows)
        hn = normed_rows(seq[2 * r : 2 * r + 2], gain)
        hn_ref[at, :] = hn
        kv_ref[at, :] = key_rows(hn, wkv_ref, cos_ref[at, :], sin_ref[at, :])
    two = 2 * HD
    for c in range(0, q_width, 2 * two):
        raw = dot_nn(hn_ref[:rows, :], wq_ref[:, c : c + 2 * two])
        for d in (0, two):
            rot = turn(raw[:, d : d + two], cos_ref[:rows, :], sin_ref[:rows, :])
            q_ref[:, c + d : c + d + two] = low(up(low(rot)) * (HD ** (-0.5)))


def project(index, pieces, seq, cosine, sine, experts, q_width):
    counts = [len(p) for p in pieces]
    flat = [h for p in pieces for h in p]
    halves_in = [h for pair in seq[:-1] for h in pair]
    rows, width = 2 * seq[0][0].shape[0], seq[0][0].shape[1]
    kv_width = flat[0].shape[1] - q_width - 128
    keys = rows * len(seq)
    return pl.pallas_call(
        functools.partial(project_kernel, counts, len(seq) - 1, experts),
        in_specs=[pl.BlockSpec(memory_space=pltpu.SMEM)] + [WHOLE] * (len(flat) + len(halves_in) + 2),
        out_specs=[WHOLE] * 7,
        out_shape=[
            jax.ShapeDtypeStruct((rows, q_width), BF16),
            jax.ShapeDtypeStruct((keys, kv_width), BF16),
            jax.ShapeDtypeStruct((keys, width), BF16),
            jax.ShapeDtypeStruct((width, q_width), BF16),
            jax.ShapeDtypeStruct((width, kv_width), BF16),
            jax.ShapeDtypeStruct((width, 128), BF16),
            jax.ShapeDtypeStruct((8, width), F32),
        ],
        scratch_shapes=[pltpu.VMEM((width, 128), BF16)],
        compiler_params=params(40),
        cost_estimate=cost(8 * width * (rows * q_width + keys * kv_width)),
        name="project",
    )(index, *flat, *halves_in, cosine, sine)


def project_last_kernel(
    a_ref, b_ref, gains_ref, wkv_ref, cos_ref, sin_ref, kv_in, hn_in, kv_out, hn_out, kv_ref, hn_ref, sems
):
    rows = kv_ref.shape[0]
    start = kv_out.shape[0] - rows
    hn = normed_rows((a_ref, b_ref), gains_ref[0:1, :])
    hn_ref[...] = hn
    hn_copy = pltpu.make_async_copy(hn_ref, hn_out.at[start : start + rows], sems.at[0])
    hn_copy.start()
    at = slice(start, start + rows)
    kv_ref[...] = key_rows(hn, wkv_ref, cos_ref[at, :], sin_ref[at, :])
    kv_copy = pltpu.make_async_copy(kv_ref, kv_out.at[start : start + rows], sems.at[1])
    kv_copy.start()
    hn_copy.wait()
    kv_copy.wait()


def project_last(last, gains, wkv, cosine, sine, keyval, hn):
    rows = 2 * last[0].shape[0]
    anywhere = pl.BlockSpec(memory_space=pl.ANY)
    return pl.pallas_call(
        project_last_kernel,
        in_specs=[WHOLE] * 6 + [anywhere] * 2,
        out_specs=[anywhere] * 2,
        out_shape=[
            jax.ShapeDtypeStruct(keyval.shape, BF16),
            jax.ShapeDtypeStruct(hn.shape, BF16),
        ],
        scratch_shapes=[
            pltpu.VMEM((rows, keyval.shape[1]), BF16),
            pltpu.VMEM((rows, hn.shape[1]), BF16),
            pltpu.SemaphoreType.DMA((2,)),
        ],
        input_output_aliases={6: 0, 7: 1},
        compiler_params=params(24),
        cost_estimate=cost(8 * rows * keyval.shape[1] * hn.shape[1]),
        name="project_last",
    )(*last, gains, wkv, cosine, sine, *hbm(keyval, hn))


def router_back_kernel(
    experts,
    total_ref,
    gates_ref,
    router_ref,
    gains_ref,
    resid_ref,
    cot_ref,
    wo_ref,
    grad_ref,
    heads_ref,
    attn_ref,
    logits_ref,
    gain_ref,
):
    width = resid_ref.shape[1]
    total = up(total_ref[...])
    side = total[:, width:]
    lane = lax.broadcasted_iota(jnp.int32, side.shape, 1)
    gate_grads = jnp.where(lane < experts, side + pltpu.roll(side, SIDE // 2, 1), 0.0)
    gates = gates_ref[...]
    mean = jnp.sum(gates * gate_grads, -1, keepdims=True)
    grad_logits = low(gates * (gate_grads - mean))
    grad_hn = total[:, :width] + dot_nt(grad_logits, router_ref[...])
    resid = resid_ref[...]
    inv = lax.rsqrt(jnp.mean(resid * resid, -1, keepdims=True) + NORM_EPS)
    normed = resid * inv
    gain = jnp.sum(grad_hn * normed, 0, keepdims=True)
    scaled = grad_hn * gains_ref[1:2, :]
    grad = up(cot_ref[...]) + inv * (scaled - normed * jnp.mean(scaled * normed, -1, keepdims=True))
    grad_ref[...] = grad
    grad_low = low(grad)
    heads_ref[...] = dot_nt(grad_low, wo_ref[...])
    attn_ref[...] = grad_low
    logits_ref[...] = grad_logits
    gain_ref[...] = jnp.broadcast_to(gain, gain_ref.shape)


def output_grad_kernel(
    experts, attn_ref, grad_ref, hn_ref, logits_ref, gain_ref, part_ref, held_ref, sems
):
    width = grad_ref.shape[1]
    copies = []

    def put(cols, value):
        held_ref[:, cols] = low(value)
        copies.append(
            pltpu.make_async_copy(held_ref.at[:, cols], part_ref.at[:, cols], sems.at[len(copies)])
        )
        copies[-1].start()

    small = dot_tn(hn_ref[:, :width], logits_ref[...])
    lane = lax.broadcasted_iota(jnp.int32, small.shape, 1)
    gain = jnp.transpose(jnp.broadcast_to(gain_ref[:1, :], (SIDE, width)))
    put(slice(width, width + SIDE), jnp.where(lane == experts, gain, small))
    attn_t = low(transposed(attn_ref[...]))
    for c in range(0, width, 256):
        put(slice(c, c + 256), dot_nn(attn_t, grad_ref[:, c : c + 256]))
    for copy in copies:
        copy.wait()


def output_grad(attn, grad, hn, logits, gain, experts):
    heads, width = attn.shape[1], grad.shape[1]
    return pl.pallas_call(
        functools.partial(output_grad_kernel, experts),
        in_specs=[WHOLE] * 5,
        out_specs=pl.BlockSpec(memory_space=pl.ANY),
        out_shape=pltpu.HBM((heads, width + SIDE), BF16),
        scratch_shapes=[
            pltpu.VMEM((heads, width + SIDE), BF16),
            pltpu.SemaphoreType.DMA((width // 256 + 1,)),
        ],
        compiler_params=params(28),
        cost_estimate=cost(4 * attn.shape[0] * heads * width),
        name="output_grad",
    )(*hbm(attn, grad, hn, logits, gain))


def router_back(total, gates, router, gains, resid, cot, wo, experts):
    rows, width = resid.shape
    heads = wo.shape[0]
    return pl.pallas_call(
        functools.partial(router_back_kernel, experts),
        in_specs=[WHOLE] * 7,
        out_specs=[WHOLE] * 5,
        out_shape=[
            pltpu.HBM((rows, width), F32),
            pltpu.HBM((rows, heads), F32),
            pltpu.HBM((rows, width), BF16),
            pltpu.HBM((rows, SIDE), BF16),
            pltpu.HBM((8, width), F32),
        ],
        compiler_params=params(30),
        cost_estimate=cost(14 * rows * heads * width),
        name="router_back",
    )(*hbm(total, gates, router), gains, *hbm(resid, cot, wo))


def transposed(v):
    return jnp.transpose(up(v))


def key_bias(place_ref, keys, rows):
    j = lax.broadcasted_iota(jnp.int32, (keys, rows), 0)
    i = lax.broadcasted_iota(jnp.int32, (keys, rows), 1)
    block = lax.div(j, rows)
    place = (place_ref[0] - block) * rows + (j - block * rows)
    allowed = (place >= 0) & (place <= place_ref[0] * rows + i) & (place < place_ref[1])
    return jnp.where(allowed, 0.0, MASK_FLOOR)


def widened(part, group):
    zero = jnp.zeros_like(part)
    return jnp.concatenate([part, zero] if group == 0 else [zero, part], 0)


def attend_kernel(
    groups,
    place_ref,
    q_ref,
    k_ref,
    v_ref,
    tok_ref,
    gains_ref,
    router_ref,
    named_ref,
    wo_all_ref,
    out_ref,
    max_ref,
    total_ref,
    resid_ref,
    hn_ref,
    low_ref,
    gates_ref,
    bias_ref,
    wo_ref,
    sem,
):
    rows = q_ref.shape[0]
    keys = k_ref.shape[0]
    width = tok_ref.shape[1]
    step = pl.program_id(0)
    load = pltpu.make_async_copy(wo_all_ref, wo_ref, sem)

    @pl.when(step == 0)
    def _():
        load.start()
        bias_ref[...] = key_bias(place_ref, keys, rows)

    q_t = low(transposed(q_ref[...]))
    v_t = low(transposed(v_ref[...]))
    outs, maxes, totals = [], [], []
    for group in range(2):
        parts = [
            widened(q_t[(group * groups + h) * HD : (group * groups + h + 1) * HD], group)
            for h in range(groups)
        ]
        scores = dot_nn(k_ref[...], jnp.concatenate(parts, 1))
        weights = []
        for h in range(groups):
            s = scores[:, h * rows : (h + 1) * rows] + bias_ref[...]
            top = jnp.max(s, 0, keepdims=True)
            w = jnp.exp(s - top)
            totals.append(jnp.sum(w, 0, keepdims=True))
            maxes.append(top)
            weights.append(low(w))
        mixed = dot_nn(v_t, jnp.concatenate(weights, 1))
        for h in range(groups):
            part = mixed[group * HD : (group + 1) * HD, h * rows : (h + 1) * rows]
            outs.append(part / totals[group * groups + h])
    attn = jnp.transpose(jnp.concatenate(outs, 0))
    out_ref[...] = attn
    heads = 2 * groups * HD
    low_ref[:, pl.ds(pl.multiple_of(step * heads, 2 * HD), heads)] = low(attn)
    pad = [jnp.ones((8 - 2 * groups, rows), F32)] if 2 * groups < 8 else []
    max_ref[0] = jnp.concatenate(maxes + pad, 0)
    total_ref[0] = jnp.concatenate(totals + pad, 0)

    @pl.when(step == pl.num_programs(0) - 1)
    def _():
        load.wait()
        resid = up(tok_ref[...]) + dot_nn(low_ref[...], wo_ref[...])
        resid_ref[...] = resid
        inv = lax.rsqrt(jnp.mean(resid * resid, -1, keepdims=True) + NORM_EPS)
        hn = low(resid * inv * gains_ref[1:2, :])
        hn_ref[:, :width] = hn
        named = up(named_ref[...]) > 0.5
        logits = jnp.where(named, dot_nn(hn, router_ref[...]), MASK_FLOOR)
        gates = jnp.where(named, jnp.exp(logits - jnp.max(logits, -1, keepdims=True)), 0.0)
        gates = gates / jnp.sum(gates, -1, keepdims=True)
        gates_ref[...] = gates
        high = up(low(gates))
        hn_ref[:, width:] = low(high + pltpu.roll(gates - high, SIDE // 2, 1))


def attend(place, queries, keyval, tokens, gains, router, named, wo, groups):
    rows, heads_all = queries.shape
    width = tokens.shape[1]
    keys, kv = keyval.shape
    steps = kv // 2 // (2 * HD)
    heads = 2 * groups * HD

    def same(*shape):
        return pl.BlockSpec(shape, lambda i, s: (0,) * len(shape))

    return pl.pallas_call(
        functools.partial(attend_kernel, groups),
        grid_spec=pltpu.PrefetchScalarGridSpec(
            num_scalar_prefetch=1,
            grid=(steps,),
            in_specs=[
                pl.BlockSpec((rows, heads), lambda i, s: (0, i)),
                pl.BlockSpec((keys, 2 * HD), lambda i, s: (0, i)),
                pl.BlockSpec((keys, 2 * HD), lambda i, s: (0, steps + i)),
                same(rows, width),
                same(8, width),
                same(width, SIDE),
                same(rows, SIDE),
                pl.BlockSpec(memory_space=pl.ANY),
            ],
            out_specs=[
                pl.BlockSpec((rows, heads), lambda i, s: (0, i)),
                pl.BlockSpec((1, 8, rows), lambda i, s: (i, 0, 0)),
                pl.BlockSpec((1, 8, rows), lambda i, s: (i, 0, 0)),
                same(rows, width),
                same(rows, width + SIDE),
                same(rows, heads_all),
                same(rows, SIDE),
            ],
            scratch_shapes=[
                pltpu.VMEM((keys, rows), F32),
                pltpu.VMEM((heads_all, width), BF16),
                pltpu.SemaphoreType.DMA,
            ],
        ),
        out_shape=[
            pltpu.HBM((rows, heads_all), F32),
            jax.ShapeDtypeStruct((steps, 8, rows), F32),
            jax.ShapeDtypeStruct((steps, 8, rows), F32),
            pltpu.HBM((rows, width), F32),
            jax.ShapeDtypeStruct((rows, width + SIDE), BF16),
            pltpu.HBM((rows, heads_all), BF16),
            jax.ShapeDtypeStruct((rows, SIDE), F32),
        ],
        compiler_params=params(40),
        cost_estimate=cost(50 * rows * keys * heads_all),
        name="attend",
    )(place, *hbm(queries, keyval, keyval, tokens), gains, router, named, *hbm(wo))


def attend_back_kernel(
    groups,
    place_ref,
    q_ref,
    k_ref,
    v_ref,
    grad_ref,
    out_ref,
    max_ref,
    total_ref,
    cos_ref,
    sin_ref,
    hn_ref,
    gq_ref,
    gk_ref,
    gv_ref,
    part_ref,
    bias_ref,
    held_ref,
    hn_t_ref,
    sems,
):
    rows = q_ref.shape[0]
    keys = k_ref.shape[0]
    chunk = 256

    @pl.when(pl.program_id(0) == 0)
    def _():
        bias_ref[...] = key_bias(place_ref, keys, rows)
        for start in range(0, keys, rows):
            hn_t_ref[:, start : start + rows] = low(transposed(hn_ref[start : start + rows, :]))

    q_t = low(transposed(q_ref[...]))
    k_t = low(transposed(k_ref[...]))
    grad_t = transposed(grad_ref[...])
    out_t = transposed(out_ref[...])
    q_parts, g_parts, deltas, tops, grads = [], [], [], [], []
    for group in range(2):
        q_part, g_part, delta = [], [], []
        for h in range(groups):
            n = group * groups + h
            total = total_ref[0, n : n + 1]
            grad = grad_t[n * HD : (n + 1) * HD]
            q_part.append(widened(q_t[n * HD : (n + 1) * HD], group))
            g_part.append(widened(low(grad / total), group))
            delta.append(jnp.sum(out_t[n * HD : (n + 1) * HD] * grad, 0, keepdims=True) / total)
        q_parts.append(jnp.concatenate(q_part, 1))
        g_parts.append(jnp.concatenate(g_part, 1))
        deltas.append(jnp.concatenate(delta, 1))
        tops.append(
            jnp.concatenate(
                [max_ref[0, group * groups + h : group * groups + h + 1] for h in range(groups)], 1
            )
        )
        grads.append(jnp.zeros((2 * HD, groups * rows), F32))
    for start in range(0, keys, chunk):
        bias = bias_ref[start : start + chunk]
        bias = jnp.concatenate([bias] * groups, 1)
        grad_k = jnp.zeros((chunk, 2 * HD), F32)
        grad_v = jnp.zeros((chunk, 2 * HD), F32)
        for group in range(2):
            scores = dot_nn(k_ref[start : start + chunk], q_parts[group])
            w = jnp.exp(scores + bias - tops[group])
            gp = dot_nn(v_ref[start : start + chunk], g_parts[group])
            gs = low(w * (gp - deltas[group]))
            grad_v = grad_v + dot_nt(low(w), g_parts[group])
            grad_k = grad_k + dot_nt(gs, q_parts[group])
            grads[group] = grads[group] + dot_nn(k_t[:, start : start + chunk], gs)
        at = slice(start, start + chunk)
        gk_ref[at] = low(turn(grad_k, cos_ref[at, :], -sin_ref[at, :]))
        gv_ref[at] = low(grad_v)
    step, slot = pl.program_id(0), lax.rem(pl.program_id(0), 2)
    steps = part_ref.shape[1] // held_ref.shape[2]
    heads, two = 2 * groups * HD, 2 * HD

    def copies(n, slot):
        spans = ((0, heads), (steps * heads, two), (steps * (heads + two), two))
        out, col = [], 0
        for i, (first, size) in enumerate(spans):
            dst = pl.ds(pl.multiple_of(first + n * size, two), size)
            src = held_ref.at[slot, :, col : col + size]
            out.append(pltpu.make_async_copy(src, part_ref.at[:, dst], sems.at[slot, i]))
            col += size
        return out

    @pl.when(step >= 2)
    def _():
        for copy in copies(step - 2, slot):
            copy.wait()

    both = jnp.concatenate([gk_ref[...], gv_ref[...]], 1)
    held_ref[slot, :, heads:] = low(dot_nn(hn_t_ref[...], both))
    parts = []
    for group in range(2):
        for h in range(groups):
            parts.append(grads[group][group * HD : (group + 1) * HD, h * rows : (h + 1) * rows])
    grad_q = jnp.transpose(jnp.concatenate(parts, 0)) * (HD ** (-0.5))
    for d in range(0, 2 * groups * HD, 2 * HD):
        gq_ref[:, d : d + 2 * HD] = low(
            turn(grad_q[:, d : d + 2 * HD], cos_ref[:rows, :], -sin_ref[:rows, :])
        )
    held_ref[slot, :, :heads] = low(dot_nn(hn_t_ref[:, :rows], gq_ref[...]))
    for copy in copies(step, slot):
        copy.start()

    @pl.when(step == steps - 1)
    def _():
        for copy in copies(step, slot):
            copy.wait()

    @pl.when((step == steps - 1) & (step >= 1))
    def _():
        for copy in copies(step - 1, 1 - slot):
            copy.wait()


def attend_back(place, queries, keyval, grad_heads, attn, tops, totals, cosine, sine, hn, groups):
    rows, width = queries.shape
    keys, kv = keyval.shape
    steps = kv // 2 // (2 * HD)
    heads = 2 * groups * HD
    model = hn.shape[1]
    head_spec = pl.BlockSpec((rows, heads), lambda i, s: (0, i))
    key_spec = pl.BlockSpec((keys, 2 * HD), lambda i, s: (0, i))
    stat_spec = pl.BlockSpec((1, 8, rows), lambda i, s: (i, 0, 0))
    return pl.pallas_call(
        functools.partial(attend_back_kernel, groups),
        grid_spec=pltpu.PrefetchScalarGridSpec(
            num_scalar_prefetch=1,
            grid=(steps,),
            in_specs=[
                head_spec,
                key_spec,
                pl.BlockSpec((keys, 2 * HD), lambda i, s: (0, steps + i)),
                head_spec,
                head_spec,
                stat_spec,
                stat_spec,
                pl.BlockSpec((keys, 2 * HD), lambda i, s: (0, 0)),
                pl.BlockSpec((keys, 2 * HD), lambda i, s: (0, 0)),
                pl.BlockSpec((keys, model), lambda i, s: (0, 0)),
            ],
            out_specs=[
                head_spec,
                key_spec,
                key_spec,
                pl.BlockSpec(memory_space=pl.ANY),
            ],
            scratch_shapes=[
                pltpu.VMEM((keys, rows), F32),
                pltpu.VMEM((2, model, heads + 4 * HD), BF16),
                pltpu.VMEM((model, keys), BF16),
                pltpu.SemaphoreType.DMA((2, 3)),
            ],
        ),
        out_shape=[
            jax.ShapeDtypeStruct((rows, width), BF16),
            jax.ShapeDtypeStruct((keys, kv // 2), BF16),
            jax.ShapeDtypeStruct((keys, kv // 2), BF16),
            pltpu.HBM((model, width + kv), BF16),
        ],
        compiler_params=params(44),
        cost_estimate=cost(64 * rows * keys * width),
        name="attend_back",
    )(place, *hbm(queries, keyval, keyval, grad_heads, attn, tops, totals, cosine, sine, hn))


def slot_pick(slot, cap):
    place = lax.broadcasted_iota(jnp.int32, (cap, slot.shape[1]), 0).astype(F32)
    return place == slot


def weight_chunks(grads, x_ref, c_ref, ggu_ref, act_ref):
    hidden, width = act_ref.shape[1], c_ref.shape[1]
    size, wide = grads[0].shape
    rest = width - wide
    half = hidden // 2
    for h in range(2):
        at = slice(h * half, (h + 1) * half)
        part = low(dot_tn(act_ref[:, at], c_ref[...]))
        grads[0][at, :] = part[:, :wide]
        grads[0][hidden:, h * rest : (h + 1) * rest] = part[:, wide:]
    step = size // 2
    for c, ref in enumerate(grads[1:]):
        for h in range(2):
            cols = slice(c * size + h * step, c * size + (h + 1) * step)
            ref[h * step : (h + 1) * step, :] = low(dot_tn(x_ref[:, cols], ggu_ref[...]))


def expert_kernel(counts, cap, tile, e, earlier, last, number_ref, *refs):
    parts, refs = refs[: sum(counts)], refs[sum(counts) :]
    cot_ref, wgu_all_ref, wd_all_ref = refs[:3]
    gin_before, refs = refs[3 : 3 + earlier], refs[3 + earlier :]
    out_ref, slots_ref, result_ref = refs[:3]
    grads = refs[3:6]
    x_ref, c_ref, ggu_ref, act_ref, sg_ref, wgu_ref, wd_ref, sems = refs[6:14]
    if last:
        gin_ref, load_ref, store_ref = refs[14:]
    else:
        gin_ref = result_ref
    loads = [
        pltpu.make_async_copy(wgu_all_ref.at[e], wgu_ref, sems.at[0]),
        pltpu.make_async_copy(wd_all_ref.at[e], wd_ref, sems.at[1]),
    ]
    for load in loads:
        load.start()
    blocks = len(counts)
    hidden, width = wd_ref.shape
    rows = cot_ref.shape[0] // blocks
    total = blocks * cap
    index, expert = number_ref[0], number_ref[1]
    lane = lax.broadcasted_iota(jnp.int32, (8, SIDE), 1)
    pick_slot = low(jnp.where(lane == expert, 1.0, 0.0))
    pick_gate = low(jnp.where((lane == expert) | (lane == expert + SIDE // 2), 1.0, 0.0))
    n = 0
    for b in range(blocks):
        hn = parts[n : n + counts[b]]
        n += counts[b]
        src = pl.ds(pl.multiple_of((index ^ b) * rows, rows), rows)
        slot = dot_nt(pick_slot, cot_ref[src, width:])[:1] - 1.0
        gate = [dot_nt(pick_gate, part[:, width:]) for part in hn]
        gate = (jnp.concatenate(gate, 1) if len(gate) > 1 else gate[0])[:1]
        slots_ref[b : b + 1, :] = slot
        hit = slot_pick(slot, cap)
        pick = low(jnp.where(hit, 1.0, 0.0))
        at = slice(b * cap, (b + 1) * cap)
        taken, start = None, 0
        for part in hn:
            piece = dot_nn(pick[:, start : start + part.shape[0]], part[:, :width])
            taken = piece if taken is None else taken + piece
            start += part.shape[0]
        x_ref[at, :] = low(taken)
        c_ref[at, :] = low(dot_nn(pick, cot_ref[src, :width]))
        gate = jnp.sum(jnp.where(hit, gate, 0.0), 1, keepdims=True)
        sg_ref[at, :] = jnp.broadcast_to(gate, (cap, 128))

    def middle(t, carry):
        at = pl.ds(pl.multiple_of(t * tile, 16), tile)
        gate_up = dot_nn(x_ref[at, :], wgu_ref[...])
        g = gate_up[:, :hidden]
        u = gate_up[:, hidden:]
        sigma = jax.nn.sigmoid(g)
        silu = g * sigma
        act = low(silu * u)
        slot_gate = sg_ref[at, :][:, :1]
        back = dot_nt(c_ref[at, :], wd_ref[...])
        gate_grad = jnp.sum(up(act) * back, 1, keepdims=True)
        back = back * slot_gate
        act_ref[at, :] = low(up(act) * slot_gate)
        ggu_ref[at, :hidden] = low(back * u * (sigma * (1.0 + g * (1.0 - sigma))))
        ggu_ref[at, hidden:] = low(back * silu)
        out_ref[at, :] = low(dot_nn(act, wd_ref[...]) * slot_gate)
        gin_ref[at, :width] = low(dot_nt(ggu_ref[at, :], wgu_ref[...]))
        lane = lax.broadcasted_iota(jnp.int32, (tile, SIDE), 1)
        high = up(low(gate_grad))
        side = jnp.where(lane == expert, high, 0.0)
        side = jnp.where(lane == expert + SIDE // 2, gate_grad - high, side)
        gin_ref[at, width:] = low(side)
        return carry

    for load in loads:
        load.wait()
    lax.fori_loop(0, total // tile, middle, 0)
    if not last:
        weight_chunks(grads, x_ref, c_ref, ggu_ref, act_ref)
        return

    def load_before(b):
        return [
            pltpu.make_async_copy(
                ref.at[b * cap : (b + 1) * cap], load_ref.at[b % 2, i], sems.at[2 + 2 * i + b % 2]
            )
            for i, ref in enumerate(gin_before)
        ]

    def store(b):
        dst = pl.ds(pl.multiple_of((index ^ b) * rows, rows), rows)
        return pltpu.make_async_copy(
            store_ref.at[b % 2], result_ref.at[dst], sems.at[2 + 2 * earlier + b % 2]
        )

    for load in load_before(0):
        load.start()
    for b in range(blocks):
        if b + 1 < blocks:
            for load in load_before(b + 1):
                load.start()
        src = pl.ds(pl.multiple_of((index ^ b) * rows, rows), rows)
        order = up(cot_ref[src, width:])
        lane = lax.broadcasted_iota(jnp.int32, order.shape, 1)
        place = lax.broadcasted_iota(jnp.int32, (rows, cap), 1).astype(F32)

        def pick(number):
            slot = jnp.sum(jnp.where(lane == number, order, 0.0), 1, keepdims=True) - 1.0
            return low(jnp.where(place == slot, 1.0, 0.0))

        acc = dot_nn(pick(expert), gin_ref[b * cap : (b + 1) * cap, :])
        for i, load in enumerate(load_before(b)):
            load.wait()
            acc = acc + dot_nn(pick(expert - earlier + i), load_ref[b % 2, i])
        if b >= 2:
            store(b - 2).wait()
        store_ref[b % 2] = low(acc)
        store(b).start()
    weight_chunks(grads, x_ref, c_ref, ggu_ref, act_ref)
    for b in range(max(blocks - 2, 0), blocks):
        store(b).wait()


def unpack_down(chunk, hidden):
    rest = chunk.shape[1] // 2
    right = jnp.concatenate([chunk[hidden:, :rest], chunk[hidden:, rest:]], 0)
    return jnp.concatenate([chunk[:hidden], right], 1)


def run_expert(number, pieces, cot, w_gate_up, w_down, e, cap, gins):
    counts = [len(p) for p in pieces]
    flat = [h for p in pieces for h in p]
    blocks = len(counts)
    rows = cot.shape[0] // blocks
    hidden, width = w_down.shape[1:]
    total = blocks * cap
    tile = max(t for t in range(16, 401, 16) if total % t == 0)
    last = e + 1 == w_down.shape[0]
    earlier = len(gins) if last else 0
    anywhere = pl.BlockSpec(memory_space=pl.ANY)
    chunk = jax.ShapeDtypeStruct((width // 2, 2 * hidden), BF16)
    work = [(total, width), (total, width), (total, 2 * hidden), (total, hidden)]
    gin_shape = (total, width + SIDE)
    scratch = [pltpu.VMEM(shape, BF16) for shape in work] + [
        pltpu.VMEM((total, 128), F32),
        pltpu.VMEM((width, 2 * hidden), BF16),
        pltpu.VMEM((hidden, width), BF16),
        pltpu.SemaphoreType.DMA((4 + 2 * earlier,)),
    ]
    if last:
        scratch += [
            pltpu.VMEM(gin_shape, BF16),
            pltpu.VMEM((2, max(earlier, 1), cap, width + SIDE), BF16),
            pltpu.VMEM((2, rows, width + SIDE), BF16),
        ]
    result = pltpu.HBM((blocks * rows, width + SIDE) if last else gin_shape, BF16)
    got = pl.pallas_call(
        functools.partial(expert_kernel, counts, cap, tile, e, earlier, last),
        in_specs=[pl.BlockSpec(memory_space=pltpu.SMEM)]
        + [WHOLE] * (len(flat) + 1)
        + [anywhere] * (2 + earlier),
        out_specs=[WHOLE, WHOLE, anywhere if last else WHOLE] + [WHOLE] * 3,
        out_shape=[
            pltpu.HBM((total, width), BF16),
            jax.ShapeDtypeStruct((blocks, rows), F32),
            result,
        ]
        + [chunk] * 3,
        scratch_shapes=scratch,
        compiler_params=params(56),
        cost_estimate=cost(44 * total * width * hidden),
        name="expert",
    )(number, *flat, cot, w_gate_up, w_down, *gins[:earlier])
    return got[0], got[1], got[2], got[3:]


def combine_kernel(count, cap, first, stride, number_ref, *refs):
    slots, parts, out_ref = refs[:count], refs[count : 2 * count], refs[2 * count]
    b = pl.program_id(0) * stride + first
    rows = slots[0].shape[1]
    place = lax.broadcasted_iota(jnp.int32, (cap, rows), 0).astype(F32)
    acc = None
    for e in range(count):
        pick = low(jnp.where(place == slots[e][pl.ds(b, 1), :], 1.0, 0.0))
        part = dot_tn(pick, parts[e][...])
        acc = part if acc is None else acc + part
    out_ref[...] = low(acc)


def combine(number, slots, parts, cap, chosen, order):
    blocks, rows = slots[0].shape
    count = len(parts)
    width = parts[0].shape[1]
    first, stride = chosen.start, chosen.step
    return pl.pallas_call(
        functools.partial(combine_kernel, count, cap, first, stride),
        grid_spec=pltpu.PrefetchScalarGridSpec(
            num_scalar_prefetch=1,
            grid=(len(chosen),),
            in_specs=[pl.BlockSpec((blocks, rows), lambda n, s: (0, 0))] * count
            + [pl.BlockSpec((cap, width), lambda n, s: (n * stride + first, 0))] * count,
            out_specs=pl.BlockSpec((rows, width), lambda n, s: (order(n, s[0]), 0)),
        ),
        out_shape=pltpu.HBM((len(chosen) * rows, width), BF16),
        compiler_params=params(20),
        cost_estimate=cost(10 * len(chosen) * cap * rows * width),
        name="combine",
    )(number, *slots, *parts)


def rope_tables(places):
    half = HD // 2
    frequency = ROPE_BASE ** (-jnp.arange(half, dtype=F32) * 2.0 / HD)
    angles = places.astype(F32)[:, None] * frequency[None, :]
    cosine, sine = jnp.cos(angles), jnp.sin(angles)
    return jnp.concatenate([cosine] * 4, 1), jnp.concatenate([-sine, sine] * 2, 1)


def per_device(
    tokens,
    lengths,
    routes,
    cotangent,
    gain_attn,
    gain_moe,
    w_query,
    w_keyval,
    w_output,
    w_router,
    w_gate_up,
    w_down,
):
    rows = tokens.shape[1]
    width = tokens.shape[2]
    experts = w_router.shape[1]
    local_experts = w_gate_up.shape[0]
    kv_width = w_keyval.shape[1] // 2
    head_total = w_query.shape[1]
    groups = head_total // kv_width
    dp_count = lax.axis_size("dp")
    ctx_count = lax.axis_size("ctx")
    dp_index = lax.axis_index("dp").astype(jnp.int32)
    ctx_index = lax.axis_index("ctx").astype(jnp.int32)
    cap = -(-(rows * 9 // 16) // 16) * 16
    length = lengths[0]
    places = ctx_index * rows + jnp.arange(rows, dtype=jnp.int32)
    valid = (places < length)[:, None]
    index = jnp.reshape(dp_index, (1,))

    pad = jnp.zeros((w_router.shape[0], 128 - experts - 2), BF16)
    first_w = Gather(
        jnp.concatenate(
            [w_query, w_keyval, w_router, gain_attn[:, None], gain_moe[:, None], pad], 1
        )
    )

    named = jnp.any(routes[0][..., None] == jnp.arange(SIDE, dtype=jnp.int32), 1).astype(BF16)
    order = dot_nn(jnp.tril(jnp.ones((rows, rows), BF16)), named) * up(named)
    grad_y = jnp.where(valid, cotangent[0], BF16(0))
    cot = jnp.concatenate([grad_y, low(order)], 1)

    seq = [halves(tokens[0])]
    back = jnp.arange(ctx_count, dtype=jnp.int32)[:, None] * rows
    tables = rope_tables((places[None, :] - back).reshape(-1))

    def next_block(part):
        return shift(seq[-1][part], 1)

    first_w.near()
    seq.append([next_block(0), next_block(1)])
    early = next_block(0)
    output_w = lax.all_gather(w_output, "dp", axis=0, tiled=True)
    _, tables, cot, seq[1], early = sync(first_w, tables, cot, seq[1], early)
    cot_all = lax.all_gather(cot, "dp", axis=0, tiled=True)
    first_w.far()
    seq.append([early, next_block(1)])
    early = next_block(0)
    _, seq[2], early = sync(first_w, seq[2], early)
    seq.append([early, next_block(1)])
    for _ in range(ctx_count - 4):
        seq.append([next_block(0), next_block(1)])
    cosine, sine = tables
    projected = project(index, first_w.pieces(), seq, cosine, sine, experts, head_total)
    queries, keyval, hn_seq, query_w, keyval_w, router_w, gains = projected
    keyval, hn_seq = project_last(seq[-1], gains, keyval_w, cosine, sine, keyval, hn_seq)

    place = jnp.stack([ctx_index, length])
    attn, tops, totals, resid, hn_two, attn_low, gates = attend(
        place, queries, keyval, tokens[0], gains, router_w, named, output_w, groups
    )

    hn_g = Gather(hn_two)
    hn_g.near()
    sync(hn_g)
    hn_pieces = hn_g.pieces()
    sums = LineSums()
    outs, gins, slots = [], [], []
    for e in range(local_experts):
        number = jnp.stack([dp_index, dp_index * local_experts + e])
        out, slot, gin, grads = run_expert(
            number, hn_pieces, cot_all, w_gate_up, w_down, e, cap, gins
        )
        outs.append(out)
        gins.append(gin)
        slots.append(slot)
        if e + 1 < local_experts:
            for c, v in enumerate(grads):
                sums.add(f"{e}.{c}", v)
            hn_pieces, cot_all = sums.step(hn_pieces, cot_all)
    for c, v in enumerate(grads):
        sums.add(f"{local_experts - 1}.{c}", v)
    (gin_tokens,) = sums.step(gins[-1])
    gin_sum = lax.psum_scatter(gin_tokens, "dp", scatter_dimension=0, tiled=True)
    outs, slots = sums.step(outs, slots)
    out_tokens = combine(index, slots, outs, cap, range(0, dp_count, 1), lambda n, i: n ^ i)

    backed = router_back(gin_sum, gates, router_w, gains, resid, grad_y, output_w, experts)
    *backed, out_tokens = sums.step(*sums.hold(*backed, out_tokens))
    grad_resid, grad_heads, *for_output = backed

    backed = attend_back(
        place, queries, keyval, grad_heads, attn, tops, totals, cosine, sine, hn_seq, groups
    )
    backed = sums.step(*backed, *for_output)
    grad_query, grad_keys, grad_values, part_first, grad_attn, grad_logits, gain_two = backed
    share_first = lax.psum_scatter(part_first, "dp", scatter_dimension=0, tiled=True)
    part_output = output_grad(attn_low, grad_attn, hn_two, grad_logits, gain_two, experts)
    (part_output,) = sums.step(part_output)
    share_output = lax.psum_scatter(part_output, "dp", scatter_dimension=0, tiled=True)
    share_query, share_keyval = share_first[:, :head_total], share_first[:, head_total:]
    gain_grad = jnp.sum(up(share_query) * up(w_query), 1, keepdims=True) + jnp.sum(
        up(share_keyval) * up(w_keyval), 1, keepdims=True
    )
    gain_grad = jnp.broadcast_to(gain_grad / up(gain_attn)[:, None], (w_query.shape[0], SIDE))
    share_keyval = jnp.concatenate([share_keyval, low(gain_grad)], 1)
    sums.step()
    sums.launch("query", share_query)
    sums.launch("keyval", share_keyval)
    gate_up, down = jnp.zeros(w_gate_up.shape, F32), jnp.zeros(w_down.shape, F32)
    placed = set()

    def place_done(gate_up, down):
        for e in range(local_experts):
            for c in range(3):
                if f"{e}.{c}" not in sums.done or f"{e}.{c}" in placed:
                    continue
                placed.add(f"{e}.{c}")
                part = sums.total(f"{e}.{c}")
                if c == 0:
                    part = unpack_down(part, w_down.shape[1])
                    down = lax.dynamic_update_slice(down, part[None], (e, 0, 0))
                else:
                    at = (e, (c - 1) * part.shape[0], 0)
                    gate_up = lax.dynamic_update_slice(gate_up, part[None], at)
        return gate_up, down

    grad_kv = jnp.concatenate([grad_keys, grad_values], 1)
    blocks = [grad_kv[r * rows : (r + 1) * rows] for r in range(ctx_count)]
    held = blocks[-1]
    for r in range(ctx_count - 2, -1, -1):
        pairs = [(i, i - 1) for i in range(r + 1, ctx_count)]
        held = add_low(lax.ppermute(held, "ctx", pairs), blocks[r])
        if r == max(ctx_count - 2, 1):
            held, out_tokens = sums.step(held, out_tokens)
            moe = lax.psum_scatter(out_tokens, "dp", scatter_dimension=0, tiled=True)
            sums.add("output", share_output)
        elif r:
            (held,) = sums.step(held)

    grad_hn_one = dot_nt(grad_query, query_w) + dot_nt(held, keyval_w)
    inputs = up(tokens[0])
    inv_one = lax.rsqrt(jnp.mean(inputs * inputs, -1, keepdims=True) + NORM_EPS)
    normed_one = inputs * inv_one
    scaled_one = grad_hn_one * gains[0:1]
    grad_inputs = grad_resid + inv_one * (
        scaled_one - normed_one * jnp.mean(scaled_one * normed_one, -1, keepdims=True)
    )
    grad_inputs = low(grad_inputs)

    outcome = low(jnp.where(valid, resid + up(moe), 0.0))

    wanted = [f"{e}.{c}" for e in range(local_experts) for c in range(3)]
    while not all(name in sums.done for name in wanted):
        sums.step()
    gate_up, down = place_done(gate_up, down)
    while not ("query" in sums.done and "keyval" in sums.done):
        sums.step()
    total_query, total_keyval = sums.total("query"), sums.total("keyval")
    ready = (total_query, total_keyval[:, : 2 * kv_width], total_keyval[:, 2 * kv_width])
    ready = sums.step(*ready, outcome, gate_up, down, grad_inputs)
    total_query, total_keyval, total_gain, outcome, gate_up, down, grad_inputs = ready
    while sums.busy():
        sums.step()
    total_output = sums.total("output")
    return (
        outcome[None],
        grad_inputs[None],
        total_gain,
        total_output[:, width + experts],
        total_query,
        total_keyval,
        total_output[:, :width],
        total_output[:, width : width + experts],
        gate_up,
        down,
    )


def solution(mesh):
    in_specs = (
        P("dp", "ctx", None),
        P("dp"),
        P("dp", "ctx", None),
        P("dp", "ctx", None),
        P("dp"),
        P("dp"),
        P("dp", None),
        P("dp", None),
        P("dp", None),
        P("dp", None),
        P("dp", None, None),
        P("dp", None, None),
    )
    out_specs = (
        P("dp", "ctx", None),
        P("dp", "ctx", None),
        P("dp"),
        P("dp"),
        P("dp", None),
        P("dp", None),
        P("dp", None),
        P("dp", None),
        P("dp", None, None),
        P("dp", None, None),
    )
    return jax.shard_map(
        per_device, mesh=mesh, in_specs=in_specs, out_specs=out_specs, check_vma=False
    )
```

```python
import functools

import jax
import jax.numpy as jnp
from jax import lax
from jax.experimental import pallas as pl
from jax.experimental.pallas import tpu as pltpu
from jax.sharding import PartitionSpec as P

HD = 64
NORM_EPS = 1e-06
ROPE_BASE = 10000.0
MASK_FLOOR = -1e30
F32 = jnp.float32
BF16 = jnp.bfloat16
MIB = 1024 * 1024
SIDE = 128
WHOLE = pl.BlockSpec()


def params(mib):
    return pltpu.CompilerParams(vmem_limit_bytes=mib * MIB)


def hbm(*arrays_in):
    return [pltpu.with_memory_space_constraint(v, pltpu.HBM) for v in arrays_in]


def cost(flops):
    return pl.CostEstimate(flops=int(flops) // 64, bytes_accessed=1024, transcendentals=0)


def up(v):
    return v.astype(F32)


def low(v):
    return v.astype(BF16)


def dot_nn(a, b):
    return lax.dot_general(a, b, (((1,), (0,)), ((), ())), preferred_element_type=F32)


def dot_nt(a, b):
    return lax.dot_general(a, b, (((1,), (1,)), ((), ())), preferred_element_type=F32)


def dot_tn(a, b):
    return lax.dot_general(a, b, (((0,), (0,)), ((), ())), preferred_element_type=F32)


def swap(v, mask):
    count = lax.axis_size("dp")
    return lax.ppermute(v, "dp", [(i, i ^ mask) for i in range(count)])


def halves(v):
    mid = v.shape[0] // 2
    return [v[:mid], v[mid:]]


class Gather:
    def __init__(self, v):
        self.special = lax.axis_size("dp") == 8
        self.stage = 0
        self.live = [v]

    def near(self):
        if self.special and self.stage == 0:
            v = self.live[0]
            self.live = [v, swap(v, 2), swap(v, 4)]
        self.stage = max(self.stage, 1)

    def far(self):
        self.near()
        if self.special and self.stage == 1:
            v, along_x, along_y = self.live
            self.live = self.live + [swap(halves(along_x)[0], 4), swap(halves(along_y)[1], 2)]
        self.stage = max(self.stage, 2)

    def pieces(self):
        self.far()
        if not self.special:
            out = [[self.live[0]]]
            bit = 1
            while bit < lax.axis_size("dp"):
                out = out + [[swap(h, bit) for h in piece] for piece in out]
                bit *= 2
            return out
        v, along_x, along_y, far_a, far_b = self.live
        even = [[v], [along_x], [along_y], [far_a, far_b]]
        out = []
        for piece in even:
            out += [piece, [swap(h, 1) for h in piece]]
        return out


def sync(*items):
    plain = [i.live if isinstance(i, Gather) else i for i in items]
    plain = lax.optimization_barrier(plain)
    for item, got in zip(items, plain):
        if isinstance(item, Gather):
            item.live = list(got)
    return plain


def add_low(a, b):
    return low(up(a) + up(b))


def shift(v, step):
    count = lax.axis_size("ctx")
    return lax.ppermute(
        v, "ctx", [(i, i + step) for i in range(count) if 0 <= i + step < count]
    )


class LineSums:
    DEPTH = 1

    def __init__(self):
        count = lax.axis_size("ctx")
        index = lax.axis_index("ctx")
        self.plain = count != 4
        self.outer = (index == 0) | (index == count - 1)
        self.waiting = []
        self.flights = [[] for _ in range(self.DEPTH)]
        self.done = {}

    def add(self, name, v):
        if self.plain:
            self.done[name] = lax.psum(v, "ctx")
        else:
            self.waiting.append((name, v))

    def busy(self):
        return bool(self.waiting or any(self.flights))

    def step(self, *critical, take=1, flush=False):
        if self.plain:
            return critical
        got = self.flights.pop(0)
        while flush and self.flights:
            got = got + self.flights.pop(0)
        ready = {"first": [], "inner": [], "last": []}
        for kind, name, v, arrived in got:
            if kind == "first":
                ready["inner"].append((name, add_low(v, arrived)))
            elif kind == "inner":
                ready["last"].append((name, add_low(v, arrived)))
            else:
                self.done[name] = (v, arrived)
        for _ in range(take):
            if self.waiting:
                ready["first"].append(self.waiting.pop(0))
        shared = []
        for first in list(ready["first"]):
            for last in list(ready["last"]):
                if first[1].shape == last[1].shape:
                    shared.append((first[0], last[0], first[1], jnp.where(self.outer, first[1], last[1])))
                    ready["first"] = [r for r in ready["first"] if r is not first]
                    ready["last"] = [r for r in ready["last"] if r is not last]
                    break
        both = [(own, payload) for _, _, own, payload in shared]
        alone = {kind: [v for _, v in entries] for kind, entries in ready.items()}
        held = lax.optimization_barrier((both, alone, self.done, critical))
        both, alone, self.done, critical = held
        flight = []
        for (first, last, _, _), (own, payload) in zip(shared, both):
            back = lax.ppermute(payload, "ctx", [(0, 1), (1, 0), (2, 3), (3, 2)])
            flight.append(("first", first, own, back))
            flight.append(("last", last, payload, back))
        routes = {
            "first": [(0, 1), (3, 2)],
            "inner": [(1, 2), (2, 1)],
            "last": [(1, 0), (2, 3)],
        }
        for kind, pairs in routes.items():
            for (name, _), v in zip(ready[kind], alone[kind]):
                flight.append((kind, name, v, lax.ppermute(v, "ctx", pairs)))
        self.flights.append(flight)
        return critical

    def launch(self, name, v):
        if self.plain:
            self.add(name, v)
        else:
            got = lax.ppermute(v, "ctx", [(0, 1), (3, 2)])
            self.flights[-1].append(("first", name, v, got))

    def hold(self, *critical):
        if self.plain:
            return critical
        own = [[entry[2] for entry in flight] for flight in self.flights]
        own, critical = lax.optimization_barrier((own, critical))
        for n, flight in enumerate(self.flights):
            self.flights[n] = [
                (kind, name, v, arrived)
                for (kind, name, _, arrived), v in zip(flight, own[n])
            ]
        return critical

    def total(self, name):
        if self.plain:
            return up(self.done[name])
        v, arrived = self.done[name]
        return up(jnp.where(self.outer, arrived, v))


def lay_rows(pieces, counts, index, put):
    n = 0
    for k, parts in enumerate(counts):
        rows = sum(pieces[n + i].shape[0] for i in range(parts))
        start = (index ^ k) * rows
        for i in range(parts):
            put(pl.multiple_of(start, 16), pieces[n + i])
            start = start + pieces[n + i].shape[0]
        n += parts


def turn(v, cosine, sine):
    lane = lax.broadcasted_iota(jnp.int32, v.shape, 1)
    first = lax.rem(lane, HD) < HD // 2
    partner = jnp.where(
        first, pltpu.roll(v, 2 * HD - HD // 2, 1), pltpu.roll(v, HD // 2, 1)
    )
    return v * cosine + partner * sine


def normed_rows(parts, gain):
    x = jnp.concatenate([up(p[...]) for p in parts], 0)
    return low(x * lax.rsqrt(jnp.mean(x * x, -1, keepdims=True) + NORM_EPS) * gain)


def key_rows(hn, wkv_ref, cosine, sine):
    raw = dot_nn(hn, wkv_ref[...])
    two = 2 * HD
    keys = raw.shape[1] // 2
    turned = [turn(raw[:, d : d + two], cosine, sine) for d in range(0, keys, two)]
    return low(jnp.concatenate(turned + [raw[:, keys:]], 1))


def project_kernel(counts, blocks, experts, index_ref, *refs):
    pieces = refs[: sum(counts)]
    seq = refs[sum(counts) : sum(counts) + 2 * blocks]
    cos_ref, sin_ref = refs[sum(counts) + 2 * blocks : sum(counts) + 2 * blocks + 2]
    q_ref, kv_ref, hn_ref, wq_ref, wkv_ref, router_ref, gains_ref, small_ref = refs[
        sum(counts) + 2 * blocks + 2 :
    ]
    q_width, kv_width = wq_ref.shape[1], wkv_ref.shape[1]

    def put(start, ref):
        at = pl.ds(start, ref.shape[0])
        wq_ref[at, :] = ref[:, :q_width]
        wkv_ref[at, :] = ref[:, q_width : q_width + kv_width]
        small_ref[at, :] = ref[:, q_width + kv_width :]

    lay_rows(pieces, counts, index_ref[0], put)
    small = up(small_ref[...])
    lane = lax.broadcasted_iota(jnp.int32, small.shape, 1)
    router_ref[...] = low(jnp.where(lane < experts, small, 0.0))
    gains_ref[...] = jnp.transpose(small)[experts : experts + 8]
    gain = gains_ref[0:1, :]
    rows = 2 * seq[0].shape[0]
    for r in range(blocks):
        at = slice(r * rows, (r + 1) * rows)
        hn = normed_rows(seq[2 * r : 2 * r + 2], gain)
        hn_ref[at, :] = hn
        kv_ref[at, :] = key_rows(hn, wkv_ref, cos_ref[at, :], sin_ref[at, :])
    two = 2 * HD
    for c in range(0, q_width, 2 * two):
        raw = dot_nn(hn_ref[:rows, :], wq_ref[:, c : c + 2 * two])
        for d in (0, two):
            rot = turn(raw[:, d : d + two], cos_ref[:rows, :], sin_ref[:rows, :])
            q_ref[:, c + d : c + d + two] = low(up(low(rot)) * (HD ** (-0.5)))


def project(index, pieces, seq, cosine, sine, experts, q_width):
    counts = [len(p) for p in pieces]
    flat = [h for p in pieces for h in p]
    halves_in = [h for pair in seq[:-1] for h in pair]
    rows, width = 2 * seq[0][0].shape[0], seq[0][0].shape[1]
    kv_width = flat[0].shape[1] - q_width - 128
    keys = rows * len(seq)
    return pl.pallas_call(
        functools.partial(project_kernel, counts, len(seq) - 1, experts),
        in_specs=[pl.BlockSpec(memory_space=pltpu.SMEM)] + [WHOLE] * (len(flat) + len(halves_in) + 2),
        out_specs=[WHOLE] * 7,
        out_shape=[
            jax.ShapeDtypeStruct((rows, q_width), BF16),
            jax.ShapeDtypeStruct((keys, kv_width), BF16),
            jax.ShapeDtypeStruct((keys, width), BF16),
            jax.ShapeDtypeStruct((width, q_width), BF16),
            jax.ShapeDtypeStruct((width, kv_width), BF16),
            jax.ShapeDtypeStruct((width, 128), BF16),
            jax.ShapeDtypeStruct((8, width), F32),
        ],
        scratch_shapes=[pltpu.VMEM((width, 128), BF16)],
        compiler_params=params(40),
        cost_estimate=cost(8 * width * (rows * q_width + keys * kv_width)),
        name="project",
    )(index, *flat, *halves_in, cosine, sine)


def project_last_kernel(
    a_ref, b_ref, gains_ref, wkv_ref, cos_ref, sin_ref, kv_in, hn_in, kv_out, hn_out, kv_ref, hn_ref, sems
):
    rows = kv_ref.shape[0]
    start = kv_out.shape[0] - rows
    hn = normed_rows((a_ref, b_ref), gains_ref[0:1, :])
    hn_ref[...] = hn
    hn_copy = pltpu.make_async_copy(hn_ref, hn_out.at[start : start + rows], sems.at[0])
    hn_copy.start()
    at = slice(start, start + rows)
    kv_ref[...] = key_rows(hn, wkv_ref, cos_ref[at, :], sin_ref[at, :])
    kv_copy = pltpu.make_async_copy(kv_ref, kv_out.at[start : start + rows], sems.at[1])
    kv_copy.start()
    hn_copy.wait()
    kv_copy.wait()


def project_last(last, gains, wkv, cosine, sine, keyval, hn):
    rows = 2 * last[0].shape[0]
    anywhere = pl.BlockSpec(memory_space=pl.ANY)
    return pl.pallas_call(
        project_last_kernel,
        in_specs=[WHOLE] * 6 + [anywhere] * 2,
        out_specs=[anywhere] * 2,
        out_shape=[
            jax.ShapeDtypeStruct(keyval.shape, BF16),
            jax.ShapeDtypeStruct(hn.shape, BF16),
        ],
        scratch_shapes=[
            pltpu.VMEM((rows, keyval.shape[1]), BF16),
            pltpu.VMEM((rows, hn.shape[1]), BF16),
            pltpu.SemaphoreType.DMA((2,)),
        ],
        input_output_aliases={6: 0, 7: 1},
        compiler_params=params(24),
        cost_estimate=cost(8 * rows * keyval.shape[1] * hn.shape[1]),
        name="project_last",
    )(*last, gains, wkv, cosine, sine, *hbm(keyval, hn))


def router_back_kernel(
    experts,
    total_ref,
    gates_ref,
    router_ref,
    gains_ref,
    resid_ref,
    cot_ref,
    wo_ref,
    grad_ref,
    heads_ref,
    attn_ref,
    logits_ref,
    gain_ref,
):
    width = resid_ref.shape[1]
    total = up(total_ref[...])
    side = total[:, width:]
    lane = lax.broadcasted_iota(jnp.int32, side.shape, 1)
    gate_grads = jnp.where(lane < experts, side + pltpu.roll(side, SIDE // 2, 1), 0.0)
    gates = gates_ref[...]
    mean = jnp.sum(gates * gate_grads, -1, keepdims=True)
    grad_logits = low(gates * (gate_grads - mean))
    grad_hn = total[:, :width] + dot_nt(grad_logits, router_ref[...])
    resid = resid_ref[...]
    inv = lax.rsqrt(jnp.mean(resid * resid, -1, keepdims=True) + NORM_EPS)
    normed = resid * inv
    gain = jnp.sum(grad_hn * normed, 0, keepdims=True)
    scaled = grad_hn * gains_ref[1:2, :]
    grad = up(cot_ref[...]) + inv * (scaled - normed * jnp.mean(scaled * normed, -1, keepdims=True))
    grad_ref[...] = grad
    grad_low = low(grad)
    heads_ref[...] = dot_nt(grad_low, wo_ref[...])
    attn_ref[...] = grad_low
    logits_ref[...] = grad_logits
    gain_ref[...] = jnp.broadcast_to(gain, gain_ref.shape)


def output_grad_kernel(
    experts, attn_ref, grad_ref, hn_ref, logits_ref, gain_ref, part_ref, held_ref, sems
):
    width = grad_ref.shape[1]
    copies = []

    def put(cols, value):
        held_ref[:, cols] = low(value)
        copies.append(
            pltpu.make_async_copy(held_ref.at[:, cols], part_ref.at[:, cols], sems.at[len(copies)])
        )
        copies[-1].start()

    small = dot_tn(hn_ref[:, :width], logits_ref[...])
    lane = lax.broadcasted_iota(jnp.int32, small.shape, 1)
    gain = jnp.transpose(jnp.broadcast_to(gain_ref[:1, :], (SIDE, width)))
    put(slice(width, width + SIDE), jnp.where(lane == experts, gain, small))
    attn_t = low(transposed(attn_ref[...]))
    for c in range(0, width, 256):
        put(slice(c, c + 256), dot_nn(attn_t, grad_ref[:, c : c + 256]))
    for copy in copies:
        copy.wait()


def output_grad(attn, grad, hn, logits, gain, experts):
    heads, width = attn.shape[1], grad.shape[1]
    return pl.pallas_call(
        functools.partial(output_grad_kernel, experts),
        in_specs=[WHOLE] * 5,
        out_specs=pl.BlockSpec(memory_space=pl.ANY),
        out_shape=pltpu.HBM((heads, width + SIDE), BF16),
        scratch_shapes=[
            pltpu.VMEM((heads, width + SIDE), BF16),
            pltpu.SemaphoreType.DMA((width // 256 + 1,)),
        ],
        compiler_params=params(28),
        cost_estimate=cost(4 * attn.shape[0] * heads * width),
        name="output_grad",
    )(*hbm(attn, grad, hn, logits, gain))


def router_back(total, gates, router, gains, resid, cot, wo, experts):
    rows, width = resid.shape
    heads = wo.shape[0]
    return pl.pallas_call(
        functools.partial(router_back_kernel, experts),
        in_specs=[WHOLE] * 7,
        out_specs=[WHOLE] * 5,
        out_shape=[
            pltpu.HBM((rows, width), F32),
            pltpu.HBM((rows, heads), F32),
            pltpu.HBM((rows, width), BF16),
            pltpu.HBM((rows, SIDE), BF16),
            pltpu.HBM((8, width), F32),
        ],
        compiler_params=params(30),
        cost_estimate=cost(14 * rows * heads * width),
        name="router_back",
    )(*hbm(total, gates, router), gains, *hbm(resid, cot, wo))


def transposed(v):
    return jnp.transpose(up(v))


def key_bias(place_ref, keys, rows):
    j = lax.broadcasted_iota(jnp.int32, (keys, rows), 0)
    i = lax.broadcasted_iota(jnp.int32, (keys, rows), 1)
    block = lax.div(j, rows)
    place = (place_ref[0] - block) * rows + (j - block * rows)
    allowed = (place >= 0) & (place <= place_ref[0] * rows + i) & (place < place_ref[1])
    return jnp.where(allowed, 0.0, MASK_FLOOR)


def widened(part, group):
    zero = jnp.zeros_like(part)
    return jnp.concatenate([part, zero] if group == 0 else [zero, part], 0)


def attend_kernel(
    groups,
    place_ref,
    q_ref,
    k_ref,
    v_ref,
    tok_ref,
    gains_ref,
    router_ref,
    named_ref,
    wo_all_ref,
    out_ref,
    max_ref,
    total_ref,
    resid_ref,
    hn_ref,
    low_ref,
    gates_ref,
    bias_ref,
    wo_ref,
    sem,
):
    rows = q_ref.shape[0]
    keys = k_ref.shape[0]
    width = tok_ref.shape[1]
    step = pl.program_id(0)
    load = pltpu.make_async_copy(wo_all_ref, wo_ref, sem)

    @pl.when(step == 0)
    def _():
        load.start()
        bias_ref[...] = key_bias(place_ref, keys, rows)

    q_t = low(transposed(q_ref[...]))
    v_t = low(transposed(v_ref[...]))
    outs, maxes, totals = [], [], []
    for group in range(2):
        parts = [
            widened(q_t[(group * groups + h) * HD : (group * groups + h + 1) * HD], group)
            for h in range(groups)
        ]
        scores = dot_nn(k_ref[...], jnp.concatenate(parts, 1))
        weights = []
        for h in range(groups):
            s = scores[:, h * rows : (h + 1) * rows] + bias_ref[...]
            top = jnp.max(s, 0, keepdims=True)
            w = jnp.exp(s - top)
            totals.append(jnp.sum(w, 0, keepdims=True))
            maxes.append(top)
            weights.append(low(w))
        mixed = dot_nn(v_t, jnp.concatenate(weights, 1))
        for h in range(groups):
            part = mixed[group * HD : (group + 1) * HD, h * rows : (h + 1) * rows]
            outs.append(part / totals[group * groups + h])
    attn = jnp.transpose(jnp.concatenate(outs, 0))
    out_ref[...] = attn
    heads = 2 * groups * HD
    low_ref[:, pl.ds(pl.multiple_of(step * heads, 2 * HD), heads)] = low(attn)
    pad = [jnp.ones((8 - 2 * groups, rows), F32)] if 2 * groups < 8 else []
    max_ref[0] = jnp.concatenate(maxes + pad, 0)
    total_ref[0] = jnp.concatenate(totals + pad, 0)

    @pl.when(step == pl.num_programs(0) - 1)
    def _():
        load.wait()
        resid = up(tok_ref[...]) + dot_nn(low_ref[...], wo_ref[...])
        resid_ref[...] = resid
        inv = lax.rsqrt(jnp.mean(resid * resid, -1, keepdims=True) + NORM_EPS)
        hn = low(resid * inv * gains_ref[1:2, :])
        hn_ref[:, :width] = hn
        named = up(named_ref[...]) > 0.5
        logits = jnp.where(named, dot_nn(hn, router_ref[...]), MASK_FLOOR)
        gates = jnp.where(named, jnp.exp(logits - jnp.max(logits, -1, keepdims=True)), 0.0)
        gates = gates / jnp.sum(gates, -1, keepdims=True)
        gates_ref[...] = gates
        high = up(low(gates))
        hn_ref[:, width:] = low(high + pltpu.roll(gates - high, SIDE // 2, 1))


def attend(place, queries, keyval, tokens, gains, router, named, wo, groups):
    rows, heads_all = queries.shape
    width = tokens.shape[1]
    keys, kv = keyval.shape
    steps = kv // 2 // (2 * HD)
    heads = 2 * groups * HD

    def same(*shape):
        return pl.BlockSpec(shape, lambda i, s: (0,) * len(shape))

    return pl.pallas_call(
        functools.partial(attend_kernel, groups),
        grid_spec=pltpu.PrefetchScalarGridSpec(
            num_scalar_prefetch=1,
            grid=(steps,),
            in_specs=[
                pl.BlockSpec((rows, heads), lambda i, s: (0, i)),
                pl.BlockSpec((keys, 2 * HD), lambda i, s: (0, i)),
                pl.BlockSpec((keys, 2 * HD), lambda i, s: (0, steps + i)),
                same(rows, width),
                same(8, width),
                same(width, SIDE),
                same(rows, SIDE),
                pl.BlockSpec(memory_space=pl.ANY),
            ],
            out_specs=[
                pl.BlockSpec((rows, heads), lambda i, s: (0, i)),
                pl.BlockSpec((1, 8, rows), lambda i, s: (i, 0, 0)),
                pl.BlockSpec((1, 8, rows), lambda i, s: (i, 0, 0)),
                same(rows, width),
                same(rows, width + SIDE),
                same(rows, heads_all),
                same(rows, SIDE),
            ],
            scratch_shapes=[
                pltpu.VMEM((keys, rows), F32),
                pltpu.VMEM((heads_all, width), BF16),
                pltpu.SemaphoreType.DMA,
            ],
        ),
        out_shape=[
            pltpu.HBM((rows, heads_all), F32),
            jax.ShapeDtypeStruct((steps, 8, rows), F32),
            jax.ShapeDtypeStruct((steps, 8, rows), F32),
            pltpu.HBM((rows, width), F32),
            jax.ShapeDtypeStruct((rows, width + SIDE), BF16),
            pltpu.HBM((rows, heads_all), BF16),
            jax.ShapeDtypeStruct((rows, SIDE), F32),
        ],
        compiler_params=params(40),
        cost_estimate=cost(50 * rows * keys * heads_all),
        name="attend",
    )(place, *hbm(queries, keyval, keyval, tokens), gains, router, named, *hbm(wo))


def attend_back_kernel(
    groups,
    place_ref,
    q_ref,
    k_ref,
    v_ref,
    grad_ref,
    out_ref,
    max_ref,
    total_ref,
    cos_ref,
    sin_ref,
    hn_ref,
    gq_ref,
    gk_ref,
    gv_ref,
    part_ref,
    bias_ref,
    held_ref,
    hn_t_ref,
    sems,
):
    rows = q_ref.shape[0]
    keys = k_ref.shape[0]
    chunk = 256

    @pl.when(pl.program_id(0) == 0)
    def _():
        bias_ref[...] = key_bias(place_ref, keys, rows)
        for start in range(0, keys, rows):
            hn_t_ref[:, start : start + rows] = low(transposed(hn_ref[start : start + rows, :]))

    q_t = low(transposed(q_ref[...]))
    k_t = low(transposed(k_ref[...]))
    grad_t = transposed(grad_ref[...])
    out_t = transposed(out_ref[...])
    q_parts, g_parts, deltas, tops, grads = [], [], [], [], []
    for group in range(2):
        q_part, g_part, delta = [], [], []
        for h in range(groups):
            n = group * groups + h
            total = total_ref[0, n : n + 1]
            grad = grad_t[n * HD : (n + 1) * HD]
            q_part.append(widened(q_t[n * HD : (n + 1) * HD], group))
            g_part.append(widened(low(grad / total), group))
            delta.append(jnp.sum(out_t[n * HD : (n + 1) * HD] * grad, 0, keepdims=True) / total)
        q_parts.append(jnp.concatenate(q_part, 1))
        g_parts.append(jnp.concatenate(g_part, 1))
        deltas.append(jnp.concatenate(delta, 1))
        tops.append(
            jnp.concatenate(
                [max_ref[0, group * groups + h : group * groups + h + 1] for h in range(groups)], 1
            )
        )
        grads.append(jnp.zeros((2 * HD, groups * rows), F32))
    for start in range(0, keys, chunk):
        bias = bias_ref[start : start + chunk]
        bias = jnp.concatenate([bias] * groups, 1)
        grad_k = jnp.zeros((chunk, 2 * HD), F32)
        grad_v = jnp.zeros((chunk, 2 * HD), F32)
        for group in range(2):
            scores = dot_nn(k_ref[start : start + chunk], q_parts[group])
            w = jnp.exp(scores + bias - tops[group])
            gp = dot_nn(v_ref[start : start + chunk], g_parts[group])
            gs = low(w * (gp - deltas[group]))
            grad_v = grad_v + dot_nt(low(w), g_parts[group])
            grad_k = grad_k + dot_nt(gs, q_parts[group])
            grads[group] = grads[group] + dot_nn(k_t[:, start : start + chunk], gs)
        at = slice(start, start + chunk)
        gk_ref[at] = low(turn(grad_k, cos_ref[at, :], -sin_ref[at, :]))
        gv_ref[at] = low(grad_v)
    step, slot = pl.program_id(0), lax.rem(pl.program_id(0), 2)
    steps = part_ref.shape[1] // held_ref.shape[2]
    heads, two = 2 * groups * HD, 2 * HD

    def copies(n, slot):
        spans = ((0, heads), (steps * heads, two), (steps * (heads + two), two))
        out, col = [], 0
        for i, (first, size) in enumerate(spans):
            dst = pl.ds(pl.multiple_of(first + n * size, two), size)
            src = held_ref.at[slot, :, col : col + size]
            out.append(pltpu.make_async_copy(src, part_ref.at[:, dst], sems.at[slot, i]))
            col += size
        return out

    @pl.when(step >= 2)
    def _():
        for copy in copies(step - 2, slot):
            copy.wait()

    both = jnp.concatenate([gk_ref[...], gv_ref[...]], 1)
    held_ref[slot, :, heads:] = low(dot_nn(hn_t_ref[...], both))
    parts = []
    for group in range(2):
        for h in range(groups):
            parts.append(grads[group][group * HD : (group + 1) * HD, h * rows : (h + 1) * rows])
    grad_q = jnp.transpose(jnp.concatenate(parts, 0)) * (HD ** (-0.5))
    for d in range(0, 2 * groups * HD, 2 * HD):
        gq_ref[:, d : d + 2 * HD] = low(
            turn(grad_q[:, d : d + 2 * HD], cos_ref[:rows, :], -sin_ref[:rows, :])
        )
    held_ref[slot, :, :heads] = low(dot_nn(hn_t_ref[:, :rows], gq_ref[...]))
    for copy in copies(step, slot):
        copy.start()

    @pl.when(step == steps - 1)
    def _():
        for copy in copies(step, slot):
            copy.wait()

    @pl.when((step == steps - 1) & (step >= 1))
    def _():
        for copy in copies(step - 1, 1 - slot):
            copy.wait()


def attend_back(place, queries, keyval, grad_heads, attn, tops, totals, cosine, sine, hn, groups):
    rows, width = queries.shape
    keys, kv = keyval.shape
    steps = kv // 2 // (2 * HD)
    heads = 2 * groups * HD
    model = hn.shape[1]
    head_spec = pl.BlockSpec((rows, heads), lambda i, s: (0, i))
    key_spec = pl.BlockSpec((keys, 2 * HD), lambda i, s: (0, i))
    stat_spec = pl.BlockSpec((1, 8, rows), lambda i, s: (i, 0, 0))
    return pl.pallas_call(
        functools.partial(attend_back_kernel, groups),
        grid_spec=pltpu.PrefetchScalarGridSpec(
            num_scalar_prefetch=1,
            grid=(steps,),
            in_specs=[
                head_spec,
                key_spec,
                pl.BlockSpec((keys, 2 * HD), lambda i, s: (0, steps + i)),
                head_spec,
                head_spec,
                stat_spec,
                stat_spec,
                pl.BlockSpec((keys, 2 * HD), lambda i, s: (0, 0)),
                pl.BlockSpec((keys, 2 * HD), lambda i, s: (0, 0)),
                pl.BlockSpec((keys, model), lambda i, s: (0, 0)),
            ],
            out_specs=[
                head_spec,
                key_spec,
                key_spec,
                pl.BlockSpec(memory_space=pl.ANY),
            ],
            scratch_shapes=[
                pltpu.VMEM((keys, rows), F32),
                pltpu.VMEM((2, model, heads + 4 * HD), BF16),
                pltpu.VMEM((model, keys), BF16),
                pltpu.SemaphoreType.DMA((2, 3)),
            ],
        ),
        out_shape=[
            jax.ShapeDtypeStruct((rows, width), BF16),
            jax.ShapeDtypeStruct((keys, kv // 2), BF16),
            jax.ShapeDtypeStruct((keys, kv // 2), BF16),
            pltpu.HBM((model, width + kv), BF16),
        ],
        compiler_params=params(44),
        cost_estimate=cost(64 * rows * keys * width),
        name="attend_back",
    )(place, *hbm(queries, keyval, keyval, grad_heads, attn, tops, totals, cosine, sine, hn))


def slot_pick(slot, cap):
    place = lax.broadcasted_iota(jnp.int32, (cap, slot.shape[1]), 0).astype(F32)
    return place == slot


def weight_chunks(grads, x_ref, c_ref, ggu_ref, act_ref):
    hidden, width = act_ref.shape[1], c_ref.shape[1]
    size, wide = grads[0].shape
    rest = width - wide
    half = hidden // 2
    for h in range(2):
        at = slice(h * half, (h + 1) * half)
        part = low(dot_tn(act_ref[:, at], c_ref[...]))
        grads[0][at, :] = part[:, :wide]
        grads[0][hidden:, h * rest : (h + 1) * rest] = part[:, wide:]
    step = size // 2
    for c, ref in enumerate(grads[1:]):
        for h in range(2):
            cols = slice(c * size + h * step, c * size + (h + 1) * step)
            ref[h * step : (h + 1) * step, :] = low(dot_tn(x_ref[:, cols], ggu_ref[...]))


def expert_kernel(counts, cap, tile, e, earlier, last, number_ref, *refs):
    parts, refs = refs[: sum(counts)], refs[sum(counts) :]
    cot_all_ref, wgu_all_ref, wd_all_ref = refs[:3]
    gin_before, refs = refs[3 : 3 + earlier], refs[3 + earlier :]
    out_ref, slots_ref, result_ref = refs[:3]
    grads = refs[3:6]
    x_ref, c_ref, ggu_ref, act_ref, sg_ref, wgu_ref, wd_ref, cot_ref, cot_sems, sems = refs[6:16]
    if last:
        gin_ref, load_ref, store_ref = refs[16:]
    else:
        gin_ref = result_ref
    blocks = len(counts)
    hidden, width = wd_ref.shape
    rows = cot_ref.shape[0] // blocks
    total = blocks * cap
    index, expert = number_ref[0], number_ref[1]
    cot_loads = []
    for b in range(blocks):
        src = pl.ds(pl.multiple_of((index ^ b) * rows, rows), rows)
        dst = cot_ref.at[b * rows : (b + 1) * rows]
        cot_loads.append(pltpu.make_async_copy(cot_all_ref.at[src], dst, cot_sems.at[b]))
    loads = [
        pltpu.make_async_copy(wgu_all_ref.at[e], wgu_ref, sems.at[0]),
        pltpu.make_async_copy(wd_all_ref.at[e], wd_ref, sems.at[1]),
    ]
    for load in cot_loads + loads:
        load.start()
    lane = lax.broadcasted_iota(jnp.int32, (8, SIDE), 1)
    pick_slot = low(jnp.where(lane == expert, 1.0, 0.0))
    pick_gate = low(jnp.where((lane == expert) | (lane == expert + SIDE // 2), 1.0, 0.0))
    n = 0
    for b in range(blocks):
        hn = parts[n : n + counts[b]]
        n += counts[b]
        src = slice(b * rows, (b + 1) * rows)
        cot_loads[b].wait()
        slot = dot_nt(pick_slot, cot_ref[src, width:])[:1] - 1.0
        gate = [dot_nt(pick_gate, part[:, width:]) for part in hn]
        gate = (jnp.concatenate(gate, 1) if len(gate) > 1 else gate[0])[:1]
        slots_ref[b : b + 1, :] = slot
        hit = slot_pick(slot, cap)
        pick = low(jnp.where(hit, 1.0, 0.0))
        at = slice(b * cap, (b + 1) * cap)
        taken, start = None, 0
        for part in hn:
            piece = dot_nn(pick[:, start : start + part.shape[0]], part[:, :width])
            taken = piece if taken is None else taken + piece
            start += part.shape[0]
        x_ref[at, :] = low(taken)
        c_ref[at, :] = low(dot_nn(pick, cot_ref[src, :width]))
        gate = jnp.sum(jnp.where(hit, gate, 0.0), 1, keepdims=True)
        sg_ref[at, :] = jnp.broadcast_to(gate, (cap, 128))

    def middle(t, carry):
        at = pl.ds(pl.multiple_of(t * tile, 16), tile)
        gate_up = dot_nn(x_ref[at, :], wgu_ref[...])
        g = gate_up[:, :hidden]
        u = gate_up[:, hidden:]
        sigma = jax.nn.sigmoid(g)
        silu = g * sigma
        act = low(silu * u)
        slot_gate = sg_ref[at, :][:, :1]
        back = dot_nt(c_ref[at, :], wd_ref[...])
        gate_grad = jnp.sum(up(act) * back, 1, keepdims=True)
        back = back * slot_gate
        act_ref[at, :] = low(up(act) * slot_gate)
        ggu_ref[at, :hidden] = low(back * u * (sigma * (1.0 + g * (1.0 - sigma))))
        ggu_ref[at, hidden:] = low(back * silu)
        out_ref[at, :] = low(dot_nn(act, wd_ref[...]) * slot_gate)
        gin_ref[at, :width] = low(dot_nt(ggu_ref[at, :], wgu_ref[...]))
        lane = lax.broadcasted_iota(jnp.int32, (tile, SIDE), 1)
        high = up(low(gate_grad))
        side = jnp.where(lane == expert, high, 0.0)
        side = jnp.where(lane == expert + SIDE // 2, gate_grad - high, side)
        gin_ref[at, width:] = low(side)
        return carry

    for load in loads:
        load.wait()
    lax.fori_loop(0, total // tile, middle, 0)
    if not last:
        weight_chunks(grads, x_ref, c_ref, ggu_ref, act_ref)
        return

    def load_before(b):
        return [
            pltpu.make_async_copy(
                ref.at[b * cap : (b + 1) * cap], load_ref.at[b % 2, i], sems.at[2 + 2 * i + b % 2]
            )
            for i, ref in enumerate(gin_before)
        ]

    def store(b):
        dst = pl.ds(pl.multiple_of((index ^ b) * rows, rows), rows)
        return pltpu.make_async_copy(
            store_ref.at[b % 2], result_ref.at[dst], sems.at[2 + 2 * earlier + b % 2]
        )

    for load in load_before(0):
        load.start()
    for b in range(blocks):
        if b + 1 < blocks:
            for load in load_before(b + 1):
                load.start()
        src = slice(b * rows, (b + 1) * rows)
        order = up(cot_ref[src, width:])
        lane = lax.broadcasted_iota(jnp.int32, order.shape, 1)
        place = lax.broadcasted_iota(jnp.int32, (rows, cap), 1).astype(F32)

        def pick(number):
            slot = jnp.sum(jnp.where(lane == number, order, 0.0), 1, keepdims=True) - 1.0
            return low(jnp.where(place == slot, 1.0, 0.0))

        acc = dot_nn(pick(expert), gin_ref[b * cap : (b + 1) * cap, :])
        for i, load in enumerate(load_before(b)):
            load.wait()
            acc = acc + dot_nn(pick(expert - earlier + i), load_ref[b % 2, i])
        if b >= 2:
            store(b - 2).wait()
        store_ref[b % 2] = low(acc)
        store(b).start()
    weight_chunks(grads, x_ref, c_ref, ggu_ref, act_ref)
    for b in range(max(blocks - 2, 0), blocks):
        store(b).wait()


def unpack_down(chunk, hidden):
    rest = chunk.shape[1] // 2
    right = jnp.concatenate([chunk[hidden:, :rest], chunk[hidden:, rest:]], 0)
    return jnp.concatenate([chunk[:hidden], right], 1)


def run_expert(number, pieces, cot, w_gate_up, w_down, e, cap, gins):
    counts = [len(p) for p in pieces]
    flat = [h for p in pieces for h in p]
    blocks = len(counts)
    rows = cot.shape[0] // blocks
    hidden, width = w_down.shape[1:]
    total = blocks * cap
    tile = max(t for t in range(16, 401, 16) if total % t == 0)
    last = e + 1 == w_down.shape[0]
    earlier = len(gins) if last else 0
    anywhere = pl.BlockSpec(memory_space=pl.ANY)
    chunk = jax.ShapeDtypeStruct((width // 2, 2 * hidden), BF16)
    work = [(total, width), (total, width), (total, 2 * hidden), (total, hidden)]
    gin_shape = (total, width + SIDE)
    scratch = [pltpu.VMEM(shape, BF16) for shape in work] + [
        pltpu.VMEM((total, 128), F32),
        pltpu.VMEM((width, 2 * hidden), BF16),
        pltpu.VMEM((hidden, width), BF16),
        pltpu.VMEM(cot.shape, BF16),
        pltpu.SemaphoreType.DMA((blocks,)),
        pltpu.SemaphoreType.DMA((4 + 2 * earlier,)),
    ]
    if last:
        scratch += [
            pltpu.VMEM(gin_shape, BF16),
            pltpu.VMEM((2, max(earlier, 1), cap, width + SIDE), BF16),
            pltpu.VMEM((2, rows, width + SIDE), BF16),
        ]
    result = pltpu.HBM((blocks * rows, width + SIDE) if last else gin_shape, BF16)
    got = pl.pallas_call(
        functools.partial(expert_kernel, counts, cap, tile, e, earlier, last),
        in_specs=[pl.BlockSpec(memory_space=pltpu.SMEM)]
        + [WHOLE] * len(flat)
        + [anywhere] * (3 + earlier),
        out_specs=[WHOLE, WHOLE, anywhere if last else WHOLE] + [WHOLE] * 3,
        out_shape=[
            pltpu.HBM((total, width), BF16),
            jax.ShapeDtypeStruct((blocks, rows), F32),
            result,
        ]
        + [chunk] * 3,
        scratch_shapes=scratch,
        compiler_params=params(56),
        cost_estimate=cost(44 * total * width * hidden),
        name="expert",
    )(number, *flat, *hbm(cot), w_gate_up, w_down, *gins[:earlier])
    return got[0], got[1], got[2], got[3:]


def combine_kernel(count, cap, first, stride, number_ref, *refs):
    slots, parts, out_ref = refs[:count], refs[count : 2 * count], refs[2 * count]
    b = pl.program_id(0) * stride + first
    rows = slots[0].shape[1]
    place = lax.broadcasted_iota(jnp.int32, (cap, rows), 0).astype(F32)
    acc = None
    for e in range(count):
        pick = low(jnp.where(place == slots[e][pl.ds(b, 1), :], 1.0, 0.0))
        part = dot_tn(pick, parts[e][...])
        acc = part if acc is None else acc + part
    out_ref[...] = low(acc)


def combine(number, slots, parts, cap, chosen, order):
    blocks, rows = slots[0].shape
    count = len(parts)
    width = parts[0].shape[1]
    first, stride = chosen.start, chosen.step
    return pl.pallas_call(
        functools.partial(combine_kernel, count, cap, first, stride),
        grid_spec=pltpu.PrefetchScalarGridSpec(
            num_scalar_prefetch=1,
            grid=(len(chosen),),
            in_specs=[pl.BlockSpec((blocks, rows), lambda n, s: (0, 0))] * count
            + [pl.BlockSpec((cap, width), lambda n, s: (n * stride + first, 0))] * count,
            out_specs=pl.BlockSpec((rows, width), lambda n, s: (order(n, s[0]), 0)),
        ),
        out_shape=pltpu.HBM((len(chosen) * rows, width), BF16),
        compiler_params=params(20),
        cost_estimate=cost(10 * len(chosen) * cap * rows * width),
        name="combine",
    )(number, *slots, *parts)


def rope_tables(places):
    half = HD // 2
    frequency = ROPE_BASE ** (-jnp.arange(half, dtype=F32) * 2.0 / HD)
    angles = places.astype(F32)[:, None] * frequency[None, :]
    cosine, sine = jnp.cos(angles), jnp.sin(angles)
    return jnp.concatenate([cosine] * 4, 1), jnp.concatenate([-sine, sine] * 2, 1)


def per_device(
    tokens,
    lengths,
    routes,
    cotangent,
    gain_attn,
    gain_moe,
    w_query,
    w_keyval,
    w_output,
    w_router,
    w_gate_up,
    w_down,
):
    rows = tokens.shape[1]
    width = tokens.shape[2]
    experts = w_router.shape[1]
    local_experts = w_gate_up.shape[0]
    kv_width = w_keyval.shape[1] // 2
    head_total = w_query.shape[1]
    groups = head_total // kv_width
    dp_count = lax.axis_size("dp")
    ctx_count = lax.axis_size("ctx")
    dp_index = lax.axis_index("dp").astype(jnp.int32)
    ctx_index = lax.axis_index("ctx").astype(jnp.int32)
    cap = -(-(rows * 9 // 16) // 16) * 16
    length = lengths[0]
    places = ctx_index * rows + jnp.arange(rows, dtype=jnp.int32)
    valid = (places < length)[:, None]
    index = jnp.reshape(dp_index, (1,))

    pad = jnp.zeros((w_router.shape[0], 128 - experts - 2), BF16)
    first_w = Gather(
        jnp.concatenate(
            [w_query, w_keyval, w_router, gain_attn[:, None], gain_moe[:, None], pad], 1
        )
    )

    named = jnp.any(routes[0][..., None] == jnp.arange(SIDE, dtype=jnp.int32), 1).astype(BF16)
    order = dot_nn(jnp.tril(jnp.ones((rows, rows), BF16)), named) * up(named)
    grad_y = jnp.where(valid, cotangent[0], BF16(0))
    cot = jnp.concatenate([grad_y, low(order)], 1)

    seq = [halves(tokens[0])]
    back = jnp.arange(ctx_count, dtype=jnp.int32)[:, None] * rows
    tables = rope_tables((places[None, :] - back).reshape(-1))

    def next_block(part):
        return shift(seq[-1][part], 1)

    first_w.near()
    seq.append([next_block(0), next_block(1)])
    early = next_block(0)
    output_w = lax.all_gather(w_output, "dp", axis=0, tiled=True)
    _, tables, cot, seq[1], early = sync(first_w, tables, cot, seq[1], early)
    cot_all = lax.all_gather(cot, "dp", axis=0, tiled=True)
    first_w.far()
    seq.append([early, next_block(1)])
    early = next_block(0)
    _, seq[2], early = sync(first_w, seq[2], early)
    seq.append([early, next_block(1)])
    for _ in range(ctx_count - 4):
        seq.append([next_block(0), next_block(1)])
    cosine, sine = tables
    projected = project(index, first_w.pieces(), seq, cosine, sine, experts, head_total)
    queries, keyval, hn_seq, query_w, keyval_w, router_w, gains = projected
    keyval, hn_seq = project_last(seq[-1], gains, keyval_w, cosine, sine, keyval, hn_seq)

    place = jnp.stack([ctx_index, length])
    attn, tops, totals, resid, hn_two, attn_low, gates = attend(
        place, queries, keyval, tokens[0], gains, router_w, named, output_w, groups
    )

    hn_g = Gather(hn_two)
    hn_g.near()
    sync(hn_g)
    hn_pieces = hn_g.pieces()
    sums = LineSums()
    outs, gins, slots = [], [], []
    for e in range(local_experts):
        number = jnp.stack([dp_index, dp_index * local_experts + e])
        out, slot, gin, grads = run_expert(
            number, hn_pieces, cot_all, w_gate_up, w_down, e, cap, gins
        )
        outs.append(out)
        gins.append(gin)
        slots.append(slot)
        if e + 1 < local_experts:
            for c, v in enumerate(grads):
                sums.add(f"{e}.{c}", v)
            hn_pieces, cot_all = sums.step(hn_pieces, cot_all)
    for c, v in enumerate(grads):
        sums.add(f"{local_experts - 1}.{c}", v)
    (gin_tokens,) = sums.step(gins[-1])
    gin_sum = lax.psum_scatter(gin_tokens, "dp", scatter_dimension=0, tiled=True)
    outs, slots = sums.step(outs, slots)
    out_tokens = combine(index, slots, outs, cap, range(0, dp_count, 1), lambda n, i: n ^ i)

    backed = router_back(gin_sum, gates, router_w, gains, resid, grad_y, output_w, experts)
    *backed, out_tokens = sums.step(*sums.hold(*backed, out_tokens))
    grad_resid, grad_heads, *for_output = backed

    backed = attend_back(
        place, queries, keyval, grad_heads, attn, tops, totals, cosine, sine, hn_seq, groups
    )
    backed = sums.step(*backed, *for_output)
    grad_query, grad_keys, grad_values, part_first, grad_attn, grad_logits, gain_two = backed
    share_first = lax.psum_scatter(part_first, "dp", scatter_dimension=0, tiled=True)
    part_output = output_grad(attn_low, grad_attn, hn_two, grad_logits, gain_two, experts)
    (part_output,) = sums.step(part_output)
    share_output = lax.psum_scatter(part_output, "dp", scatter_dimension=0, tiled=True)
    share_query, share_keyval = share_first[:, :head_total], share_first[:, head_total:]
    gain_grad = jnp.sum(up(share_query) * up(w_query), 1, keepdims=True) + jnp.sum(
        up(share_keyval) * up(w_keyval), 1, keepdims=True
    )
    gain_grad = jnp.broadcast_to(gain_grad / up(gain_attn)[:, None], (w_query.shape[0], SIDE))
    share_keyval = jnp.concatenate([share_keyval, low(gain_grad)], 1)
    sums.step()
    sums.launch("query", share_query)
    sums.launch("keyval", share_keyval)
    gate_up, down = jnp.zeros(w_gate_up.shape, F32), jnp.zeros(w_down.shape, F32)
    placed = set()

    def place_done(gate_up, down):
        for e in range(local_experts):
            for c in range(3):
                if f"{e}.{c}" not in sums.done or f"{e}.{c}" in placed:
                    continue
                placed.add(f"{e}.{c}")
                part = sums.total(f"{e}.{c}")
                if c == 0:
                    part = unpack_down(part, w_down.shape[1])
                    down = lax.dynamic_update_slice(down, part[None], (e, 0, 0))
                else:
                    at = (e, (c - 1) * part.shape[0], 0)
                    gate_up = lax.dynamic_update_slice(gate_up, part[None], at)
        return gate_up, down

    grad_kv = jnp.concatenate([grad_keys, grad_values], 1)
    blocks = [grad_kv[r * rows : (r + 1) * rows] for r in range(ctx_count)]
    held = blocks[-1]
    for r in range(ctx_count - 2, -1, -1):
        pairs = [(i, i - 1) for i in range(r + 1, ctx_count)]
        held = add_low(lax.ppermute(held, "ctx", pairs), blocks[r])
        if r == max(ctx_count - 2, 1):
            held, out_tokens = sums.step(held, out_tokens)
            moe = lax.psum_scatter(out_tokens, "dp", scatter_dimension=0, tiled=True)
            sums.add("output", share_output)
        elif r:
            (held,) = sums.step(held)

    grad_hn_one = dot_nt(grad_query, query_w) + dot_nt(held, keyval_w)
    inputs = up(tokens[0])
    inv_one = lax.rsqrt(jnp.mean(inputs * inputs, -1, keepdims=True) + NORM_EPS)
    normed_one = inputs * inv_one
    scaled_one = grad_hn_one * gains[0:1]
    grad_inputs = grad_resid + inv_one * (
        scaled_one - normed_one * jnp.mean(scaled_one * normed_one, -1, keepdims=True)
    )
    grad_inputs = low(grad_inputs)

    outcome = low(jnp.where(valid, resid + up(moe), 0.0))

    wanted = [f"{e}.{c}" for e in range(local_experts) for c in range(3)]
    while not all(name in sums.done for name in wanted):
        sums.step()
    gate_up, down = place_done(gate_up, down)
    while not ("query" in sums.done and "keyval" in sums.done):
        sums.step()
    total_query, total_keyval = sums.total("query"), sums.total("keyval")
    ready = (total_query, total_keyval[:, : 2 * kv_width], total_keyval[:, 2 * kv_width])
    ready = sums.step(*ready, outcome, gate_up, down, grad_inputs)
    total_query, total_keyval, total_gain, outcome, gate_up, down, grad_inputs = ready
    while sums.busy():
        sums.step()
    total_output = sums.total("output")
    return (
        outcome[None],
        grad_inputs[None],
        total_gain,
        total_output[:, width + experts],
        total_query,
        total_keyval,
        total_output[:, :width],
        total_output[:, width : width + experts],
        gate_up,
        down,
    )


def solution(mesh):
    in_specs = (
        P("dp", "ctx", None),
        P("dp"),
        P("dp", "ctx", None),
        P("dp", "ctx", None),
        P("dp"),
        P("dp"),
        P("dp", None),
        P("dp", None),
        P("dp", None),
        P("dp", None),
        P("dp", None, None),
        P("dp", None, None),
    )
    out_specs = (
        P("dp", "ctx", None),
        P("dp", "ctx", None),
        P("dp"),
        P("dp"),
        P("dp", None),
        P("dp", None),
        P("dp", None),
        P("dp", None),
        P("dp", None, None),
        P("dp", None, None),
    )
    return jax.shard_map(
        per_device, mesh=mesh, in_specs=in_specs, out_specs=out_specs, check_vma=False
    )
```
